32 devices in a mesh: dp: 16 (over z, x, core), fsdp: 2 (over y).
Axes of the slice: x: 2, y: 2, z: 4, core: 2. Of those that a mesh axis runs over, the one named last changes fastest.
Arguments:
- block_input: bfloat16 [3, 32, 64, 64, 192], P(None, 'dp', 'fsdp'), may hold values from -12 to 12
- embedding: bfloat16 [3, 32, 768], P(None, 'dp'), may hold values from -6 to 6
- out_cotangent: bfloat16 [3, 32, 64, 64, 192], P(None, 'dp', 'fsdp'), may hold values from -6 to 6
- conv_weights: bfloat16 [3, 2, 3, 3, 192, 192], P(None, None, None, None, 'fsdp'), may hold values from -0.15625 to 0.15625
- affine_weight: bfloat16 [3, 768, 384], P(None, 'fsdp'), may hold values from -0.21875 to 0.21875
- gains: bfloat16 [3, 2, 192], P(None, None, 'fsdp'), may hold values from 0.5 to 1.5
- biases: bfloat16 [3, 6, 192], P(None, None, 'fsdp'), may hold values from -2 to 2
- counts: int32 [16], P('dp'), may hold values from 0 to 2, as said below
Outputs:
- block_output: bfloat16 [3, 32, 64, 64, 192], P(None, 'dp', 'fsdp')
- input_grad: bfloat16 [3, 32, 64, 64, 192], P(None, 'dp', 'fsdp')
- conv_grads: float32 [2, 2, 3, 3, 192, 192], P(None, None, None, None, 'fsdp')
- affine_grad: float32 [2, 768, 384], P(None, 'fsdp')
- gain_grads: float32 [2, 2, 192], P(None, None, 'fsdp')
- bias_grads: float32 [2, 6, 192], P(None, None, 'fsdp')
The draws below stay inside these ranges and needn't reach their ends.
Inputs may be any that keep to these rules, and one draw needn't show every extreme that they name: `counts`: some index of dp holds 2 images and some holds none in every draw.
All inputs are finite; a program needn't handle non-finite values.
Results may differ from the reference program's by a relative error of at most 0.0019.
The reference program's roundings to bfloat16 on the way count: a program that leaves them out, or rounds other values in their place, can miss the bound.
Values may be sent and summed in bfloat16 or wider, within the bound.
A program may use at most 384 MiB of HBM per device.

```python
import jax
import jax.numpy as jnp
from jax import lax

C = 192
E = 768
GROUPS = 32
H = 64
W = 64
NETS = 3
IMG_CAP = 2
IMAGES = 32
N_DP = 16


def draw_block_input(key, part):
    key = jax.random.fold_in(key, 11)
    first_key, second_key = jax.random.split(key, 2)
    ramp = 0.6 * 3.0 ** (jnp.arange(H, dtype=jnp.float32) / (H - 1))
    rough = jax.random.uniform(second_key, (NETS, IMAGES, H, 1, 1), minval=0.7, maxval=1.4)
    row_scale = ramp.reshape(1, 1, H, 1, 1) * rough
    values = jax.random.normal(first_key, (NETS, IMAGES, H, W, C)) * row_scale
    return jnp.clip(values, -12.0, 12.0).astype(jnp.bfloat16)


def draw_counts(key, part):
    key = jax.random.fold_in(key, 23)
    first_key, second_key = jax.random.split(key)
    values = jax.random.randint(first_key, (N_DP,), 0, IMG_CAP + 1)
    order = jax.random.permutation(second_key, N_DP)
    values = values.at[order[0]].set(IMG_CAP).at[order[1]].set(0)
    return values.astype(jnp.int32)


def steps_of(stream_key, dims, pieces, least, high):
    gain, own = 1.0, jax.random.fold_in(stream_key, 6)
    for position, parts in pieces:
        draws = jnp.exp(jax.random.uniform(jax.random.fold_in(own, position), (parts,), jnp.float32, least / len(pieces), high / len(pieces)))
        gain = gain * jnp.repeat(draws, dims[position] // parts).reshape([-1 if axis == position else 1 for axis in range(len(dims))])
    return gain


def bell_draw(rng, shape, width, limit, cuts=(), kind=jnp.bfloat16):
    gain = steps_of(rng, shape, cuts, -0.22, 0.18) if cuts else 1.0
    entries = jax.random.normal(rng, shape, jnp.float32) * width * gain
    return jnp.minimum(jnp.maximum(entries, -limit), limit).astype(kind)


def setup_inputs(seed: int = 0) -> dict:
    key_of = jax.random.split(jax.random.key(seed), 9)
    return {
        "block_input": draw_block_input(jax.random.fold_in(key_of[8], 71), 0),
        "embedding": bell_draw(key_of[1], (NETS, IMAGES, E), 1.0, 6.0, ((1, 16),)),
        "out_cotangent": bell_draw(key_of[2], (NETS, IMAGES, H, W, C), 1.0, 6.0, ((1, 16), (2, 2))),
        "conv_weights": bell_draw(key_of[3], (NETS, 2, 3, 3, C, C), (9 * C) ** -0.5, 0.15625, ((4, 2),)),
        "affine_weight": bell_draw(key_of[4], (NETS, E, 2 * C), E ** -0.5, 0.21875, ((1, 2),)),
        "gains": jnp.clip(1.0 + 0.1 * jax.random.normal(key_of[5], (NETS, 2, C), jnp.float32), 0.5, 1.5).astype(jnp.bfloat16),
        "biases": bell_draw(key_of[6], (NETS, 6, C), 0.3, 2.0, ((2, 2),)),
        "counts": draw_counts(jax.random.fold_in(key_of[8], 71), 0),
    }


EPSILON = 1e-05

@jax.custom_vjp
def low(v):
    return lax.optimization_barrier(v.astype(jnp.bfloat16)).astype(jnp.float32)

@jax.custom_vjp
def low_back(v):
    return v

def low_keep(v):
    return (low(v), None)

def low_pass(kept, grad):
    return (grad,)

def back_keep(v):
    return (v, None)

def back_low(kept, grad):
    return (low(grad),)
low.defvjp(low_keep, low_pass)
low_back.defvjp(back_keep, back_low)

def group_norm(value):
    grouped = value.reshape(H, W, GROUPS, C // GROUPS)
    mean_value = lax.optimization_barrier(jnp.mean(grouped, axis=(0, 1, 3), keepdims=True))
    square_mean = lax.optimization_barrier(jnp.mean(grouped * grouped, axis=(0, 1, 3), keepdims=True))
    variance = square_mean - mean_value * mean_value
    return ((grouped - mean_value) * lax.rsqrt(variance + EPSILON)).reshape(H, W, C)

def convolve(image, kernel):
    result = lax.conv_general_dilated(image[None], kernel, (1, 1), 'SAME', dimension_numbers=('NHWC', 'HWIO', 'NHWC'), precision=lax.Precision.HIGHEST)
    return result[0]

def block_forward(image, embed_row, keep_value, kernels, affine, gain_rows, bias_rows):
    zeroth = group_norm(image) * gain_rows[0] + bias_rows[0]
    first_act = low(jax.nn.silu(zeroth))
    hidden = low_back(convolve(first_act, kernels[0])) + bias_rows[1]
    normed = group_norm(hidden) * gain_rows[1] + bias_rows[2]
    modulation = low_back(jnp.dot(embed_row, affine, precision=lax.Precision.HIGHEST))
    modulation = modulation + jnp.concatenate([bias_rows[4], bias_rows[5]])
    scale_part = modulation[:C]
    shift_part = modulation[C:]
    second_act = low(jax.nn.silu(shift_part + normed * (scale_part + 1.0)))
    branch = convolve(second_act, kernels[1]) + bias_rows[3]
    return (branch + image) * keep_value

def reference(block_input, embedding, out_cotangent, conv_weights, affine_weight, gains, biases, counts):
    slots = jnp.arange(IMAGES, dtype=jnp.int32)
    keep_mask = (slots % IMG_CAP < counts[slots // IMG_CAP]).astype(jnp.float32)
    outputs = []
    in_grads = []
    trained = []
    for network in range(NETS):
        kernels = conv_weights[network].astype(jnp.float32)
        affine = affine_weight[network].astype(jnp.float32)
        gain_rows = gains[network].astype(jnp.float32)
        bias_rows = biases[network].astype(jnp.float32)

        def image_step(carry, item):
            image, embed_row, cotangent, keep_value = item
            embed_float = embed_row.astype(jnp.float32)

            def forward(image_float, kernel_arg, affine_arg, gain_arg, bias_arg):
                return block_forward(image_float, embed_float, keep_value, kernel_arg, affine_arg, gain_arg, bias_arg)
            result, pullback = jax.vjp(forward, image.astype(jnp.float32), kernels, affine, gain_rows, bias_rows)
            grads = pullback(cotangent.astype(jnp.float32))
            new_carry = (carry[0] + grads[1], carry[1] + grads[2], carry[2] + grads[3], carry[3] + grads[4])
            return (new_carry, (result.astype(jnp.bfloat16), grads[0].astype(jnp.bfloat16)))
        start = (jnp.zeros((2, 3, 3, C, C), jnp.float32), jnp.zeros((E, 2 * C), jnp.float32), jnp.zeros((2, C), jnp.float32), jnp.zeros((6, C), jnp.float32))
        totals, (result_rows, grad_rows) = lax.scan(image_step, start, (block_input[network], embedding[network], out_cotangent[network], keep_mask))
        outputs.append(result_rows)
        in_grads.append(grad_rows)
        if network != 1:
            trained.append(totals)
    return (jnp.stack(outputs), jnp.stack(in_grads), jnp.stack([trained[0][0], trained[1][0]]), jnp.stack([trained[0][1], trained[1][1]]), jnp.stack([trained[0][2], trained[1][2]]), jnp.stack([trained[0][3], trained[1][3]]))
```

```python
import functools
import types

import jax
import jax.numpy as jnp
from jax import lax
from jax.experimental import pallas as pl
from jax.experimental.pallas import tpu as pltpu
from jax.sharding import PartitionSpec as P

GROUPS = 32
EPSILON = 1e-05
LANES = 128
CHUNK = 64
MESH = pl.DeviceIdType.MESH
F32 = jnp.float32
BF16 = jnp.bfloat16

MU0, R0, G0, G1, B1, B2, B3, SC1, SH, SGY, MU1, R1, SUMH = range(13)
PA0, PB0, PMU0, PBIAS, PA1, PB1, PMU1, PDA, PDB, PDC = range(10)


def settings(dp_size, fsdp_size, nets, slots, rows, width, chans, embed_rows):
    g = types.SimpleNamespace()
    g.dp, g.f, g.nets, g.s, g.r, g.w, g.c, g.ef = (
        dp_size, fsdp_size, nets, slots, rows, width, chans, embed_rows,
    )
    g.np = rows // 2
    g.u = min(4, g.np)
    g.px = g.np * LANES
    g.count = float(rows * fsdp_size * width * (chans // GROUPS))
    g.pixels = float(rows * fsdp_size * width)
    g.bits = dp_size.bit_length() - 1
    g.shard = chans // fsdp_size
    g.low_rows = 9 * g.shard
    g.high_rows = -(-g.low_rows // 16) * 8
    unit = 8 << (g.bits - 1)
    g.pack = -(-(g.low_rows + g.high_rows) // unit) * unit
    g.wide = max(2 * chans, embed_rows)
    g.stages = 2 * g.bits
    return g


def kernel_body(
    g,
    x_h, gy_h, w_h, aff, emb, gb, keep,
    y_h, dx_h, cg_h, ag_h, sg,
    rx, rg, xc, gc, xa0, xa1, xg, hb, xe, hbuf, dub, wraw, wf, wb, gacc, pk, r0b, ryb, rbb,
    ys, cgs, ags, ex1, ex2, sb, acc, rowt, prm,
    lx, lg, ysem, hs, hr, es, er, wl, wys, wyr, wcs, wcr, cs, cr, ss, sr, osem,
):
    me = lax.axis_index("fsdp")
    dp = lax.axis_index("dp")
    C, NP, F, S, R = g.c, g.np, g.f, g.s, g.r
    PX = g.px

    def net_of(i):
        return (2 * i) % g.nets

    def peer(df):
        return (me + df) % F

    def source(df):
        return (me + F - df) % F

    def bit(b):
        return (dp // (1 << b)) % 2

    def partner(b):
        return dp + (1 << b) * (1 - 2 * bit(b))

    def remote(src, dst, send, recv, where):
        return pltpu.make_async_remote_copy(
            src_ref=src, dst_ref=dst, send_sem=send, recv_sem=recv,
            device_id=where, device_id_type=MESH,
        )

    def tile(t):
        if isinstance(t, int):
            return pl.ds(t * LANES, LANES)
        return pl.ds(pl.multiple_of(t * LANES, LANES), LANES)

    lane = lax.broadcasted_iota(jnp.int32, (C, LANES), 1)
    low_lanes = lane < g.w
    top = (me > 0).astype(jnp.int32)
    bottom = (me < F - 1).astype(jnp.int32)
    edge_ok = jnp.where(low_lanes, top, bottom) > 0


    def halo_copy(i, s, t, down):
        src = (x_h, gy_h)[t]
        n = net_of(i)
        if down:
            return remote(
                src.at[n, s, pl.ds(R - 2, 2)], hb.at[i, s, t, 0],
                hs.at[i, s, t, 1], hr.at[i, s, t, 1], {"fsdp": (me + 1) % F},
            )
        return remote(
            src.at[n, s, pl.ds(0, 2)], hb.at[i, s, t, 1],
            hs.at[i, s, t, 0], hr.at[i, s, t, 0], {"fsdp": (me + F - 1) % F},
        )

    def halo_start(i, s, t):
        @pl.when(me > 0)
        def _():
            halo_copy(i, s, t, False).start()

        @pl.when(me < F - 1)
        def _():
            halo_copy(i, s, t, True).start()

    def halo_take(i, s, t):
        @pl.when(me > 0)
        def _():
            halo_copy(i, s, t, True).wait_recv()

        @pl.when(me < F - 1)
        def _():
            halo_copy(i, s, t, False).wait_recv()

    def halo_sent(i, s, t):
        @pl.when(me > 0)
        def _():
            halo_copy(i, s, t, False).wait_send()

        @pl.when(me < F - 1)
        def _():
            halo_copy(i, s, t, True).wait_send()

    def row_copy(i, e, s, df, who):
        ref = ex1.at[i, s, who] if e == 0 else ex2.at[i, e - 1, s, who]
        return remote(ref, ref, es.at[i, e, s, df], er.at[i, e, s, df], {"fsdp": peer(df)})

    def rows_start(i, e, s):
        for df in range(1, F):
            row_copy(i, e, s, df, me).start()

    def rows_take(i, e, s):
        for df in range(1, F):
            row_copy(i, e, s, df, source(df)).wait_recv()
        parts = [ex1[i, s, f] if e == 0 else ex2[i, e - 1, s, f] for f in range(F)]
        total = parts[0]
        for part in parts[1:]:
            total = total + part
        return total

    mine = dp % 2
    sibling = partner(0)

    def weight_copy(i, df, who):
        return remote(
            w_h.at[net_of(i), mine], wraw.at[i, who, mine],
            wys.at[i, df], wyr.at[i, df], {"fsdp": peer(df)},
        )

    def weight_share(i, df, kind):
        ref = wraw.at[i, source(df), kind]
        return remote(ref, ref, wcs.at[i, df], wcr.at[i, df], {"dp": sibling})

    def weight_local(i):
        return pltpu.make_async_copy(w_h.at[net_of(i)], wraw.at[i, me], wl.at[i])

    def weights_start(i):
        for df in range(1, F):
            weight_copy(i, df, me).start()
        weight_local(i).start()

    def weights_forward(i):
        for df in range(1, F):
            weight_copy(i, df, source(df)).wait_recv()
            weight_share(i, df, mine).start()

    def weights_take(i):
        weight_local(i).wait()
        for df in range(1, F):
            weight_share(i, df, 1 - mine).wait_recv()

    def net_start(i):
        for t in range(2):
            for s in range(S):
                halo_start(i, s, t)
        weights_start(i)


    def part(b):
        return g.pack >> (b + 1)

    def base(b):
        offset = 0
        for b2 in range(b + 1):
            offset = offset + bit(b2) * part(b2)
        return offset

    def rows_at(offset, size):
        if not isinstance(offset, int):
            offset = pl.multiple_of(offset, 8)
        return pl.ds(offset, size)

    def away(b):
        return rows_at(base(b - 1) + (1 - bit(b)) * part(b), part(b))

    def home(b):
        return rows_at(base(b), part(b))

    def region(b):
        return sum(part(b2) for b2 in range(1, b))

    last_bit = g.bits - 1

    def stage_copies(m, k, t):
        if t == 0:
            return [(
                remote(pk.at[k, :, away(0)], r0b.at[k], cs.at[m, k, 0, 0], cr.at[m, k, 0, 0], {"dp": partner(0)}),
                None,
            )]
        if t == 1:
            return [
                (
                    remote(
                        pk.at[k, peer(df), home(0)], ryb.at[k, df - 1],
                        cs.at[m, k, 1, df - 1], cr.at[m, k, 1, df - 1], {"fsdp": peer(df)},
                    ),
                    None,
                )
                for df in range(1, F)
            ]
        if t <= g.bits:
            b = t - 1
            rows = home(b - 1) if b == last_bit else away(b)
            size = part(b - 1) if b == last_bit else part(b)
            return [(
                remote(
                    pk.at[k, me, rows], rbb.at[k, pl.ds(region(b), size)],
                    cs.at[m, k, t, 0], cr.at[m, k, t, 0], {"dp": partner(b)},
                ),
                None,
            )]
        b = 2 * g.bits - 1 - t
        own = pk.at[k, me, home(b)]
        other = pk.at[k, me, away(b)]
        where = {"dp": partner(b)}
        return [(
            remote(own, own, cs.at[m, k, t, 0], cr.at[m, k, t, 0], where),
            remote(own, other, cs.at[m, k, t, 0], cr.at[m, k, t, 0], where),
        )]

    def add_rows(dst, dst_start, src, src_start, size):
        step = part(last_bit - 1)

        def body(j, carry):
            a = rows_at(dst_start + j * step, step)
            b = rows_at(src_start + j * step, step)
            dst[a, :] = dst[a, :] + src[b, :]
            return carry

        lax.fori_loop(0, size // step, body, 0)

    def stage_start(m, k, t):
        for copy, _ in stage_copies(m, k, t):
            copy.start()

    def stage_finish(m, k, t):
        for copy, received in stage_copies(m, k, t):
            copy.wait_send()
            (received or copy).wait_recv()
        if t == 0:
            for f in range(F):
                add_rows(pk.at[k, f], base(0), r0b.at[k, f], 0, part(0))
        elif t == 1:
            for df in range(1, F):
                add_rows(pk.at[k, me], base(0), ryb.at[k, df - 1], 0, part(0))
        elif t <= g.bits:
            b = t - 1
            kept = last_bit - 1 if b == last_bit else b
            add_rows(pk.at[k, me], base(kept), rbb.at[k], region(b), part(kept))

    def small_copy(m, b, received):
        size = 1 << b
        start = (dp // size) * size
        there = start + size * (1 - 2 * bit(b))
        own = sb.at[m, pl.ds(start, size)]
        dst = sb.at[m, pl.ds(there, size)] if received else own
        return remote(own, dst, ss.at[m, b], sr.at[m, b], {"dp": partner(b)})

    round_at = [1] + [b + 2 for b in range(1, g.bits)]

    def tick(i, t):
        @pl.when(i > 0)
        def _():
            m = i - 1
            for k in range(2):
                stage_finish(m, k, t - 1)
            for b in range(g.bits):
                ends = round_at[b + 1] if b + 1 < g.bits else round_at[b] + 1
                if t == ends:
                    small_copy(m, b, False).wait_send()
                    small_copy(m, b, True).wait_recv()
            for b in range(g.bits):
                if t == round_at[b]:
                    small_copy(m, b, False).start()
            if t < g.stages:
                for k in range(2):
                    stage_start(m, k, t)
            else:
                finish_large(m)
            if t == round_at[-1] + 1:
                finish_small(m)

    def finish_small(m):
        total = sb[m, 0, 0:8, 0:C]
        for d in range(1, g.dp):
            total = total + sb[m, d, 0:8, 0:C]
        sg[m] = total
        block = sb[m, :, 8:16, :].reshape(g.dp * 8, g.wide)
        index = lax.broadcasted_iota(jnp.int32, (g.dp * 8, g.ef), 0) & 7
        left = jnp.where(index < S, block[:, : g.ef], 0.0).astype(BF16)
        right = pltpu.roll(block[:, : 2 * C], g.dp * 8 - S, 0).astype(BF16)

        @pl.when(m > 0)
        def _():
            pltpu.make_async_copy(ags, ag_h.at[m], osem.at[2]).wait()

        ags[...] = lax.dot_general(left, right, (((0,), (0,)), ((), ())), preferred_element_type=F32)
        pltpu.make_async_copy(ags, ag_h.at[m], osem.at[2]).start()

    def finish_large(m):
        for k in range(2):
            out = pltpu.make_async_copy(cgs.at[k], cg_h.at[m, k], osem.at[k])

            @pl.when(m > 0)
            def _():
                out.wait()

            cgs[k, :, 0:LANES] = pk[k, me, 0 : g.low_rows, :]
            split = g.low_rows - g.high_rows
            cgs[k, 0 : g.high_rows, LANES:C] = pk[k, me, g.low_rows : g.low_rows + g.high_rows, 0 : C - LANES]
            cgs[k, g.high_rows : g.low_rows, LANES:C] = pk[k, me, g.low_rows : g.low_rows + split, CHUNK : CHUNK + C - LANES]
            out.start()

    def pack_start(m):
        for k in range(2):
            for f in range(F):
                for tap in range(9):
                    first, last = tap * g.shard, (tap + 1) * g.shard
                    c0 = tap * C + f * g.shard
                    pk[k, f, first:last, :] = gacc[k, c0 : c0 + g.shard, 0:LANES]
                    for lo, hi, lanes in ((0, g.high_rows, 0), (g.high_rows, g.low_rows, CHUNK)):
                        a, b = max(first, lo), min(last, hi)
                        if a < b:
                            at = g.low_rows + a - lo
                            pk[k, f, at : at + b - a, lanes : lanes + C - LANES] = gacc[
                                k, c0 + a - first : c0 + b - first, LANES:C
                            ]
            stage_start(m, k, 0)


    def shifted(v):
        col = lax.broadcasted_iota(jnp.int32, v.shape, 1) & (g.w - 1)
        left = jnp.where(col == 0, 0.0, pltpu.roll(v, 1, 1))
        right = jnp.where(col == g.w - 1, 0.0, pltpu.roll(v, LANES - 1, 1))
        return left, v, right

    def put(buf, s, rows, t, v):
        for j, moved in enumerate(shifted(v)):
            buf[s, j, rows, tile(t)] = moved.astype(BF16)

    def put_edges(buf, s, first_edge, second_edge):
        near = shifted(first_edge)
        far = None if second_edge is None else shifted(second_edge)
        for j in range(3):
            first = buf[s, j, :, tile(1)].astype(F32)
            last = buf[s, j, :, tile(NP)].astype(F32)
            buf[s, j, :, tile(0)] = jnp.where(low_lanes, near[j], pltpu.roll(last, g.w, 1)).astype(BF16)
            buf[s, j, :, tile(NP + 1)] = jnp.where(low_lanes, pltpu.roll(first, g.w, 1), near[j]).astype(BF16)
            if far is not None:
                buf[s, j, :, tile(NP + 2)] = jnp.where(low_lanes, far[j], last).astype(BF16)
                buf[s, j, :, tile(NP + 3)] = near[j].astype(BF16)
                buf[s, j, :, tile(NP + 4)] = jnp.where(low_lanes, first, far[j]).astype(BF16)

    def windows(buf, s, back, edge):
        pieces = []
        for i in range(3):
            for j in range(3):
                ti, tj = (2 - i, 2 - j) if back else (i, j)
                piece = buf[s, tj, :, ti * LANES : ti * LANES + PX]
                if edge:
                    piece = jnp.concatenate([piece, buf[s, tj, :, tile(NP + 2 + ti)]], axis=1)
                pieces.append(piece)
        return jnp.concatenate(pieces, axis=0)

    def chunks():
        return [pl.ds(c0, CHUNK) for c0 in range(0, C, CHUNK)]

    def over_tiles(body):
        def step(block, carry):
            body([block * g.u + u for u in range(g.u)])
            return carry

        lax.fori_loop(0, NP // g.u, step, 0)

    def clear(count):
        for k in range(count):
            acc[k] = jnp.zeros((C, LANES), F32)

    def total_row(k):
        return jnp.sum(acc[k].T, axis=0, keepdims=True)

    def group_rows(rows):
        high = rows.astype(BF16)
        rest = rows - high.astype(F32)
        middle = rest.astype(BF16)
        low = (rest - middle.astype(F32)).astype(BF16)
        a = lax.broadcasted_iota(jnp.int32, (C, C), 0) // (C // GROUPS)
        b = lax.broadcasted_iota(jnp.int32, (C, C), 1) // (C // GROUPS)
        same = jnp.where(a == b, 1.0, 0.0).astype(BF16)
        three = jnp.dot(jnp.concatenate([high, middle, low], axis=0).astype(BF16), same, preferred_element_type=F32)
        n = rows.shape[0]
        return three[0:n] + three[n : 2 * n] + three[2 * n : 3 * n]

    def stack(*rows):
        fill = 8 - len(rows)
        return jnp.concatenate(list(rows) + [jnp.zeros((fill, C), F32)] * (fill > 0), axis=0)

    def spread(s, k, row):
        prm[s, k] = jnp.broadcast_to(row, (LANES, C)).T

    def save(s, k, row):
        rowt[s, k : k + 1, :] = row

    def row(s, k):
        return rowt[s, k : k + 1, :]

    def moments(total):
        grouped = group_rows(total)
        mean = grouped[0:1] / g.count
        variance = grouped[1:2] / g.count - mean * mean
        return mean, lax.rsqrt(variance + EPSILON)

    def slope_twice(w, t):
        return (1.0 + t) * (1.0 + w * (1.0 - t))

    def pair(buf, s, q):
        return jnp.concatenate([buf[s, q], buf[s, q + NP]], axis=0)

    def pixels(s):
        return jnp.concatenate([rg[s, h] for q in range(NP) for h in (q, q + NP)], axis=0)


    def read_phase(i, s):
        n = net_of(i)
        kf = keep[s]
        pltpu.make_async_copy(x_h.at[n, s], rx.at[s], lx.at[s]).wait()
        pltpu.make_async_copy(gy_h.at[n, s], rg.at[s], lg.at[s]).wait()
        clear(3)

        def body(qs):
            for q in qs:
                xc[s, :, tile(q)] = pair(rx, s, q).T
                gc[s, :, tile(q)] = (pair(rg, s, q).T.astype(F32) * kf).astype(BF16)
            for rows in chunks():
                a0, a1, a2 = acc[0, rows], acc[1, rows], acc[2, rows]
                for q in qs:
                    xf = xc[s, rows, tile(q)].astype(F32)
                    a0 = a0 + xf
                    a1 = a1 + xf * xf
                    gf = gc[s, rows, tile(q)].astype(F32)
                    a2 = a2 + gf
                    put(xg, s, rows, q + 1, gf)
                acc[0, rows], acc[1, rows], acc[2, rows] = a0, a1, a2

        over_tiles(body)
        eight = emb[n, s]
        ex1[i, s, me, 0:8] = stack(
            total_row(0), total_row(1), total_row(2),
            jnp.dot(eight, aff[n, 0], preferred_element_type=F32)[0:1],
            jnp.dot(eight, aff[n, 1], preferred_element_type=F32)[0:1],
        )
        ex1[i, s, me, 8:16] = gb[n]
        rows_start(i, 0, s)

    def edge_phase(i, s):
        kf = keep[s]
        halo_take(i, s, 0)
        halo_take(i, s, 1)
        for t in range(2):
            near = jnp.concatenate([hb[i, s, t, 0, 1], hb[i, s, t, 1, 0]], axis=0).T.astype(F32)
            far = jnp.concatenate([hb[i, s, t, 0, 0], hb[i, s, t, 1, 1]], axis=0).T.astype(F32)
            near = jnp.where(edge_ok, near, 0.0)
            far = jnp.where(edge_ok, far, 0.0)
            if t == 0:
                xe[s, 0] = near
                xe[s, 1] = far
            else:
                put_edges(xg, s, near * kf, far * kf)

    def weights_ready(i):
        for k in range(2):
            for tap in range(9):
                blocks = [wraw[i, f, k, tap] for f in range(F)]
                if g.shard % 16:
                    blocks = [b.astype(F32) for b in blocks]
                whole = jnp.concatenate(blocks, axis=0).astype(BF16)
                wb[k, :, tap * C : (tap + 1) * C] = whole
                wf[k, :, tap * C : (tap + 1) * C] = whole.T

    def first_phase(i, s):
        total = rows_take(i, 0, s)
        mean, inverse = moments(total[0:8])
        save(s, MU0, mean)
        save(s, R0, inverse)
        save(s, SGY, total[2:3])
        gain0, gain1 = total[8:9], total[9:10]
        save(s, G0, gain0)
        save(s, G1, gain1)
        save(s, B1, total[11:12])
        save(s, B2, total[12:13])
        save(s, B3, total[13:14])
        save(s, SC1, total[3:4] + total[14:15] + 1.0)
        save(s, SH, total[4:5] + total[15:16])
        scale = inverse * gain0
        spread(s, PA0, 0.5 * scale)
        spread(s, PB0, 0.5 * (total[10:11] - mean * scale))
        spread(s, PMU0, mean)
        spread(s, PBIAS, total[11:12])

        def act(xf, a, b):
            w = xf * a + b
            return w * jnp.tanh(w) + w

        def body(qs):
            for rows in chunks():
                a, b = prm[s, PA0, rows], prm[s, PB0, rows]
                for q in qs:
                    put(xa0, s, rows, q + 1, act(xc[s, rows, tile(q)].astype(F32), a, b))

        over_tiles(body)
        edges = [jnp.where(edge_ok, act(xe[s, t], prm[s, PA0], prm[s, PB0]), 0.0) for t in range(2)]
        put_edges(xa0, s, edges[0], edges[1])
        dub[s] = jnp.dot(wb[1], windows(xg, s, True, True), preferred_element_type=F32)

    def hidden_phase(i, s):
        hbuf[s] = jnp.dot(wf[0], windows(xa0, s, False, True), preferred_element_type=F32)
        clear(2)

        def body(qs):
            for rows in chunks():
                bias = prm[s, PBIAS, rows]
                a0, a1 = acc[0, rows], acc[1, rows]
                for q in qs:
                    h = hbuf[s, rows, tile(q)] + bias
                    hbuf[s, rows, tile(q)] = h
                    a0 = a0 + h
                    a1 = a1 + h * h
                acc[0, rows], acc[1, rows] = a0, a1

        over_tiles(body)
        hbuf[s, :, tile(NP)] = hbuf[s, :, tile(NP)] + prm[s, PBIAS]
        ex2[i, 0, s, me] = stack(total_row(0), total_row(1))
        rows_start(i, 1, s)

    def second_phase(i, s):
        total = rows_take(i, 1, s)
        mean, inverse = moments(total)
        save(s, MU1, mean)
        save(s, R1, inverse)
        save(s, SUMH, total[0:1])
        scale = inverse * row(s, G1)
        spread(s, PA1, 0.5 * scale * row(s, SC1))
        spread(s, PB1, 0.5 * (row(s, SH) + (row(s, B2) - mean * scale) * row(s, SC1)))
        spread(s, PMU1, mean)
        clear(2)

        def body(qs):
            for rows in chunks():
                a, b, mu = prm[s, PA1, rows], prm[s, PB1, rows], prm[s, PMU1, rows]
                a0, a1 = acc[0, rows], acc[1, rows]
                for q in qs:
                    h = hbuf[s, rows, tile(q)]
                    w = h * a + b
                    t = jnp.tanh(w)
                    put(xa1, s, rows, q + 1, w * t + w)
                    d = dub[s, rows, tile(q)] * slope_twice(w, t)
                    dub[s, rows, tile(q)] = d
                    a0 = a0 + d
                    a1 = a1 + d * (h - mu)
                acc[0, rows], acc[1, rows] = a0, a1

        over_tiles(body)
        w = hbuf[s, :, tile(NP)] * prm[s, PA1] + prm[s, PB1]
        t = jnp.tanh(w)
        put_edges(xa1, s, jnp.where(edge_ok, w * t + w, 0.0), None)
        dub[s, :, tile(NP)] = dub[s, :, tile(NP)] * slope_twice(w, t)
        ex2[i, 1, s, me] = stack(0.5 * total_row(0), 0.5 * total_row(1))
        rows_start(i, 2, s)

    def out_copy(i, s):
        return pltpu.make_async_copy(ys.at[s], y_h.at[net_of(i), s], ysem.at[s])

    def in_grad_copy(i, s):
        return pltpu.make_async_copy(ys.at[s], dx_h.at[net_of(i), s], ysem.at[s])

    def put_pixels(s, q, v):
        flat = v.astype(BF16).T
        ys[s, q] = flat[0 : g.w]
        ys[s, q + NP] = flat[g.w : 2 * g.w]

    def output_phase(i, s):
        kf = keep[s]
        spread(s, PBIAS, row(s, B3))
        branch = jnp.dot(wf[1], windows(xa1, s, False, False), preferred_element_type=F32)

        @pl.when(i > 0)
        def _():
            in_grad_copy(i, s).wait()

        for q in range(NP):
            v = branch[:, q * LANES : (q + 1) * LANES] + prm[s, PBIAS] + xc[s, :, tile(q)].astype(F32)
            put_pixels(s, q, v * kf)
        out_copy(i, s).start()

        @pl.when(i < 2)
        def _():
            o = jnp.dot(windows(xa1, s, False, False), pixels(s), preferred_element_type=F32)
            gacc[1] = gacc[1] + o * kf

    def hidden_grad_phase(i, s):
        total = rows_take(i, 2, s)
        s1, s2 = total[0:1], total[1:2] * row(s, R1)
        sc1, gain1, inverse, mean = row(s, SC1), row(s, G1), row(s, R1), row(s, MU1)
        grouped = group_rows(stack(gain1 * sc1 * s1, gain1 * sc1 * s2))
        m1, m2 = grouped[0:1] / g.count, grouped[1:2] / g.count
        a = inverse * sc1 * gain1
        b = -inverse * inverse * m2
        c = -inverse * m1 - mean * b
        spread(s, PDA, 0.5 * a)
        spread(s, PDB, b)
        spread(s, PDC, c)

        @pl.when(i < 2)
        def _():
            dscale = gain1 * s2 + row(s, B2) * s1
            here = sb.at[i, dp]
            here[1:2, 0:C] = here[1:2, 0:C] + sc1 * s2
            here[3:4, 0:C] = here[3:4, 0:C] + a * s1 + b * row(s, SUMH) + c * g.pixels
            here[4:5, 0:C] = here[4:5, 0:C] + sc1 * s1
            here[5:6, 0:C] = here[5:6, 0:C] + row(s, SGY)
            here[6:7, 0:C] = here[6:7, 0:C] + dscale
            here[7:8, 0:C] = here[7:8, 0:C] + s1
            modulation = jnp.concatenate([dscale, s1], axis=1).astype(BF16).astype(F32)
            for slot in range(S):
                @pl.when(s == slot)
                def _():
                    here[8 + slot : 9 + slot, 0 : g.ef] = emb[net_of(i), s].astype(F32)[0:1]
                    here[8 + S + slot : 9 + S + slot, 0 : 2 * C] = modulation

        def body(qs):
            for rows in chunks():
                a, b, c = prm[s, PDA, rows], prm[s, PDB, rows], prm[s, PDC, rows]
                for q in qs:
                    d = dub[s, rows, tile(q)] * a + hbuf[s, rows, tile(q)] * b + c
                    put(xg, s, rows, q + 1, d)
            for q in qs:
                flat = xg[s, 1, :, tile(q + 1)].T
                rg[s, q] = flat[0 : g.w]
                rg[s, q + NP] = flat[g.w : 2 * g.w]

        over_tiles(body)
        d = dub[s, :, tile(NP)] * prm[s, PDA] + hbuf[s, :, tile(NP)] * prm[s, PDB] + prm[s, PDC]
        put_edges(xg, s, jnp.where(edge_ok, d, 0.0), None)

    def input_grad_phase(i, s):
        hbuf[s, :, 0:PX] = jnp.dot(wb[0], windows(xg, s, True, False), preferred_element_type=F32)
        clear(2)

        def body(qs):
            for rows in chunks():
                a, b, mu = prm[s, PA0, rows], prm[s, PB0, rows], prm[s, PMU0, rows]
                a0, a1 = acc[0, rows], acc[1, rows]
                for q in qs:
                    xf = xc[s, rows, tile(q)].astype(F32)
                    w = xf * a + b
                    d = hbuf[s, rows, tile(q)] * slope_twice(w, jnp.tanh(w))
                    hbuf[s, rows, tile(q)] = d
                    a0 = a0 + d
                    a1 = a1 + d * (xf - mu)
                acc[0, rows], acc[1, rows] = a0, a1

        over_tiles(body)
        ex2[i, 2, s, me] = stack(0.5 * total_row(0), 0.5 * total_row(1))
        rows_start(i, 3, s)

    def weight_phase(i, s):
        gacc[0] = gacc[0] + jnp.dot(windows(xa0, s, False, False), pixels(s), preferred_element_type=F32)

    def last_phase(i, s):
        total = rows_take(i, 3, s)
        inverse, mean, gain0 = row(s, R0), row(s, MU0), row(s, G0)
        s3, s4 = total[0:1], total[1:2] * inverse
        grouped = group_rows(stack(gain0 * s3, gain0 * s4))
        m1, m2 = grouped[0:1] / g.count, grouped[1:2] / g.count
        b = -inverse * inverse * m2
        spread(s, PA1, 0.5 * inverse * gain0)
        spread(s, PB1, b)
        spread(s, PMU1, -inverse * m1 - mean * b)

        @pl.when(i < 2)
        def _():
            here = sb.at[i, dp]
            here[0:1, 0:C] = here[0:1, 0:C] + s4
            here[2:3, 0:C] = here[2:3, 0:C] + s3

        out_copy(i, s).wait()

        def body(qs):
            for q in qs:
                xf = xc[s, :, tile(q)].astype(F32)
                v = hbuf[s, :, tile(q)] * prm[s, PA1] + xf * prm[s, PB1] + prm[s, PMU1]
                put_pixels(s, q, v + gc[s, :, tile(q)].astype(F32))

        over_tiles(body)
        in_grad_copy(i, s).start()


    def slots(phase, i):
        def step(s, carry):
            phase(i, s)
            return carry

        lax.fori_loop(0, S, step, 0)

    def load_x(i):
        for s in range(S):
            pltpu.make_async_copy(x_h.at[net_of(i), s], rx.at[s], lx.at[s]).start()

    def load_gy(i):
        for s in range(S):
            pltpu.make_async_copy(gy_h.at[net_of(i), s], rg.at[s], lg.at[s]).start()

    load_x(0)
    load_gy(0)
    pk[:, :, g.low_rows + g.high_rows :, :] = jnp.zeros((2, F, g.pack - g.low_rows - g.high_rows, LANES), F32)

    @pl.when(me == 0)
    def _():
        hb[:, :, :, 0] = jnp.zeros(hb.shape[:3] + hb.shape[4:], BF16)

    @pl.when(me == F - 1)
    def _():
        hb[:, :, :, 1] = jnp.zeros(hb.shape[:3] + hb.shape[4:], BF16)

    barrier = pltpu.get_barrier_semaphore()
    for df in range(1, F):
        pl.semaphore_signal(barrier, inc=1, device_id={"fsdp": peer(df)}, device_id_type=MESH)
    for b in range(g.bits):
        pl.semaphore_signal(barrier, inc=1, device_id={"dp": partner(b)}, device_id_type=MESH)
    pl.semaphore_wait(barrier, F - 1 + g.bits)
    net_start(0)

    def network(i, carry):
        @pl.when(i < 2)
        def _():
            net_start(i + 1)
            sb[i, dp] = jnp.zeros((16, g.wide), F32)
            gacc[...] = jnp.zeros(gacc.shape, F32)

        slots(read_phase, i)

        @pl.when(i < 2)
        def _():
            load_x(i + 1)

        slots(edge_phase, i)
        tick(i, 1)
        weights_forward(i)
        weights_take(i)
        weights_ready(i)
        slots(first_phase, i)
        slots(hidden_phase, i)
        slots(second_phase, i)
        tick(i, 2)
        slots(output_phase, i)
        tick(i, 3)
        slots(hidden_grad_phase, i)
        tick(i, 4)
        slots(input_grad_phase, i)
        tick(i, 5)

        @pl.when(i < 2)
        def _():
            slots(weight_phase, i)
            load_gy(i + 1)

        slots(last_phase, i)
        for t in range(6, g.stages + 1):
            tick(i, t)

        @pl.when(i < 2)
        def _():
            pack_start(i)

        return carry

    lax.fori_loop(0, 3, network, 0)


    def drain(i, carry):
        for s in range(S):
            for t in range(2):
                halo_sent(i, s, t)
            for e in range(4):
                for df in range(1, F):
                    row_copy(i, e, s, df, me).wait_send()
        for df in range(1, F):
            weight_copy(i, df, me).wait_send()
            weight_share(i, df, mine).wait_send()
        return carry

    lax.fori_loop(0, 3, drain, 0)
    for s in range(S):
        in_grad_copy(2, s).wait()
    for k in range(2):
        pltpu.make_async_copy(cgs.at[k], cg_h.at[1, k], osem.at[k]).wait()
    pltpu.make_async_copy(ags, ag_h.at[1], osem.at[2]).wait()


def on_device(
    block_input, embedding, out_cotangent, conv_weights, affine_weight, gains, biases, counts
):
    nets, slots, rows, width, chans = block_input.shape
    fsdp = lax.axis_size("fsdp")
    dp = lax.axis_size("dp")
    me = lax.axis_index("fsdp")
    embed_rows = affine_weight.shape[1]
    g = settings(dp, fsdp, nets, slots, rows, width, chans, embed_rows)

    keep = (jnp.arange(slots) < counts[0]).astype(F32)
    weights = conv_weights.reshape(nets, 2, 9, g.shard, chans)
    affine = affine_weight.reshape(nets, embed_rows, 2, chans).transpose(0, 2, 1, 3)
    embed = lax.dynamic_slice_in_dim(embedding, me * embed_rows, embed_rows, 2)
    embed = jnp.broadcast_to(embed[:, :, None, :], (nets, slots, 16, embed_rows))
    vectors = jnp.concatenate([gains, biases], axis=1).astype(F32)
    vectors = lax.dynamic_update_slice_in_dim(
        jnp.zeros((nets, 8, chans), F32), vectors, me * g.shard, 2
    )

    tiles = (g.np + 1) * LANES
    dma = pltpu.SemaphoreType.DMA
    scratch = [
        pltpu.VMEM((slots, rows, width, chans), BF16),
        pltpu.VMEM((slots, rows, width, chans), BF16),
        pltpu.VMEM((slots, chans, g.px), BF16),
        pltpu.VMEM((slots, chans, g.px), BF16),
        pltpu.VMEM((slots, 3, chans, (g.np + 5) * LANES), BF16),
        pltpu.VMEM((slots, 3, chans, (g.np + 2) * LANES), BF16),
        pltpu.VMEM((slots, 3, chans, (g.np + 5) * LANES), BF16),
        pltpu.VMEM((3, slots, 2, 2, 2, width, chans), BF16),
        pltpu.VMEM((slots, 2, chans, LANES), F32),
        pltpu.VMEM((slots, chans, tiles), F32),
        pltpu.VMEM((slots, chans, tiles), F32),
        pltpu.VMEM((3, fsdp, 2, 9, g.shard, chans), BF16),
        pltpu.VMEM((2, chans, 9 * chans), BF16),
        pltpu.VMEM((2, chans, 9 * chans), BF16),
        pltpu.VMEM((2, 9 * chans, chans), F32),
        pltpu.VMEM((2, fsdp, g.pack, LANES), F32),
        pltpu.VMEM((2, fsdp, g.pack // 2, LANES), F32),
        pltpu.VMEM((2, fsdp - 1, g.pack // 2, LANES), F32),
        pltpu.VMEM((2, g.pack // 2, LANES), F32),
        pltpu.VMEM((slots, rows, width, chans), BF16),
        pltpu.VMEM((2, g.low_rows, chans), F32),
        pltpu.VMEM((embed_rows, 2 * chans), F32),
        pltpu.VMEM((3, slots, fsdp, 16, chans), F32),
        pltpu.VMEM((3, 3, slots, fsdp, 8, chans), F32),
        pltpu.VMEM((2, dp, 16, g.wide), F32),
        pltpu.VMEM((3, chans, LANES), F32),
        pltpu.VMEM((slots, 16, chans), F32),
        pltpu.VMEM((slots, 10, chans, LANES), F32),
        dma((slots,)),
        dma((slots,)),
        dma((slots,)),
        dma((3, slots, 2, 2)),
        dma((3, slots, 2, 2)),
        dma((3, 4, slots, fsdp)),
        dma((3, 4, slots, fsdp)),
        dma((3,)),
        dma((3, fsdp)),
        dma((3, fsdp)),
        dma((3, fsdp)),
        dma((3, fsdp)),
        dma((2, 2, g.stages, fsdp)),
        dma((2, 2, g.stages, fsdp)),
        dma((2, g.bits)),
        dma((2, g.bits)),
        dma((3,)),
    ]
    hbm = pl.BlockSpec(memory_space=pl.ANY)
    vmem = pl.BlockSpec(memory_space=pltpu.VMEM)
    smem = pl.BlockSpec(memory_space=pltpu.SMEM)
    block_output, input_grad, conv_grads, affine_grad, sums = pl.pallas_call(
        functools.partial(kernel_body, g),
        out_shape=(
            jax.ShapeDtypeStruct(block_input.shape, BF16),
            jax.ShapeDtypeStruct(block_input.shape, BF16),
            jax.ShapeDtypeStruct((2, 2, g.low_rows, chans), F32),
            jax.ShapeDtypeStruct((2, embed_rows, 2 * chans), F32),
            jax.ShapeDtypeStruct((2, 8, chans), F32),
        ),
        in_specs=[hbm, hbm, hbm, vmem, vmem, vmem, smem],
        out_specs=(hbm, hbm, hbm, hbm, vmem),
        scratch_shapes=scratch,
        compiler_params=pltpu.CompilerParams(
            collective_id=0, has_side_effects=True, vmem_limit_bytes=64 << 20
        ),
    )(block_input, out_cotangent, weights, affine, embed, vectors, keep)
    conv_grads = conv_grads.reshape(2, 2, 3, 3, g.shard, chans)
    piece = lax.dynamic_slice_in_dim(sums, me * g.shard, g.shard, 2)
    return block_output, input_grad, conv_grads, affine_grad, piece[:, 0:2], piece[:, 2:8]


def solution(mesh):
    placed = (
        P(None, "dp", "fsdp", None, None),
        P(None, "dp", None),
        P(None, "dp", "fsdp", None, None),
        P(None, None, None, None, "fsdp", None),
        P(None, "fsdp", None),
        P(None, None, "fsdp"),
        P(None, None, "fsdp"),
        P("dp"),
    )
    return jax.shard_map(
        on_device,
        mesh=mesh,
        in_specs=placed,
        out_specs=(
            P(None, "dp", "fsdp", None, None),
            P(None, "dp", "fsdp", None, None),
            P(None, None, None, None, "fsdp", None),
            P(None, "fsdp", None),
            P(None, None, "fsdp"),
            P(None, None, "fsdp"),
        ),
        check_vma=False,
    )
```

```python
import functools
import types

import jax
import jax.numpy as jnp
from jax import lax
from jax.experimental import pallas as pl
from jax.experimental.pallas import tpu as pltpu
from jax.sharding import PartitionSpec as P

GROUPS = 32
EPSILON = 1e-05
LANES = 128
CHUNK = 64
MESH = pl.DeviceIdType.MESH
F32 = jnp.float32
BF16 = jnp.bfloat16

MU0, R0, G0, G1, B1, B2, B3, SC1, SH, SGY, MU1, R1, SUMH = range(13)
PA0, PB0, PMU0, PBIAS, PA1, PB1, PMU1, PDA, PDB, PDC = range(10)


def settings(dp_size, fsdp_size, nets, slots, rows, width, chans, embed_rows):
    g = types.SimpleNamespace()
    g.dp, g.f, g.nets, g.s, g.r, g.w, g.c, g.ef = (
        dp_size, fsdp_size, nets, slots, rows, width, chans, embed_rows,
    )
    g.np = rows // 2
    g.px = g.np * LANES
    g.count = float(rows * fsdp_size * width * (chans // GROUPS))
    g.pixels = float(rows * fsdp_size * width)
    g.bits = dp_size.bit_length() - 1
    g.shard = chans // fsdp_size
    g.low_rows = 9 * g.shard
    g.high_rows = -(-g.low_rows // 16) * 8
    g.pack = -(-(g.low_rows + g.high_rows) // 64) * 64
    g.half = g.pack // 2
    g.piece = g.pack // 8
    g.wide = max(2 * chans, embed_rows)
    g.stages = g.bits + 2
    return g


def kernel_body(
    g,
    x_h, gy_h, w_h, aff, emb, gains, biases, counts,
    y_h, dx_h, cg_h, ag_h, sg,
    rx, rg, dhp, xc, gc, xa0, xa1, xg, hb, hbuf, dub, wraw, wf, wb, gacc, pk, r0b, r1b, ry0, ry1, rbb,
    yc, ags, ex1, ex2, sb, acc, rowt, prm,
    lx, lg, ysem, hs, hr, es, er, wl, wys, wyr, wcs, wcr, cs, cr, ss, sr, osem,
):
    me = lax.axis_index("fsdp")
    dp = lax.axis_index("dp")
    C, NP, F, S, R = g.c, g.np, g.f, g.s, g.r
    PX = g.px

    def net_of(i):
        return (2 * i) % g.nets

    def peer(df):
        return (me + df) % F

    def source(df):
        return (me + F - df) % F

    def bit(b):
        return (dp // (1 << b)) % 2

    def other(*bits):
        where = dp
        for b in bits:
            where = where + (1 << b) * (1 - 2 * bit(b))
        return where

    def remote(src, dst, send, recv, where):
        return pltpu.make_async_remote_copy(
            src_ref=src, dst_ref=dst, send_sem=send, recv_sem=recv,
            device_id=where, device_id_type=MESH,
        )

    def tile(t):
        if isinstance(t, int):
            return pl.ds(t * LANES, LANES)
        return pl.ds(pl.multiple_of(t * LANES, LANES), LANES)

    def kept(s):
        return jnp.where(s < counts[0], 1.0, 0.0)

    lane = lax.broadcasted_iota(jnp.int32, (C, LANES), 1)
    low_lanes = lane < g.w
    top = (me > 0).astype(jnp.int32)
    bottom = (me < F - 1).astype(jnp.int32)
    edge_ok = jnp.where(low_lanes, top, bottom) > 0


    def halo_copy(i, s, t, down):
        src = (x_h, gy_h)[t]
        n = net_of(i)
        if down:
            return remote(
                src.at[n, s, pl.ds(R - 2, 2)], hb.at[i % 2, s, t, 0],
                hs.at[i, s, t, 1], hr.at[i, s, t, 1], {"fsdp": (me + 1) % F},
            )
        return remote(
            src.at[n, s, pl.ds(0, 2)], hb.at[i % 2, s, t, 1],
            hs.at[i, s, t, 0], hr.at[i, s, t, 0], {"fsdp": (me + F - 1) % F},
        )

    def halo_start(i, s, t):
        @pl.when(me > 0)
        def _():
            halo_copy(i, s, t, False).start()

        @pl.when(me < F - 1)
        def _():
            halo_copy(i, s, t, True).start()

    def halo_take(i, s, t):
        @pl.when(me > 0)
        def _():
            halo_copy(i, s, t, True).wait_recv()

        @pl.when(me < F - 1)
        def _():
            halo_copy(i, s, t, False).wait_recv()

    def halo_sent(i, s, t):
        @pl.when(me > 0)
        def _():
            halo_copy(i, s, t, False).wait_send()

        @pl.when(me < F - 1)
        def _():
            halo_copy(i, s, t, True).wait_send()

    def row_copy(i, e, s, df, who):
        ref = ex1.at[i, s, who] if e == 0 else ex2.at[i, e - 1, s, who]
        return remote(ref, ref, es.at[i, e, s, df], er.at[i, e, s, df], {"fsdp": peer(df)})

    def rows_start(i, e, s):
        for df in range(1, F):
            row_copy(i, e, s, df, me).start()

    def rows_take(i, e, s):
        for df in range(1, F):
            row_copy(i, e, s, df, source(df)).wait_recv()
        parts = [ex1[i, s, f] if e == 0 else ex2[i, e - 1, s, f] for f in range(F)]
        total = parts[0]
        for part in parts[1:]:
            total = total + part
        return total

    mine = dp % 2

    def weight_copy(i, df, who):
        return remote(
            w_h.at[net_of(i), mine], wraw.at[i % 2, who, mine],
            wys.at[i, df], wyr.at[i, df], {"fsdp": peer(df)},
        )

    def weight_share(i, df, kind):
        ref = wraw.at[i % 2, source(df), kind]
        return remote(ref, ref, wcs.at[i, df], wcr.at[i, df], {"dp": other(0)})

    def weight_local(i):
        return pltpu.make_async_copy(w_h.at[net_of(i)], wraw.at[i % 2, me], wl.at[i])

    def weights_start(i):
        for df in range(1, F):
            weight_copy(i, df, me).start()
        weight_local(i).start()

    def weights_forward(i):
        for df in range(1, F):
            weight_copy(i, df, source(df)).wait_recv()
            weight_share(i, df, mine).start()

    def weights_take(i):
        weight_local(i).wait()
        for df in range(1, F):
            weight_share(i, df, 1 - mine).wait_recv()

    def weights_sent(i):
        for df in range(1, F):
            weight_share(i, df, mine).wait_send()

    def halos_start(i, t):
        for s in range(S):
            halo_start(i, s, t)


    def rows_at(offset, size):
        if not isinstance(offset, int):
            offset = pl.multiple_of(offset, 8)
        return pl.ds(offset, size)

    half_start = bit(0) * g.half
    PAIR = ((1,), (2,), (1, 2))

    def piece_start(bits):
        b1 = 1 - bit(1) if 1 in bits else bit(1)
        b2 = 1 - bit(2) if 2 in bits else bit(2)
        return half_start + (2 * b1 + b2) * g.piece

    def stage_copies(m, k, t):
        def sems(j):
            return cs.at[m, k, t, j], cr.at[m, k, t, j]

        mine_at = rows_at(piece_start(()), g.piece)
        gather = g.bits
        if t == 0:
            there = rows_at((1 - bit(0)) * g.half, g.half)
            return [(remote(pk.at[m, k, :, there], r0b.at[k], *sems(0), {"dp": other(0)}), None)]
        if t in (1, 2) and (t == 1) == (k == 1):
            rows = rows_at(half_start, g.half) if k else mine_at
            into = ry1 if k else ry0
            return [
                (remote(pk.at[m, k, peer(df), rows], into.at[m, df - 1], *sems(df), {"fsdp": peer(df)}), None)
                for df in range(1, F)
            ]
        if t in (1, 2):
            copies = []
            for j, bits in enumerate(PAIR):
                rows = rows_at(piece_start(bits), g.piece)
                src = pk.at[m, k, me, rows] if k else pk.at[m, k, :, rows]
                dst = r1b.at[k, j, 0] if k else r1b.at[k, j]
                copies.append((remote(src, dst, *sems(j), {"dp": other(*bits)}), None))
            return copies
        if t < gather:
            return [(
                remote(pk.at[m, k, me, mine_at], rbb.at[k, t - 3], *sems(0), {"dp": other(t)}), None,
            )]
        if t == gather:
            own = pk.at[m, k, me, mine_at]
            return [
                (
                    remote(own, own, *sems(j), {"dp": other(*bits)}),
                    remote(own, pk.at[m, k, me, rows_at(piece_start(bits), g.piece)], *sems(j), {"dp": other(*bits)}),
                )
                for j, bits in enumerate(PAIR)
            ]
        own = pk.at[m, k, me, rows_at(half_start, g.half)]
        there = pk.at[m, k, me, rows_at((1 - bit(0)) * g.half, g.half)]
        return [(
            remote(own, own, *sems(0), {"dp": other(0)}), remote(own, there, *sems(0), {"dp": other(0)}),
        )]

    def add_rows(dst, start, sources, size):
        step = max(n for n in range(8, 65, 8) if size % n == 0)

        def body(j, carry):
            at = rows_at(start + j * step, step)
            total = dst[at, :]
            for src in sources:
                total = total + src[rows_at(j * step, step), :]
            dst[at, :] = total
            return carry

        lax.fori_loop(0, size // step, body, 0)

    def stage_start(m, k, t):
        for copy, _ in stage_copies(m, k, t):
            copy.start()

    def stage_finish(m, k, t):
        for copy, received in stage_copies(m, k, t):
            copy.wait_send()
            (received or copy).wait_recv()
        if t == 0:
            for f in range(F):
                add_rows(pk.at[m, k, f], half_start, [r0b.at[k, f]], g.half)
        elif t in (1, 2) and (t == 1) == (k == 1):
            into = ry1 if k else ry0
            start, size = (half_start, g.half) if k else (piece_start(()), g.piece)
            add_rows(pk.at[m, k, me], start, [into.at[m, df - 1] for df in range(1, F)], size)
        elif t in (1, 2):
            if k:
                add_rows(pk.at[m, k, me], piece_start(()), [r1b.at[k, j, 0] for j in range(3)], g.piece)
            else:
                for f in range(F):
                    add_rows(pk.at[m, k, f], piece_start(()), [r1b.at[k, j, f] for j in range(3)], g.piece)
        elif t < g.bits:
            add_rows(pk.at[m, k, me], piece_start(()), [rbb.at[k, t - 3]], g.piece)

    def small_copies(m, r, received):
        groups = [((0,),), PAIR]
        if r < 2:
            size, targets, sem = (1, groups[0], 0) if r == 0 else (2, groups[1], 1)
        else:
            size, targets, sem = 1 << (r + 1), ((r + 1,),), r + 2
        copies = []
        for j, bits in enumerate(targets):
            own = sb.at[m, pl.ds((dp // size) * size, size)]
            dst = sb.at[m, pl.ds((other(*bits) // size) * size, size)] if received else own
            copies.append(remote(own, dst, ss.at[m, sem + j], sr.at[m, sem + j], {"dp": other(*bits)}))
        return copies

    def small_start(m, r):
        for copy in small_copies(m, r, False):
            copy.start()

    def small_finish(m, r):
        for copy in small_copies(m, r, False):
            copy.wait_send()
        for copy in small_copies(m, r, True):
            copy.wait_recv()

    rounds = [(2, 3), (3, 4)] + [(b + 1, b + 2) for b in range(3, g.bits)]

    def tick(m, t):
        if t == 0:
            for k in range(2):
                pack_rows(m, k)
                stage_start(m, k, 0)
            return
        for k in range(2):
            stage_finish(m, k, t - 1)
        for r, (_, last) in enumerate(rounds):
            if t == last:
                small_finish(m, r)
        for r, (first, _) in enumerate(rounds):
            if t == first:
                small_start(m, r)
        if t < g.stages:
            for k in range(2):
                stage_start(m, k, t)
        else:
            for k in range(2):
                pltpu.make_async_copy(pk.at[m, k, me], cg_h.at[m, k], osem.at[m, k]).start()
        if t == rounds[-1][1]:
            finish_small(m)

    def finish_small(m):
        total = sb[m, 0, 0:8, 0 : 2 * LANES]
        for d in range(1, g.dp):
            total = total + sb[m, d, 0:8, 0 : 2 * LANES]
        sg[m] = pltpu.roll(total, 2 * LANES - me * g.shard, 1)
        block = sb[m, :, 8:16, :].reshape(g.dp * 8, g.wide)
        index = lax.broadcasted_iota(jnp.int32, (g.dp * 8, g.ef), 0) & 7
        left = jnp.where(index < S, block[:, : g.ef], 0.0).astype(BF16)
        right = pltpu.roll(block[:, : 2 * C], g.dp * 8 - S, 0).astype(BF16)
        if m > 0:
            pltpu.make_async_copy(ags, ag_h.at[m - 1], osem.at[m - 1, 2]).wait()
        ags[...] = lax.dot_general(left, right, (((0,), (0,)), ((), ())), preferred_element_type=F32)
        pltpu.make_async_copy(ags, ag_h.at[m], osem.at[m, 2]).start()

    def pack_rows(m, k):
        for f in range(F):
            for tap in range(9):
                first, last = tap * g.shard, (tap + 1) * g.shard
                c0 = tap * C + f * g.shard
                pk[m, k, f, first:last, :] = gacc[k, c0 : c0 + g.shard, 0:LANES]
                for lo, hi, lanes in ((0, g.high_rows, 0), (g.high_rows, g.low_rows, CHUNK)):
                    a, b = max(first, lo), min(last, hi)
                    if a < b:
                        at = g.low_rows + a - lo
                        pk[m, k, f, at : at + b - a, lanes : lanes + C - LANES] = gacc[
                            k, c0 + a - first : c0 + b - first, LANES:C
                        ]


    def shifted(v):
        col = lax.broadcasted_iota(jnp.int32, v.shape, 1) & (g.w - 1)
        left = jnp.where(col == 0, 0.0, pltpu.roll(v, 1, 1))
        right = jnp.where(col == g.w - 1, 0.0, pltpu.roll(v, LANES - 1, 1))
        return left, v, right

    def put(buf, s, rows, t, v):
        for j, moved in enumerate(shifted(v)):
            buf[s, j, rows, tile(t)] = moved.astype(BF16)

    def put_edges(buf, s, first_edge, second_edge):
        near = shifted(first_edge)
        far = None if second_edge is None else shifted(second_edge)
        for j in range(3):
            first = buf[s, j, :, tile(1)].astype(F32)
            last = buf[s, j, :, tile(NP)].astype(F32)
            buf[s, j, :, tile(0)] = jnp.where(low_lanes, near[j], pltpu.roll(last, g.w, 1)).astype(BF16)
            buf[s, j, :, tile(NP + 1)] = jnp.where(low_lanes, pltpu.roll(first, g.w, 1), near[j]).astype(BF16)
            if far is not None:
                buf[s, j, :, tile(NP + 2)] = jnp.where(low_lanes, far[j], last).astype(BF16)
                buf[s, j, :, tile(NP + 3)] = near[j].astype(BF16)
                buf[s, j, :, tile(NP + 4)] = jnp.where(low_lanes, first, far[j]).astype(BF16)

    def windows(buf, s, back, edge):
        pieces = []
        for i in range(3):
            for j in range(3):
                ti, tj = (2 - i, 2 - j) if back else (i, j)
                piece = buf[s, tj, :, ti * LANES : ti * LANES + PX]
                if edge:
                    piece = jnp.concatenate([piece, buf[s, tj, :, tile(NP + 2 + ti)]], axis=1)
                pieces.append(piece)
        return jnp.concatenate(pieces, axis=0)

    def chunks():
        return [pl.ds(c0, CHUNK) for c0 in range(0, C, CHUNK)]

    def quads():
        order = [NP - 1] + list(range(NP - 1))
        return [order[q : q + 4] for q in range(0, NP, 4)]

    def clear(count):
        for k in range(count):
            acc[k] = jnp.zeros((C, LANES), F32)

    def total_row(k):
        return jnp.sum(acc[k].T, axis=0, keepdims=True)

    def group_rows(rows):
        high = rows.astype(BF16)
        rest = rows - high.astype(F32)
        middle = rest.astype(BF16)
        low = (rest - middle.astype(F32)).astype(BF16)
        a = lax.broadcasted_iota(jnp.int32, (C, C), 0) // (C // GROUPS)
        b = lax.broadcasted_iota(jnp.int32, (C, C), 1) // (C // GROUPS)
        same = jnp.where(a == b, 1.0, 0.0).astype(BF16)
        three = jnp.dot(jnp.concatenate([high, middle, low], axis=0).astype(BF16), same, preferred_element_type=F32)
        n = rows.shape[0]
        return three[0:n] + three[n : 2 * n] + three[2 * n : 3 * n]

    def stack(*rows):
        fill = 8 - len(rows)
        return jnp.concatenate(list(rows) + [jnp.zeros((fill, C), F32)] * (fill > 0), axis=0)

    def spread(s, k, row):
        prm[s, k] = jnp.broadcast_to(row, (LANES, C)).T

    def save(s, k, row):
        rowt[s, k : k + 1, :] = row

    def row(s, k):
        return rowt[s, k : k + 1, :]

    def moments(total):
        grouped = group_rows(total)
        mean = grouped[0:1] / g.count
        variance = grouped[1:2] / g.count - mean * mean
        return mean, lax.rsqrt(variance + EPSILON)

    def slope_twice(w, t):
        return (1.0 + t) * (1.0 + w * (1.0 - t))

    def pair(buf, s, q):
        return jnp.concatenate([buf[s, q], buf[s, q + NP]], axis=0)

    def pixels(buf, s):
        return jnp.concatenate([buf[s, h] for q in range(NP) for h in (q, q + NP)], axis=0)

    def own_embedding(n):
        whole = emb[n].astype(F32)
        return pltpu.roll(whole, whole.shape[1] - me * g.ef, 1)[:, 0 : g.ef]


    def sums_phase(i, s):
        n = net_of(i)
        pltpu.make_async_copy(x_h.at[n, s], rx.at[s], lx.at[s]).wait()

        def step(h, carry):
            a, b = carry
            v = rx[s, h].astype(F32)
            v = v.reshape(g.w // 8, 8, C)
            return a + jnp.sum(v, axis=0), b + jnp.sum(v * v, axis=0)

        zero = jnp.zeros((8, C), F32)
        a, b = lax.fori_loop(0, R, step, (zero, zero), unroll=4)
        mod = jnp.dot(own_embedding(n).astype(BF16), aff[n], preferred_element_type=F32)
        which = lax.broadcasted_iota(jnp.int32, mod.shape, 0) == s
        mod = jnp.sum(jnp.where(which, mod, 0.0), axis=0, keepdims=True)
        ex1[i, s, me, 0:8] = stack(
            jnp.sum(a, axis=0, keepdims=True), jnp.sum(b, axis=0, keepdims=True), mod[:, 0:C], mod[:, C : 2 * C],
        )
        vectors = jnp.concatenate([gains[n], biases[n]], axis=0).astype(F32)
        vectors = jnp.concatenate([vectors, jnp.zeros((8, 2 * LANES - g.shard), F32)], axis=1)
        ex1[i, s, me, 8:16] = pltpu.roll(vectors, me * g.shard, 1)[:, 0:C]
        rows_start(i, 0, s)

    def weights_ready(i):
        for k in range(2):
            for tap in range(9):
                blocks = [wraw[i % 2, f, k, tap] for f in range(F)]
                if g.shard % 16:
                    blocks = [b.astype(F32) for b in blocks]
                whole = jnp.concatenate(blocks, axis=0).astype(BF16)
                wb[k, :, tap * C : (tap + 1) * C] = whole
                wf[k, :, tap * C : (tap + 1) * C] = whole.T

    def edge_tiles(i, s, t):
        near = jnp.concatenate([hb[i % 2, s, t, 0, 1], hb[i % 2, s, t, 1, 0]], axis=0).T.astype(F32)
        far = jnp.concatenate([hb[i % 2, s, t, 0, 0], hb[i % 2, s, t, 1, 1]], axis=0).T.astype(F32)
        return near, far

    def first_phase(i, s):
        kf = kept(s)
        pltpu.make_async_copy(gy_h.at[net_of(i), s], rg.at[s], lg.at[s]).wait()
        halo_take(i, s, 0)
        halo_take(i, s, 1)
        total = rows_take(i, 0, s)
        mean, inverse = moments(total[0:8])
        save(s, MU0, mean)
        save(s, R0, inverse)
        gain0, gain1 = total[8:9], total[9:10]
        save(s, G0, gain0)
        save(s, G1, gain1)
        save(s, B2, total[12:13])
        save(s, B3, total[13:14])
        save(s, SC1, total[2:3] + total[14:15] + 1.0)
        save(s, SH, total[3:4] + total[15:16])
        scale = inverse * gain0
        spread(s, PA0, 0.5 * scale)
        spread(s, PB0, 0.5 * (total[10:11] - mean * scale))
        spread(s, PMU0, mean)
        spread(s, PBIAS, total[11:12])
        clear(3)

        def act(xf, a, b):
            w = xf * a + b
            return w * jnp.tanh(w) + w

        def body(qs):
            for q in qs:
                xc[s, :, tile(q)] = pair(rx, s, q).T
            for rows in chunks():
                a, b = prm[s, PA0, rows], prm[s, PB0, rows]
                for q in qs:
                    put(xa0, s, rows, q + 1, act(xc[s, rows, tile(q)].astype(F32), a, b))

        def edges():
            near, far = edge_tiles(i, s, 0)
            near = jnp.where(edge_ok, act(near, prm[s, PA0], prm[s, PB0]), 0.0)
            far = jnp.where(edge_ok, act(far, prm[s, PA0], prm[s, PB0]), 0.0)
            put_edges(xa0, s, near, far)

        for n, qs in enumerate(quads()):
            body(qs)
            if n == 0:
                edges()
        hbuf[s] = jnp.dot(wf[0], windows(xa0, s, False, True), preferred_element_type=F32)
        for q in range(NP + 1):
            for rows in chunks():
                h = hbuf[s, rows, tile(q)] + prm[s, PBIAS, rows]
                hbuf[s, rows, tile(q)] = h
                if q < NP:
                    acc[0, rows] = acc[0, rows] + h
                    acc[1, rows] = acc[1, rows] + h * h
        for qs in quads():
            for q in qs:
                gc[s, :, tile(q)] = (pair(rg, s, q).T.astype(F32) * kf).astype(BF16)
            for rows in chunks():
                a2 = acc[2, rows]
                for q in qs:
                    gf = gc[s, rows, tile(q)].astype(F32)
                    a2 = a2 + gf
                    put(xg, s, rows, q + 1, gf)
                acc[2, rows] = a2
        near, far = edge_tiles(i, s, 1)
        put_edges(xg, s, jnp.where(edge_ok, near, 0.0) * kf, jnp.where(edge_ok, far, 0.0) * kf)
        ex2[i, 0, s, me] = stack(total_row(0), total_row(1), total_row(2))
        rows_start(i, 1, s)

    def second_phase(i, s):
        total = rows_take(i, 1, s)
        mean, inverse = moments(total)
        save(s, MU1, mean)
        save(s, R1, inverse)
        save(s, SUMH, total[0:1])
        save(s, SGY, total[2:3])
        scale = inverse * row(s, G1)
        spread(s, PA1, 0.5 * scale * row(s, SC1))
        spread(s, PB1, 0.5 * (row(s, SH) + (row(s, B2) - mean * scale) * row(s, SC1)))
        spread(s, PMU1, mean)
        clear(2)
        dub[s] = jnp.dot(wb[1], windows(xg, s, True, True), preferred_element_type=F32)
        for q in range(NP + 1):
            for rows in chunks():
                a, b, mu = prm[s, PA1, rows], prm[s, PB1, rows], prm[s, PMU1, rows]
                h = hbuf[s, rows, tile(q)]
                w = h * a + b
                t = jnp.tanh(w)
                d = dub[s, rows, tile(q)] * slope_twice(w, t)
                dub[s, rows, tile(q)] = d
                if q < NP:
                    put(xa1, s, rows, q + 1, w * t + w)
                    acc[0, rows] = acc[0, rows] + d
                    acc[1, rows] = acc[1, rows] + d * (h - mu)
        w = hbuf[s, :, tile(NP)] * prm[s, PA1] + prm[s, PB1]
        put_edges(xa1, s, jnp.where(edge_ok, w * jnp.tanh(w) + w, 0.0), None)
        ex2[i, 1, s, me] = stack(0.5 * total_row(0), 0.5 * total_row(1))
        rows_start(i, 2, s)

    def out_copy(i, s):
        return pltpu.make_async_copy(yc.at[s], y_h.at[net_of(i), s], ysem.at[s])

    def in_grad_copy(i, s):
        return pltpu.make_async_copy(yc.at[s], dx_h.at[net_of(i), s], ysem.at[s])

    def third_phase(i, s):
        kf = kept(s)

        @pl.when(i > 0)
        def _():
            in_grad_copy(i, s).wait()

        total = rows_take(i, 2, s)
        s1, s2 = total[0:1], total[1:2] * row(s, R1)
        sc1, gain1, inverse, mean = row(s, SC1), row(s, G1), row(s, R1), row(s, MU1)
        grouped = group_rows(stack(gain1 * sc1 * s1, gain1 * sc1 * s2))
        m1, m2 = grouped[0:1] / g.count, grouped[1:2] / g.count
        a = inverse * sc1 * gain1
        b = -inverse * inverse * m2
        c = -inverse * m1 - mean * b
        spread(s, PDA, 0.5 * a)
        spread(s, PDB, b)
        spread(s, PDC, c)
        spread(s, PBIAS, row(s, B3))
        dscale = gain1 * s2 + row(s, B2) * s1
        here = sb.at[i, dp]
        here[1:2, 0:C] = here[1:2, 0:C] + sc1 * s2
        here[3:4, 0:C] = here[3:4, 0:C] + a * s1 + b * row(s, SUMH) + c * g.pixels
        here[4:5, 0:C] = here[4:5, 0:C] + sc1 * s1
        here[5:6, 0:C] = here[5:6, 0:C] + row(s, SGY)
        here[6:7, 0:C] = here[6:7, 0:C] + dscale
        here[7:8, 0:C] = here[7:8, 0:C] + s1
        modulation = jnp.concatenate([dscale, s1], axis=1).astype(BF16).astype(F32)
        for slot in range(S):
            at = 8 + S + slot
            here[at : at + 1, 0 : 2 * C] = jnp.where(s == slot, modulation, here[at : at + 1, 0 : 2 * C])

        def hidden_grad(with_weights):
            for n, qs in enumerate(quads()):
                for rows in chunks():
                    pa, pb, pc = prm[s, PDA, rows], prm[s, PDB, rows], prm[s, PDC, rows]
                    for q in qs:
                        d = dub[s, rows, tile(q)] * pa + hbuf[s, rows, tile(q)] * pb + pc
                        put(xg, s, rows, q + 1, d)
                if with_weights:
                    for q in qs:
                        flat = xg[s, 1, :, tile(q + 1)].T
                        dhp[s, q] = flat[0 : g.w]
                        dhp[s, q + NP] = flat[g.w : 2 * g.w]
                if n == 0:
                    d = dub[s, :, tile(NP)] * prm[s, PDA] + hbuf[s, :, tile(NP)] * prm[s, PDB] + prm[s, PDC]
                    put_edges(xg, s, jnp.where(edge_ok, d, 0.0), None)
            if with_weights:
                o = jnp.dot(windows(xa1, s, False, False), pixels(rg, s), preferred_element_type=F32)
                gacc[1] = gacc[1] + o * kf

        def output(with_weights):
            dub[s, :, 0:PX] = jnp.dot(wf[1], windows(xa1, s, False, False), preferred_element_type=F32)
            for q in range(NP):
                for rows in chunks():
                    v = dub[s, rows, tile(q)] + prm[s, PBIAS, rows]
                    v = (v + xc[s, rows, tile(q)].astype(F32)) * kf
                    yc[s, rows, tile(q)] = v.astype(BF16)
            if with_weights:
                gacc[0] = gacc[0] + jnp.dot(windows(xa0, s, False, False), pixels(dhp, s), preferred_element_type=F32)

        for piece in (hidden_grad, output):
            pl.when(i < 2)(functools.partial(piece, True))
            pl.when(i == 2)(functools.partial(piece, False))

        out_copy(i, s).start()

    def fourth_phase(i, s):
        clear(2)
        hbuf[s, :, 0:PX] = jnp.dot(wb[0], windows(xg, s, True, False), preferred_element_type=F32)
        for q in range(NP):
            for rows in chunks():
                xf = xc[s, rows, tile(q)].astype(F32)
                w = xf * prm[s, PA0, rows] + prm[s, PB0, rows]
                d = hbuf[s, rows, tile(q)] * slope_twice(w, jnp.tanh(w))
                hbuf[s, rows, tile(q)] = d
                acc[0, rows] = acc[0, rows] + d
                acc[1, rows] = acc[1, rows] + d * (xf - prm[s, PMU0, rows])
        ex2[i, 2, s, me] = stack(0.5 * total_row(0), 0.5 * total_row(1))
        rows_start(i, 3, s)

    def last_phase(i, s):
        total = rows_take(i, 3, s)
        inverse, mean, gain0 = row(s, R0), row(s, MU0), row(s, G0)
        s3, s4 = total[0:1], total[1:2] * inverse
        grouped = group_rows(stack(gain0 * s3, gain0 * s4))
        m1, m2 = grouped[0:1] / g.count, grouped[1:2] / g.count
        b = -inverse * inverse * m2
        spread(s, PA1, 0.5 * inverse * gain0)
        spread(s, PB1, b)
        spread(s, PMU1, -inverse * m1 - mean * b)
        here = sb.at[i, dp]
        here[0:1, 0:C] = here[0:1, 0:C] + s4
        here[2:3, 0:C] = here[2:3, 0:C] + s3
        out_copy(i, s).wait()
        for qs in quads():
            for rows in chunks():
                pa, pb, pc = prm[s, PA1, rows], prm[s, PB1, rows], prm[s, PMU1, rows]
                for q in qs:
                    xf = xc[s, rows, tile(q)].astype(F32)
                    v = hbuf[s, rows, tile(q)] * pa + xf * pb + pc + gc[s, rows, tile(q)].astype(F32)
                    yc[s, rows, tile(q)] = v.astype(BF16)
        in_grad_copy(i, s).start()


    final = list(range(5, g.stages + 1))
    plan = {
        (0, 3, S - 1): [(0, 0)],
        (0, 4, S - 1): [(0, 1)],
        (1, 2, 0): [(0, 2)],
        (1, 3, 0): [(0, 3)],
        (1, 3, S - 1): [(1, 0)],
        (1, 4, S - 1): [(0, 4), (1, 1)],
        (2, 1, S - 1): [(0, t) for t in final[:-1]],
        (2, 2, 0): [(1, 2)],
        (2, 2, S - 1): [(0, final[-1])],
        (2, 3, 0): [(1, 3)],
        (2, 5, S - 1): [(1, 4)] + [(1, t) for t in final],
    }

    def slots(number, phase, i):
        def step(s, carry):
            phase(i, s)
            for (at, where, slot), ticks in plan.items():
                if where == number:
                    @pl.when((i == at) & (s == slot))
                    def _():
                        for m, t in ticks:
                            tick(m, t)
            return carry

        lax.fori_loop(0, S, step, 0)

    def load_x(i):
        for s in range(S):
            pltpu.make_async_copy(x_h.at[net_of(i), s], rx.at[s], lx.at[s]).start()

    def load_gy(i):
        for s in range(S):
            pltpu.make_async_copy(gy_h.at[net_of(i), s], rg.at[s], lg.at[s]).start()

    load_x(0)
    load_gy(0)
    fill = g.low_rows + g.high_rows
    pk[:, :, :, fill:, :] = jnp.zeros((2, 2, F, g.pack - fill, LANES), F32)
    sb[:, dp] = jnp.zeros((3, 16, g.wide), F32)
    for n in range(g.nets):
        own = own_embedding(n)
        for i in range(3):
            if (2 * i) % g.nets == n:
                sb[i, dp, 8 : 8 + S, 0 : g.ef] = own.astype(F32)

    @pl.when(me == 0)
    def _():
        hb[:, :, :, 0] = jnp.zeros(hb.shape[:3] + hb.shape[4:], BF16)

    @pl.when(me == F - 1)
    def _():
        hb[:, :, :, 1] = jnp.zeros(hb.shape[:3] + hb.shape[4:], BF16)

    barrier = pltpu.get_barrier_semaphore()
    partners = [(b,) for b in range(g.bits)] + [(1, 2)]
    for df in range(1, F):
        pl.semaphore_signal(barrier, inc=1, device_id={"fsdp": peer(df)}, device_id_type=MESH)
    for bits in partners:
        pl.semaphore_signal(barrier, inc=1, device_id={"dp": other(*bits)}, device_id_type=MESH)
    pl.semaphore_wait(barrier, F - 1 + len(partners))
    halos_start(0, 0)
    weights_start(0)
    slots(0, sums_phase, 0)
    halos_start(0, 1)

    def network(i, carry):
        @pl.when(i < 2)
        def _():
            gacc[...] = jnp.zeros(gacc.shape, F32)

        weights_forward(i)
        weights_take(i)
        weights_ready(i)
        slots(1, first_phase, i)
        weights_sent(i)

        @pl.when(i < 2)
        def _():
            load_x(i + 1)
            halos_start(i + 1, 0)
            weights_start(i + 1)
            halos_start(i + 1, 1)

        slots(2, second_phase, i)
        slots(3, third_phase, i)

        @pl.when(i < 2)
        def _():
            load_gy(i + 1)

        slots(4, fourth_phase, i)

        @pl.when(i < 2)
        def _():
            slots(0, sums_phase, i + 1)

        slots(5, last_phase, i)
        return carry

    lax.fori_loop(0, 3, network, 0)


    def drain(i, carry):
        for s in range(S):
            for t in range(2):
                halo_sent(i, s, t)
            for e in range(4):
                for df in range(1, F):
                    row_copy(i, e, s, df, me).wait_send()
        for df in range(1, F):
            weight_copy(i, df, me).wait_send()
        return carry

    lax.fori_loop(0, 3, drain, 0)
    for s in range(S):
        in_grad_copy(2, s).wait()
    for m in range(2):
        for k in range(2):
            pltpu.make_async_copy(pk.at[m, k, me], cg_h.at[m, k], osem.at[m, k]).wait()
    pltpu.make_async_copy(ags, ag_h.at[1], osem.at[1, 2]).wait()


def place_body(g, y_c, dx_c, packed, affine, sums, y, dx, conv, affine_out, gain_out, bias_out):
    for src, dst in ((y_c, y), (dx_c, dx)):
        for q in range(g.np):
            flat = src[0, 0, :, q * LANES : (q + 1) * LANES].T
            dst[0, 0, q] = flat[0 : g.w]
            dst[0, 0, q + g.np] = flat[g.w : 2 * g.w]
    step = pl.program_id(0)

    @pl.when(step < 4)
    def _():
        split = g.low_rows - g.high_rows
        rest = g.c - LANES
        conv[0, 0, :, 0:LANES] = packed[0, 0, 0 : g.low_rows, :]
        conv[0, 0, 0 : g.high_rows, LANES : g.c] = packed[0, 0, g.low_rows : g.low_rows + g.high_rows, 0:rest]
        conv[0, 0, g.high_rows : g.low_rows, LANES : g.c] = packed[
            0, 0, g.low_rows : g.low_rows + split, CHUNK : CHUNK + rest
        ]

    @pl.when(step < 2)
    def _():
        affine_out[...] = affine[...]

    @pl.when(step == 0)
    def _():
        gain_out[...] = sums[:, 0:2, 0 : g.shard]
        bias_out[...] = sums[:, 2:8, 0 : g.shard]


def on_device(
    block_input, embedding, out_cotangent, conv_weights, affine_weight, gains, biases, counts
):
    nets, slots, rows, width, chans = block_input.shape
    fsdp = lax.axis_size("fsdp")
    dp = lax.axis_size("dp")
    embed_rows = affine_weight.shape[1]
    g = settings(dp, fsdp, nets, slots, rows, width, chans, embed_rows)
    weights = conv_weights.reshape(nets, 2, 9, g.shard, chans)

    tiles = (g.np + 1) * LANES
    dma = pltpu.SemaphoreType.DMA
    scratch = [
        pltpu.VMEM((slots, rows, width, chans), BF16),
        pltpu.VMEM((slots, rows, width, chans), BF16),
        pltpu.VMEM((slots, rows, width, chans), BF16),
        pltpu.VMEM((slots, chans, g.px), BF16),
        pltpu.VMEM((slots, chans, g.px), BF16),
        pltpu.VMEM((slots, 3, chans, (g.np + 5) * LANES), BF16),
        pltpu.VMEM((slots, 3, chans, (g.np + 2) * LANES), BF16),
        pltpu.VMEM((slots, 3, chans, (g.np + 5) * LANES), BF16),
        pltpu.VMEM((2, slots, 2, 2, 2, width, chans), BF16),
        pltpu.VMEM((slots, chans, tiles), F32),
        pltpu.VMEM((slots, chans, tiles), F32),
        pltpu.VMEM((2, fsdp, 2, 9, g.shard, chans), BF16),
        pltpu.VMEM((2, chans, 9 * chans), BF16),
        pltpu.VMEM((2, chans, 9 * chans), BF16),
        pltpu.VMEM((2, 9 * chans, chans), F32),
        pltpu.VMEM((2, 2, fsdp, g.pack, LANES), F32),
        pltpu.VMEM((2, fsdp, g.half, LANES), F32),
        pltpu.VMEM((2, 3, fsdp, g.piece, LANES), F32),
        pltpu.VMEM((2, fsdp - 1, g.piece, LANES), F32),
        pltpu.VMEM((2, fsdp - 1, g.half, LANES), F32),
        pltpu.VMEM((2, g.bits - 3, g.piece, LANES), F32),
        pltpu.VMEM((slots, chans, g.px), BF16),
        pltpu.VMEM((embed_rows, 2 * chans), F32),
        pltpu.VMEM((3, slots, fsdp, 16, chans), F32),
        pltpu.VMEM((3, 3, slots, fsdp, 8, chans), F32),
        pltpu.VMEM((3, dp, 16, g.wide), F32),
        pltpu.VMEM((3, chans, LANES), F32),
        pltpu.VMEM((slots, 16, chans), F32),
        pltpu.VMEM((slots, 10, chans, LANES), F32),
        dma((slots,)),
        dma((slots,)),
        dma((slots,)),
        dma((3, slots, 2, 2)),
        dma((3, slots, 2, 2)),
        dma((3, 4, slots, fsdp)),
        dma((3, 4, slots, fsdp)),
        dma((3,)),
        dma((3, fsdp)),
        dma((3, fsdp)),
        dma((3, fsdp)),
        dma((3, fsdp)),
        dma((2, 2, g.stages, max(3, fsdp))),
        dma((2, 2, g.stages, max(3, fsdp))),
        dma((2, g.bits + 2)),
        dma((2, g.bits + 2)),
        dma((2, 3)),
    ]
    hbm = pl.BlockSpec(memory_space=pl.ANY)
    vmem = pl.BlockSpec(memory_space=pltpu.VMEM)
    smem = pl.BlockSpec(memory_space=pltpu.SMEM)
    channel_major = jax.ShapeDtypeStruct((nets, slots, chans, g.px), BF16)
    main = pl.pallas_call(
        functools.partial(kernel_body, g),
        out_shape=(
            channel_major,
            channel_major,
            jax.ShapeDtypeStruct((2, 2, g.pack, LANES), F32),
            jax.ShapeDtypeStruct((2, embed_rows, 2 * chans), F32),
            jax.ShapeDtypeStruct((2, 8, 2 * LANES), F32),
        ),
        in_specs=[hbm, hbm, hbm, vmem, vmem, vmem, vmem, smem],
        out_specs=(hbm, hbm, hbm, hbm, vmem),
        scratch_shapes=scratch,
        compiler_params=pltpu.CompilerParams(
            collective_id=0, has_side_effects=True, vmem_limit_bytes=64 << 20
        ),
    )(block_input, out_cotangent, weights, affine_weight, embedding, gains, biases, counts)

    def by_slot(step):
        return (step // slots, step % slots, 0, 0)

    def by_conv(step):
        return (jnp.minimum(step, 3) // 2, jnp.minimum(step, 3) % 2, 0, 0)

    def by_net(step):
        return (jnp.minimum(step, 1), 0, 0)

    image = pl.BlockSpec((1, 1, rows, width, chans), lambda step: by_slot(step) + (0,))
    block_output, input_grad, conv_grads, affine_grad, gain_grads, bias_grads = pl.pallas_call(
        functools.partial(place_body, g),
        grid=(nets * slots,),
        out_shape=(
            jax.ShapeDtypeStruct(block_input.shape, BF16),
            jax.ShapeDtypeStruct(block_input.shape, BF16),
            jax.ShapeDtypeStruct((2, 2, g.low_rows, chans), F32),
            jax.ShapeDtypeStruct((2, embed_rows, 2 * chans), F32),
            jax.ShapeDtypeStruct((2, 2, g.shard), F32),
            jax.ShapeDtypeStruct((2, 6, g.shard), F32),
        ),
        in_specs=[
            pl.BlockSpec((1, 1, chans, g.px), by_slot),
            pl.BlockSpec((1, 1, chans, g.px), by_slot),
            pl.BlockSpec((1, 1, g.pack, LANES), by_conv),
            pl.BlockSpec((1, embed_rows, 2 * chans), by_net),
            vmem,
        ],
        out_specs=(
            image,
            image,
            pl.BlockSpec((1, 1, g.low_rows, chans), by_conv),
            pl.BlockSpec((1, embed_rows, 2 * chans), by_net),
            vmem,
            vmem,
        ),
        compiler_params=pltpu.CompilerParams(vmem_limit_bytes=48 << 20),
    )(*main)
    conv_grads = conv_grads.reshape(2, 2, 3, 3, g.shard, chans)
    return block_output, input_grad, conv_grads, affine_grad, gain_grads, bias_grads


def solution(mesh):
    placed = (
        P(None, "dp", "fsdp", None, None),
        P(None, "dp", None),
        P(None, "dp", "fsdp", None, None),
        P(None, None, None, None, "fsdp", None),
        P(None, "fsdp", None),
        P(None, None, "fsdp"),
        P(None, None, "fsdp"),
        P("dp"),
    )
    return jax.shard_map(
        on_device,
        mesh=mesh,
        in_specs=placed,
        out_specs=(
            P(None, "dp", "fsdp", None, None),
            P(None, "dp", "fsdp", None, None),
            P(None, None, None, None, "fsdp", None),
            P(None, "fsdp", None),
            P(None, None, "fsdp"),
            P(None, None, "fsdp"),
        ),
        check_vma=False,
    )
```

```python
import functools
import types

import jax
import jax.numpy as jnp
from jax import lax
from jax.experimental import pallas as pl
from jax.experimental.pallas import tpu as pltpu
from jax.sharding import PartitionSpec as P

GROUPS = 32
EPSILON = 1e-05
LANES = 128
CHUNK = 64
MESH = pl.DeviceIdType.MESH
F32 = jnp.float32
BF16 = jnp.bfloat16

MU0, R0, G0, G1, B1, B2, B3, SC1, SH, SGY, MU1, R1, SUMH = range(13)
PA0, PB0, PMU0, PBIAS, PA1, PB1, PMU1, PDA, PDB, PDC = range(10)


def settings(dp_size, fsdp_size, nets, slots, rows, width, chans, embed_rows):
    g = types.SimpleNamespace()
    g.dp, g.f, g.nets, g.s, g.r, g.w, g.c, g.ef = (
        dp_size, fsdp_size, nets, slots, rows, width, chans, embed_rows,
    )
    g.np = rows // 2
    g.px = g.np * LANES
    g.count = float(rows * fsdp_size * width * (chans // GROUPS))
    g.pixels = float(rows * fsdp_size * width)
    g.bits = dp_size.bit_length() - 1
    g.shard = chans // fsdp_size
    g.low_rows = 9 * g.shard
    g.high_rows = -(-g.low_rows // 16) * 8
    g.pack = -(-(g.low_rows + g.high_rows) // 64) * 64
    g.half = g.pack // 2
    g.piece = g.pack // 8
    g.wide = max(2 * chans, embed_rows)
    g.stages = g.bits + 2
    g.split = 2 if g.shard % 32 == 0 else 1
    g.rows = g.shard // g.split
    return g


def kernel_body(
    g,
    x_h, gy_h, w_h, aff, emb, gains, biases, counts,
    y_h, dx_h, cg_h, ag_h, sg,
    rx, rg, dhp, xc, gc, xa0, xa1, xg, hb, hbuf, dub, wraw, wf, wb, gacc, pk, r0b, r1b, ryb, rbb,
    ybuf, yc, ags, ex1, ex2, sb, acc, rowt, prm,
    lx, lg, ysem, hs, hr, es, er, wl, wys, wyr, wcs, wcr, cs, cr, ss, sr, osem,
):
    me = lax.axis_index("fsdp")
    dp = lax.axis_index("dp")
    C, NP, F, S, R = g.c, g.np, g.f, g.s, g.r
    PX = g.px

    def net_of(i):
        return (2 * i) % g.nets

    def peer(df):
        return (me + df) % F

    def source(df):
        return (me + F - df) % F

    def bit(b):
        return (dp // (1 << b)) % 2

    def other(*bits):
        where = dp
        for b in bits:
            where = where + (1 << b) * (1 - 2 * bit(b))
        return where

    def remote(src, dst, send, recv, where):
        return pltpu.make_async_remote_copy(
            src_ref=src, dst_ref=dst, send_sem=send, recv_sem=recv,
            device_id=where, device_id_type=MESH,
        )

    def tile(t):
        if isinstance(t, int):
            return pl.ds(t * LANES, LANES)
        return pl.ds(pl.multiple_of(t * LANES, LANES), LANES)

    def kept(s):
        return jnp.where(s < counts[0], 1.0, 0.0)

    lane = lax.broadcasted_iota(jnp.int32, (C, LANES), 1)
    low_lanes = lane < g.w
    top = (me > 0).astype(jnp.int32)
    bottom = (me < F - 1).astype(jnp.int32)
    edge_ok = jnp.where(low_lanes, top, bottom) > 0


    def halo_copy(i, s, t, down):
        src = (x_h, gy_h)[t]
        n = net_of(i)
        if down:
            return remote(
                src.at[n, s, pl.ds(R - 2, 2)], hb.at[i % 2, s, t, 0],
                hs.at[i, s, t, 1], hr.at[i, s, t, 1], {"fsdp": (me + 1) % F},
            )
        return remote(
            src.at[n, s, pl.ds(0, 2)], hb.at[i % 2, s, t, 1],
            hs.at[i, s, t, 0], hr.at[i, s, t, 0], {"fsdp": (me + F - 1) % F},
        )

    def halo_start(i, s, t):
        @pl.when(me > 0)
        def _():
            halo_copy(i, s, t, False).start()

        @pl.when(me < F - 1)
        def _():
            halo_copy(i, s, t, True).start()

    def halo_take(i, s, t):
        @pl.when(me > 0)
        def _():
            halo_copy(i, s, t, True).wait_recv()

        @pl.when(me < F - 1)
        def _():
            halo_copy(i, s, t, False).wait_recv()

    def halo_sent(i, s, t):
        @pl.when(me > 0)
        def _():
            halo_copy(i, s, t, False).wait_send()

        @pl.when(me < F - 1)
        def _():
            halo_copy(i, s, t, True).wait_send()

    def row_copy(i, e, s, df, who):
        ref = ex1.at[i, s, who] if e == 0 else ex2.at[i, e - 1, s, who]
        return remote(ref, ref, es.at[i, e, s, df], er.at[i, e, s, df], {"fsdp": peer(df)})

    def rows_start(i, e, s):
        for df in range(1, F):
            row_copy(i, e, s, df, me).start()

    def rows_take(i, e, s):
        for df in range(1, F):
            row_copy(i, e, s, df, source(df)).wait_recv()
        parts = [ex1[i, s, f] if e == 0 else ex2[i, e - 1, s, f] for f in range(F)]
        total = parts[0]
        for part in parts[1:]:
            total = total + part
        return total

    mine = dp % 2

    TRIPLES = 3

    def weight_rows(half):
        return pl.ds(pl.multiple_of(half * g.rows, g.rows), g.rows)

    def weight_copy(i, k, j, df, who):
        taps, rows = pl.ds(3 * j, 3), weight_rows(mine if g.split == 2 else 0)
        return remote(
            w_h.at[net_of(i), k, taps, rows], wraw.at[i % 2, who, k, taps, rows],
            wys.at[i, k, j, df], wyr.at[i, k, j, df], {"fsdp": peer(df)},
        )

    def weight_share(i, k, df, half):
        ref = wraw.at[i % 2, source(df), k, :, weight_rows(half)]
        return remote(ref, ref, wcs.at[i, k, df], wcr.at[i, k, df], {"dp": other(0)})

    def weight_local(i):
        return pltpu.make_async_copy(w_h.at[net_of(i)], wraw.at[i % 2, me], wl.at[i])

    def weights_start(i, k, j):
        for df in range(1, F):
            weight_copy(i, k, j, df, me).start()

    def weights_forward(i, k):
        for df in range(1, F):
            for j in range(TRIPLES):
                weight_copy(i, k, j, df, source(df)).wait_recv()
            if g.split == 2:
                weight_share(i, k, df, mine).start()

    def weights_take(i, k):
        if g.split == 2:
            for df in range(1, F):
                weight_share(i, k, df, 1 - mine).wait_recv()

    def weights_sent(i):
        for k in range(2):
            for df in range(1, F):
                for j in range(TRIPLES):
                    weight_copy(i, k, j, df, me).wait_send()
                if g.split == 2:
                    weight_share(i, k, df, mine).wait_send()


    def rows_at(offset, size):
        if not isinstance(offset, int):
            offset = pl.multiple_of(offset, 8)
        return pl.ds(offset, size)

    half_start = bit(0) * g.half
    PAIR = ((1,), (2,), (1, 2))

    def piece_start(bits):
        b1 = 1 - bit(1) if 1 in bits else bit(1)
        b2 = 1 - bit(2) if 2 in bits else bit(2)
        return half_start + (2 * b1 + b2) * g.piece

    def core_sums(m, k):
        return r0b.at[0 if g.split == 2 else m, k]

    def stage_copies(m, k, t):
        def sems(j):
            return cs.at[m, k, t, j], cr.at[m, k, t, j]

        mine_at = rows_at(piece_start(()), g.piece)
        own = pk.at[m, k, me, mine_at]
        if t == 0:
            there = rows_at((1 - bit(0)) * g.half, g.half)
            return [(remote(pk.at[m, k, :, there], core_sums(m, k), *sems(0), {"dp": other(0)}), None)]
        if t == 1:
            return [
                (
                    remote(
                        pk.at[m, k, :, rows_at(piece_start(bits), g.piece)], r1b.at[k, j],
                        *sems(j), {"dp": other(*bits)},
                    ),
                    None,
                )
                for j, bits in enumerate(PAIR)
            ]
        if t == 2:
            return [
                (remote(pk.at[m, k, peer(df), mine_at], ryb.at[m, k, df - 1], *sems(df - 1), {"fsdp": peer(df)}), None)
                for df in range(1, F)
            ]
        if t < g.bits:
            return [(remote(own, rbb.at[k, t - 3], *sems(0), {"dp": other(t)}), None)]
        if t == g.bits:
            return [
                (
                    remote(own, own, *sems(j), {"dp": other(*bits)}),
                    remote(own, pk.at[m, k, me, rows_at(piece_start(bits), g.piece)], *sems(j), {"dp": other(*bits)}),
                )
                for j, bits in enumerate(PAIR)
            ]
        own = pk.at[m, k, me, rows_at(half_start, g.half)]
        there = pk.at[m, k, me, rows_at((1 - bit(0)) * g.half, g.half)]
        return [(
            remote(own, own, *sems(0), {"dp": other(0)}), remote(own, there, *sems(0), {"dp": other(0)}),
        )]

    def add_rows(dst, start, sources, size):
        step = max(n for n in range(8, 65, 8) if size % n == 0)

        def body(j, carry):
            at = rows_at(start + j * step, step)
            total = dst[at, :]
            for src in sources:
                total = total + src[rows_at(j * step, step), :]
            dst[at, :] = total
            return carry

        lax.fori_loop(0, size // step, body, 0)

    def stage_start(m, k, t):
        for copy, _ in stage_copies(m, k, t):
            copy.start()

    def stage_finish(m, k, t):
        for copy, received in stage_copies(m, k, t):
            copy.wait_send()
            (received or copy).wait_recv()
        if t == 0:
            for f in range(F):
                add_rows(pk.at[m, k, f], half_start, [core_sums(m, k).at[f]], g.half)
        elif t == 1:
            for f in range(F):
                add_rows(pk.at[m, k, f], piece_start(()), [r1b.at[k, j, f] for j in range(3)], g.piece)
        elif t == 2:
            add_rows(pk.at[m, k, me], piece_start(()), [ryb.at[m, k, df - 1] for df in range(1, F)], g.piece)
        elif t < g.bits:
            add_rows(pk.at[m, k, me], piece_start(()), [rbb.at[k, t - 3]], g.piece)

    place = bit(1) + 2 * bit(2) + 4 * bit(0) + (dp // 8) * 8

    def small_copies(m, r, received):
        targets = PAIR if r == 0 else ((0,),) if r == 1 else ((r + 1,),)
        size = 1 if r == 0 else 1 << (r + 1)
        flips = {1: 1, 2: 2, 0: 4}
        copies = []
        for j, bits in enumerate(targets):
            there = place
            for b in bits:
                there = there + flips.get(b, 1 << b) * (1 - 2 * bit(b))
            own = sb.at[m, pl.ds((place // size) * size, size)]
            dst = sb.at[m, pl.ds((there // size) * size, size)] if received else own
            sem = j if r == 0 else r + 2
            copies.append(remote(own, dst, ss.at[m, sem], sr.at[m, sem], {"dp": other(*bits)}))
        return copies

    def small_start(m, r):
        for copy in small_copies(m, r, False):
            copy.start()

    def small_finish(m, r):
        for copy in small_copies(m, r, False):
            copy.wait_send()
        for copy in small_copies(m, r, True):
            copy.wait_recv()
        if r == g.bits - 2:
            finish_small(m)

    def tick(m, k, t):
        if t == 0:
            pack_rows(m, k)
        else:
            stage_finish(m, k, t - 1)
        if t < g.stages:
            stage_start(m, k, t)
        else:
            pltpu.make_async_copy(pk.at[m, k, me], cg_h.at[m, k], osem.at[m, k]).start()

    def finish_small(m):
        total = sb[m, 0, 0:8, 0 : 2 * LANES]
        for d in range(1, g.dp):
            total = total + sb[m, d, 0:8, 0 : 2 * LANES]
        sg[m] = pltpu.roll(total, 2 * LANES - me * g.shard, 1)
        block = sb[m, :, 8:16, :].reshape(g.dp * 8, g.wide)
        index = lax.broadcasted_iota(jnp.int32, (g.dp * 8, g.ef), 0) & 7
        left = jnp.where(index < S, block[:, : g.ef], 0.0).astype(BF16)
        right = pltpu.roll(block[:, : 2 * C], g.dp * 8 - S, 0).astype(BF16)
        if m > 0:
            pltpu.make_async_copy(ags, ag_h.at[m - 1], osem.at[m - 1, 2]).wait()
        ags[...] = lax.dot_general(left, right, (((0,), (0,)), ((), ())), preferred_element_type=F32)
        pltpu.make_async_copy(ags, ag_h.at[m], osem.at[m, 2]).start()

    def pack_rows(m, k):
        for f in range(F):
            for tap in range(9):
                first, last = tap * g.shard, (tap + 1) * g.shard
                c0 = tap * C + f * g.shard
                pk[m, k, f, first:last, :] = gacc[k, c0 : c0 + g.shard, 0:LANES]
                for lo, hi, lanes in ((0, g.high_rows, 0), (g.high_rows, g.low_rows, CHUNK)):
                    a, b = max(first, lo), min(last, hi)
                    if a < b:
                        at = g.low_rows + a - lo
                        pk[m, k, f, at : at + b - a, lanes : lanes + C - LANES] = gacc[
                            k, c0 + a - first : c0 + b - first, LANES:C
                        ]


    def shifted(v):
        col = lax.broadcasted_iota(jnp.int32, v.shape, 1) & (g.w - 1)
        left = jnp.where(col == 0, 0.0, pltpu.roll(v, 1, 1))
        right = jnp.where(col == g.w - 1, 0.0, pltpu.roll(v, LANES - 1, 1))
        return left, v, right

    def put(buf, s, rows, t, v):
        for j, moved in enumerate(shifted(v)):
            buf[s, j, rows, tile(t)] = moved.astype(BF16)

    def put_edges(buf, s, first_edge, second_edge):
        near = shifted(first_edge)
        far = None if second_edge is None else shifted(second_edge)
        for j in range(3):
            first = buf[s, j, :, tile(1)].astype(F32)
            last = buf[s, j, :, tile(NP)].astype(F32)
            buf[s, j, :, tile(0)] = jnp.where(low_lanes, near[j], pltpu.roll(last, g.w, 1)).astype(BF16)
            buf[s, j, :, tile(NP + 1)] = jnp.where(low_lanes, pltpu.roll(first, g.w, 1), near[j]).astype(BF16)
            if far is not None:
                buf[s, j, :, tile(NP + 2)] = jnp.where(low_lanes, far[j], last).astype(BF16)
                buf[s, j, :, tile(NP + 3)] = near[j].astype(BF16)
                buf[s, j, :, tile(NP + 4)] = jnp.where(low_lanes, first, far[j]).astype(BF16)

    def windows(buf, s, back, edge):
        pieces = []
        for i in range(3):
            for j in range(3):
                ti, tj = (2 - i, 2 - j) if back else (i, j)
                piece = buf[s, tj, :, ti * LANES : ti * LANES + PX]
                if edge:
                    piece = jnp.concatenate([piece, buf[s, tj, :, tile(NP + 2 + ti)]], axis=1)
                pieces.append(piece)
        return jnp.concatenate(pieces, axis=0)

    def chunks():
        return [pl.ds(c0, CHUNK) for c0 in range(0, C, CHUNK)]

    def quads():
        order = [NP - 1] + list(range(NP - 1))
        return [order[q : q + 4] for q in range(0, NP, 4)]

    def clear(count):
        for k in range(count):
            acc[k] = jnp.zeros((C, LANES), F32)

    def total_row(k):
        return jnp.sum(acc[k].T, axis=0, keepdims=True)

    def group_rows(rows):
        high = rows.astype(BF16)
        rest = rows - high.astype(F32)
        middle = rest.astype(BF16)
        low = (rest - middle.astype(F32)).astype(BF16)
        a = lax.broadcasted_iota(jnp.int32, (C, C), 0) // (C // GROUPS)
        b = lax.broadcasted_iota(jnp.int32, (C, C), 1) // (C // GROUPS)
        same = jnp.where(a == b, 1.0, 0.0).astype(BF16)
        three = jnp.dot(jnp.concatenate([high, middle, low], axis=0).astype(BF16), same, preferred_element_type=F32)
        n = rows.shape[0]
        return three[0:n] + three[n : 2 * n] + three[2 * n : 3 * n]

    def stack(*rows):
        fill = 8 - len(rows)
        return jnp.concatenate(list(rows) + [jnp.zeros((fill, C), F32)] * (fill > 0), axis=0)

    def spread(s, k, row):
        prm[s, k] = jnp.broadcast_to(row, (LANES, C)).T

    def save(s, k, row):
        rowt[s, k : k + 1, :] = row

    def row(s, k):
        return rowt[s, k : k + 1, :]

    def moments(total):
        grouped = group_rows(total)
        mean = grouped[0:1] / g.count
        variance = grouped[1:2] / g.count - mean * mean
        return mean, lax.rsqrt(variance + EPSILON)

    def slope_twice(w, t):
        return (1.0 + t) * (1.0 + w * (1.0 - t))

    def pair(buf, s, q):
        return jnp.concatenate([buf[s, q], buf[s, q + NP]], axis=0)

    def pixels(buf, s):
        return jnp.concatenate([buf[s, h] for q in range(NP) for h in (q, q + NP)], axis=0)

    def own_embedding(n):
        whole = emb[n].astype(F32)
        return pltpu.roll(whole, whole.shape[1] - me * g.ef, 1)[:, 0 : g.ef]

    def weight_sums(k, acts, grads, s, factor):
        right = pixels(grads, s)
        for i in range(3):
            left = jnp.concatenate(
                [acts[s, j, :, i * LANES : i * LANES + PX] for j in range(3)], axis=0
            )
            rows = pl.ds(3 * C * i, 3 * C)
            o = jnp.dot(left, right, preferred_element_type=F32)
            gacc[k, rows] = gacc[k, rows] + (o if factor is None else o * factor)


    def sums_phase(i, s):
        n = net_of(i)
        pltpu.make_async_copy(x_h.at[n, s], rx.at[s], lx.at[s]).wait()

        def step(h, carry):
            a, b = carry
            v = rx[s, h].astype(F32)
            v = v.reshape(g.w // 8, 8, C)
            return a + jnp.sum(v, axis=0), b + jnp.sum(v * v, axis=0)

        zero = jnp.zeros((8, C), F32)
        a, b = lax.fori_loop(0, R, step, (zero, zero), unroll=4)
        mod = jnp.dot(own_embedding(n).astype(BF16), aff[n], preferred_element_type=F32)
        which = lax.broadcasted_iota(jnp.int32, mod.shape, 0) == s
        mod = jnp.sum(jnp.where(which, mod, 0.0), axis=0, keepdims=True)
        ex1[i, s, me, 0:8] = stack(
            jnp.sum(a, axis=0, keepdims=True), jnp.sum(b, axis=0, keepdims=True), mod[:, 0:C], mod[:, C : 2 * C],
        )
        vectors = jnp.concatenate([gains[n], biases[n]], axis=0).astype(F32)
        vectors = jnp.concatenate([vectors, jnp.zeros((8, 2 * LANES - g.shard), F32)], axis=1)
        ex1[i, s, me, 8:16] = pltpu.roll(vectors, me * g.shard, 1)[:, 0:C]
        rows_start(i, 0, s)

    def weights_ready(i, k):
        for tap in range(9):
            blocks = [wraw[i % 2, f, k, tap] for f in range(F)]
            if g.shard % 16:
                blocks = [b.astype(F32) for b in blocks]
            whole = jnp.concatenate(blocks, axis=0).astype(BF16)
            wb[k, :, tap * C : (tap + 1) * C] = whole
            wf[k, :, tap * C : (tap + 1) * C] = whole.T

    def edge_tiles(i, s, t):
        near = jnp.concatenate([hb[i % 2, s, t, 0, 1], hb[i % 2, s, t, 1, 0]], axis=0).T.astype(F32)
        far = jnp.concatenate([hb[i % 2, s, t, 0, 0], hb[i % 2, s, t, 1, 1]], axis=0).T.astype(F32)
        return near, far

    def first_phase(i, s):
        kf = kept(s)
        pltpu.make_async_copy(gy_h.at[net_of(i), s], rg.at[s], lg.at[s]).wait()
        halo_take(i, s, 0)
        halo_take(i, s, 1)
        total = rows_take(i, 0, s)
        mean, inverse = moments(total[0:8])
        save(s, MU0, mean)
        save(s, R0, inverse)
        gain0, gain1 = total[8:9], total[9:10]
        save(s, G0, gain0)
        save(s, G1, gain1)
        save(s, B2, total[12:13])
        save(s, B3, total[13:14])
        save(s, SC1, total[2:3] + total[14:15] + 1.0)
        save(s, SH, total[3:4] + total[15:16])
        scale = inverse * gain0
        spread(s, PA0, 0.5 * scale)
        spread(s, PB0, 0.5 * (total[10:11] - mean * scale))
        spread(s, PMU0, mean)
        spread(s, PBIAS, total[11:12])
        clear(3)

        def act(xf, a, b):
            w = xf * a + b
            return w * jnp.tanh(w) + w

        def body(qs):
            for q in qs:
                xc[s, :, tile(q)] = pair(rx, s, q).T
            for rows in chunks():
                a, b = prm[s, PA0, rows], prm[s, PB0, rows]
                for q in qs:
                    put(xa0, s, rows, q + 1, act(xc[s, rows, tile(q)].astype(F32), a, b))

        def edges():
            near, far = edge_tiles(i, s, 0)
            near = jnp.where(edge_ok, act(near, prm[s, PA0], prm[s, PB0]), 0.0)
            far = jnp.where(edge_ok, act(far, prm[s, PA0], prm[s, PB0]), 0.0)
            put_edges(xa0, s, near, far)

        for n, qs in enumerate(quads()):
            body(qs)
            if n == 0:
                edges()
        hbuf[s] = jnp.dot(wf[0], windows(xa0, s, False, True), preferred_element_type=F32)
        for q in range(NP + 1):
            for rows in chunks():
                h = hbuf[s, rows, tile(q)] + prm[s, PBIAS, rows]
                hbuf[s, rows, tile(q)] = h
                if q < NP:
                    acc[0, rows] = acc[0, rows] + h
                    acc[1, rows] = acc[1, rows] + h * h
        for qs in quads():
            for q in qs:
                gc[s, :, tile(q)] = (pair(rg, s, q).T.astype(F32) * kf).astype(BF16)
            for rows in chunks():
                a2 = acc[2, rows]
                for q in qs:
                    gf = gc[s, rows, tile(q)].astype(F32)
                    a2 = a2 + gf
                    put(xg, s, rows, q + 1, gf)
                acc[2, rows] = a2
        near, far = edge_tiles(i, s, 1)
        put_edges(xg, s, jnp.where(edge_ok, near, 0.0) * kf, jnp.where(edge_ok, far, 0.0) * kf)
        ex2[i, 0, s, me] = stack(total_row(0), total_row(1), total_row(2))
        rows_start(i, 1, s)

    def second_phase(i, s):
        total = rows_take(i, 1, s)
        window(2, i, s)
        mean, inverse = moments(total)
        save(s, MU1, mean)
        save(s, R1, inverse)
        save(s, SUMH, total[0:1])
        save(s, SGY, total[2:3])
        scale = inverse * row(s, G1)
        spread(s, PA1, 0.5 * scale * row(s, SC1))
        spread(s, PB1, 0.5 * (row(s, SH) + (row(s, B2) - mean * scale) * row(s, SC1)))
        spread(s, PMU1, mean)
        clear(2)
        dub[s] = jnp.dot(wb[1], windows(xg, s, True, True), preferred_element_type=F32)
        for q in range(NP + 1):
            for rows in chunks():
                a, b, mu = prm[s, PA1, rows], prm[s, PB1, rows], prm[s, PMU1, rows]
                h = hbuf[s, rows, tile(q)]
                w = h * a + b
                t = jnp.tanh(w)
                d = dub[s, rows, tile(q)] * slope_twice(w, t)
                dub[s, rows, tile(q)] = d
                if q < NP:
                    put(xa1, s, rows, q + 1, w * t + w)
                    acc[0, rows] = acc[0, rows] + d
                    acc[1, rows] = acc[1, rows] + d * (h - mu)
        w = hbuf[s, :, tile(NP)] * prm[s, PA1] + prm[s, PB1]
        put_edges(xa1, s, jnp.where(edge_ok, w * jnp.tanh(w) + w, 0.0), None)
        ex2[i, 1, s, me] = stack(0.5 * total_row(0), 0.5 * total_row(1))
        rows_start(i, 2, s)

        @pl.when(i < 2)
        def _():
            weight_sums(1, xa1, rg, s, kept(s))

    def out_copy(i, s):
        return pltpu.make_async_copy(yc.at[s], y_h.at[net_of(i), s], ysem.at[s])

    def in_grad_copy(i, s):
        return pltpu.make_async_copy(yc.at[s], dx_h.at[net_of(i), s], ysem.at[s])

    def third_phase(i, s):
        kf = kept(s)
        total = rows_take(i, 2, s)
        window(3, i, s)
        spread(s, PBIAS, row(s, B3))
        s1, s2 = total[0:1], total[1:2] * row(s, R1)
        sc1, gain1, inverse, mean = row(s, SC1), row(s, G1), row(s, R1), row(s, MU1)
        grouped = group_rows(stack(gain1 * sc1 * s1, gain1 * sc1 * s2))
        m1, m2 = grouped[0:1] / g.count, grouped[1:2] / g.count
        a = inverse * sc1 * gain1
        b = -inverse * inverse * m2
        c = -inverse * m1 - mean * b
        spread(s, PDA, 0.5 * a)
        spread(s, PDB, b)
        spread(s, PDC, c)
        dscale = gain1 * s2 + row(s, B2) * s1
        here = sb.at[i, place]
        here[1:2, 0:C] = here[1:2, 0:C] + sc1 * s2
        here[3:4, 0:C] = here[3:4, 0:C] + a * s1 + b * row(s, SUMH) + c * g.pixels
        here[4:5, 0:C] = here[4:5, 0:C] + sc1 * s1
        here[5:6, 0:C] = here[5:6, 0:C] + row(s, SGY)
        here[6:7, 0:C] = here[6:7, 0:C] + dscale
        here[7:8, 0:C] = here[7:8, 0:C] + s1
        modulation = jnp.concatenate([dscale, s1], axis=1).astype(BF16).astype(F32)
        for slot in range(S):
            at = 8 + S + slot
            here[at : at + 1, 0 : 2 * C] = jnp.where(s == slot, modulation, here[at : at + 1, 0 : 2 * C])

        def output():
            for q in range(NP):
                for rows in chunks():
                    v = ybuf[rows, tile(q)] + prm[s, PBIAS, rows]
                    v = (v + xc[s, rows, tile(q)].astype(F32)) * kf
                    yc[s, rows, tile(q)] = v.astype(BF16)

        def hidden_grad(with_weights):
            ybuf[...] = jnp.dot(wf[1], windows(xa1, s, False, False), preferred_element_type=F32)
            for n, qs in enumerate(quads()):
                for rows in chunks():
                    pa, pb, pc = prm[s, PDA, rows], prm[s, PDB, rows], prm[s, PDC, rows]
                    for q in qs:
                        d = dub[s, rows, tile(q)] * pa + hbuf[s, rows, tile(q)] * pb + pc
                        put(xg, s, rows, q + 1, d)
                if with_weights:
                    for q in qs:
                        flat = xg[s, 1, :, tile(q + 1)].T
                        dhp[s, q] = flat[0 : g.w]
                        dhp[s, q + NP] = flat[g.w : 2 * g.w]
                if n == 0:
                    d = dub[s, :, tile(NP)] * prm[s, PDA] + hbuf[s, :, tile(NP)] * prm[s, PDB] + prm[s, PDC]
                    put_edges(xg, s, jnp.where(edge_ok, d, 0.0), None)

        @pl.when(i > 0)
        def _():
            in_grad_copy(i, s).wait()

        @pl.when(i < 2)
        def _():
            hidden_grad(True)
            output()
            weight_sums(0, xa0, dhp, s, None)

        @pl.when(i == 2)
        def _():
            hidden_grad(False)
            output()

        out_copy(i, s).start()

    def fourth_phase(i, s):
        window(4, i, s)
        clear(2)
        hbuf[s, :, 0:PX] = jnp.dot(wb[0], windows(xg, s, True, False), preferred_element_type=F32)
        for q in range(NP):
            for rows in chunks():
                xf = xc[s, rows, tile(q)].astype(F32)
                w = xf * prm[s, PA0, rows] + prm[s, PB0, rows]
                d = hbuf[s, rows, tile(q)] * slope_twice(w, jnp.tanh(w))
                hbuf[s, rows, tile(q)] = d
                acc[0, rows] = acc[0, rows] + d
                acc[1, rows] = acc[1, rows] + d * (xf - prm[s, PMU0, rows])
        ex2[i, 2, s, me] = stack(0.5 * total_row(0), 0.5 * total_row(1))
        rows_start(i, 3, s)

    def last_phase(i, s):
        total = rows_take(i, 3, s)
        inverse, mean, gain0 = row(s, R0), row(s, MU0), row(s, G0)
        s3, s4 = total[0:1], total[1:2] * inverse
        grouped = group_rows(stack(gain0 * s3, gain0 * s4))
        m1, m2 = grouped[0:1] / g.count, grouped[1:2] / g.count
        b = -inverse * inverse * m2
        spread(s, PA1, 0.5 * inverse * gain0)
        spread(s, PB1, b)
        spread(s, PMU1, -inverse * m1 - mean * b)
        here = sb.at[i, place]
        here[0:1, 0:C] = here[0:1, 0:C] + s4
        here[2:3, 0:C] = here[2:3, 0:C] + s3
        out_copy(i, s).wait()
        for qs in quads():
            for rows in chunks():
                pa, pb, pc = prm[s, PA1, rows], prm[s, PB1, rows], prm[s, PMU1, rows]
                for q in qs:
                    xf = xc[s, rows, tile(q)].astype(F32)
                    v = hbuf[s, rows, tile(q)] * pa + xf * pb + pc + gc[s, rows, tile(q)].astype(F32)
                    yc[s, rows, tile(q)] = v.astype(BF16)
        in_grad_copy(i, s).start()


    last_slot = S - 1
    plan = {}

    def at(i, number, slot, action, *args):
        plan.setdefault((i, number, slot), []).append(functools.partial(action, *args))

    for m in range(2):
        at(m, 2, last_slot, tick, m, 1, 0)
        at(m, 3, 0, tick, m, 1, 1)
        at(m, 3, last_slot, tick, m, 0, 0)
        at(m, 4, last_slot, tick, m, 1, 2)
        at(m, 4, last_slot, tick, m, 0, 1)
        at(m + 1, 1, 0, tick, m, 1, 3)
        at(m + 1, 1, last_slot, tick, m, 0, 2)
        at(m + 1, 1, last_slot, small_start, m, 0)
        at(m + 1, 2, last_slot, small_finish, m, 0)
        at(m + 1, 2, last_slot, small_start, m, 1)
        for t in range(4, g.bits + 1):
            at(m + 1, 2, last_slot, tick, m, 1, t)
        at(m + 1, 2, last_slot, tick, m, 0, 3)
        at(m + 1, 3, last_slot, small_finish, m, 1)
        at(m + 1, 3, last_slot, tick, m, 1, g.bits + 1)
        for t in range(4, g.bits + 1):
            at(m + 1, 3, last_slot, tick, m, 0, t)
        for r in range(2, g.bits - 1):
            at(m + 1, 3, last_slot, small_start, m, r)
            if r < g.bits - 2:
                at(m + 1, 3, last_slot, small_finish, m, r)
        at(m + 1, 4, 0, tick, m, 1, g.stages)
        at(m + 1, 5, last_slot, small_finish, m, g.bits - 2)
        at(m + 1, 5, last_slot, tick, m, 0, g.bits + 1)
        end = (m + 2, 1, 0) if m == 0 else (m + 1, 5, last_slot)
        at(*end, tick, m, 0, g.stages)

    def start_x(s):
        return lambda i: halo_start(i, s, 0)

    def start_gy(s):
        return lambda i: halo_start(i, s, 1)

    def start_weights(k, j):
        return lambda i: weights_start(i, k, j)

    sends = {
        (2, 0): [start_x(0)],
        (2, 1): [start_x(1)],
        (3, 0): [start_weights(0, j) for j in range(TRIPLES)],
        (3, S - 1): [start_weights(1, j) for j in range(TRIPLES)],
        (4, 0): [start_gy(0)],
        (4, 1): [start_gy(1)],
    }
    def window(number, i, s):
        for (where, slot), actions in sends.items():
            if where == number:
                @pl.when((i < 2) & (s == slot))
                def _():
                    for action in actions:
                        action(i + 1)

    def slots(number, phase, i):
        def step(s, carry):
            phase(i, s)
            for (turn, where, slot), actions in plan.items():
                if where == number:
                    @pl.when((i == turn) & (s == slot))
                    def _():
                        for action in actions:
                            action()
            return carry

        lax.fori_loop(0, S, step, 0)

    def load_x(i):
        for s in range(S):
            pltpu.make_async_copy(x_h.at[net_of(i), s], rx.at[s], lx.at[s]).start()

    def load_gy(i):
        for s in range(S):
            pltpu.make_async_copy(gy_h.at[net_of(i), s], rg.at[s], lg.at[s]).start()

    load_x(0)
    load_gy(0)
    fill = g.low_rows + g.high_rows
    pk[:, :, :, fill:, :] = jnp.zeros((2, 2, F, g.pack - fill, LANES), F32)
    sb[:, place] = jnp.zeros((3, 16, g.wide), F32)
    for n in range(g.nets):
        own = own_embedding(n)
        for i in range(3):
            if (2 * i) % g.nets == n:
                sb[i, place, 8 : 8 + S, 0 : g.ef] = own.astype(F32)

    @pl.when(me == 0)
    def _():
        hb[:, :, :, 0] = jnp.zeros(hb.shape[:3] + hb.shape[4:], BF16)

    @pl.when(me == F - 1)
    def _():
        hb[:, :, :, 1] = jnp.zeros(hb.shape[:3] + hb.shape[4:], BF16)

    barrier = pltpu.get_barrier_semaphore()
    partners = [(b,) for b in range(g.bits)] + [(1, 2)]
    for df in range(1, F):
        pl.semaphore_signal(barrier, inc=1, device_id={"fsdp": peer(df)}, device_id_type=MESH)
    for bits in partners:
        pl.semaphore_signal(barrier, inc=1, device_id={"dp": other(*bits)}, device_id_type=MESH)
    pl.semaphore_wait(barrier, F - 1 + len(partners))
    weight_local(0).start()
    halo_start(0, 0, 0)
    for j in range(TRIPLES):
        weights_start(0, 0, j)
    for s in range(1, S):
        halo_start(0, s, 0)
    for j in range(TRIPLES):
        weights_start(0, 1, j)
    for s in range(S):
        halo_start(0, s, 1)
    slots(0, sums_phase, 0)
    weights_forward(0, 0)
    weight_local(0).wait()
    weights_take(0, 0)
    weights_ready(0, 0)

    def first_of_all(i, s):
        first_phase(i, s)

        @pl.when((i == 0) & (s == 0))
        def _():
            weights_forward(0, 1)
            weights_take(0, 1)
            weights_ready(0, 1)

    def fourth_and_weights(i, s):
        fourth_phase(i, s)

        @pl.when((i < 2) & (s == 0))
        def _():
            for k in range(2):
                weights_forward(i + 1, k)

    def network(i, carry):
        @pl.when(i < 2)
        def _():
            gacc[...] = jnp.zeros(gacc.shape, F32)

        slots(1, first_of_all, i)
        weights_sent(i)

        @pl.when(i < 2)
        def _():
            load_x(i + 1)
            weight_local(i + 1).start()

        slots(2, second_phase, i)
        slots(3, third_phase, i)

        @pl.when(i < 2)
        def _():
            load_gy(i + 1)

        slots(4, fourth_and_weights, i)

        @pl.when(i < 2)
        def _():
            slots(0, sums_phase, i + 1)
            weight_local(i + 1).wait()
            for k in range(2):
                weights_take(i + 1, k)
                weights_ready(i + 1, k)

        slots(5, last_phase, i)
        return carry

    lax.fori_loop(0, 3, network, 0)


    def drain(i, carry):
        for s in range(S):
            for t in range(2):
                halo_sent(i, s, t)
            for e in range(4):
                for df in range(1, F):
                    row_copy(i, e, s, df, me).wait_send()
        return carry

    lax.fori_loop(0, 3, drain, 0)
    for s in range(S):
        in_grad_copy(2, s).wait()
    for m in range(2):
        for k in range(2):
            pltpu.make_async_copy(pk.at[m, k, me], cg_h.at[m, k], osem.at[m, k]).wait()
    pltpu.make_async_copy(ags, ag_h.at[1], osem.at[1, 2]).wait()


def place_body(g, y_c, dx_c, packed, affine, sums, y, dx, conv, affine_out, gain_out, bias_out):
    for src, dst in ((y_c, y), (dx_c, dx)):
        for q in range(g.np):
            flat = src[0, 0, :, q * LANES : (q + 1) * LANES].T
            dst[0, 0, q] = flat[0 : g.w]
            dst[0, 0, q + g.np] = flat[g.w : 2 * g.w]
    step = pl.program_id(0)

    @pl.when(step < 4)
    def _():
        split = g.low_rows - g.high_rows
        rest = g.c - LANES
        conv[0, 0, :, 0:LANES] = packed[0, 0, 0 : g.low_rows, :]
        conv[0, 0, 0 : g.high_rows, LANES : g.c] = packed[0, 0, g.low_rows : g.low_rows + g.high_rows, 0:rest]
        conv[0, 0, g.high_rows : g.low_rows, LANES : g.c] = packed[
            0, 0, g.low_rows : g.low_rows + split, CHUNK : CHUNK + rest
        ]

    @pl.when(step < 2)
    def _():
        affine_out[...] = affine[...]

    @pl.when(step == 0)
    def _():
        gain_out[...] = sums[:, 0:2, 0 : g.shard]
        bias_out[...] = sums[:, 2:8, 0 : g.shard]


def on_device(
    block_input, embedding, out_cotangent, conv_weights, affine_weight, gains, biases, counts
):
    nets, slots, rows, width, chans = block_input.shape
    fsdp = lax.axis_size("fsdp")
    dp = lax.axis_size("dp")
    embed_rows = affine_weight.shape[1]
    g = settings(dp, fsdp, nets, slots, rows, width, chans, embed_rows)
    weights = conv_weights.reshape(nets, 2, 9, g.shard, chans)

    tiles = (g.np + 1) * LANES
    dma = pltpu.SemaphoreType.DMA
    scratch = [
        pltpu.VMEM((slots, rows, width, chans), BF16),
        pltpu.VMEM((slots, rows, width, chans), BF16),
        pltpu.VMEM((slots, rows, width, chans), BF16),
        pltpu.VMEM((slots, chans, g.px), BF16),
        pltpu.VMEM((slots, chans, g.px), BF16),
        pltpu.VMEM((slots, 3, chans, (g.np + 5) * LANES), BF16),
        pltpu.VMEM((slots, 3, chans, (g.np + 2) * LANES), BF16),
        pltpu.VMEM((slots, 3, chans, (g.np + 5) * LANES), BF16),
        pltpu.VMEM((2, slots, 2, 2, 2, width, chans), BF16),
        pltpu.VMEM((slots, chans, tiles), F32),
        pltpu.VMEM((slots, chans, tiles), F32),
        pltpu.VMEM((2, fsdp, 2, 9, g.shard, chans), BF16),
        pltpu.VMEM((2, chans, 9 * chans), BF16),
        pltpu.VMEM((2, chans, 9 * chans), BF16),
        pltpu.VMEM((2, 9 * chans, chans), F32),
        pltpu.VMEM((2, 2, fsdp, g.pack, LANES), F32),
        pltpu.VMEM((3 - g.split, 2, fsdp, g.half, LANES), F32),
        pltpu.VMEM((2, 3, fsdp, g.piece, LANES), F32),
        pltpu.VMEM((2, 2, fsdp - 1, g.piece, LANES), F32),
        pltpu.VMEM((2, g.bits - 3, g.piece, LANES), F32),
        pltpu.VMEM((chans, g.px), F32),
        pltpu.VMEM((slots, chans, g.px), BF16),
        pltpu.VMEM((embed_rows, 2 * chans), F32),
        pltpu.VMEM((3, slots, fsdp, 16, chans), F32),
        pltpu.VMEM((3, 3, slots, fsdp, 8, chans), F32),
        pltpu.VMEM((3, dp, 16, g.wide), F32),
        pltpu.VMEM((3, chans, LANES), F32),
        pltpu.VMEM((slots, 16, chans), F32),
        pltpu.VMEM((slots, 10, chans, LANES), F32),
        dma((slots,)),
        dma((slots,)),
        dma((slots,)),
        dma((3, slots, 2, 2)),
        dma((3, slots, 2, 2)),
        dma((3, 4, slots, fsdp)),
        dma((3, 4, slots, fsdp)),
        dma((3,)),
        dma((3, 2, 3, fsdp)),
        dma((3, 2, 3, fsdp)),
        dma((3, 2, fsdp)),
        dma((3, 2, fsdp)),
        dma((2, 2, g.stages, max(3, fsdp - 1))),
        dma((2, 2, g.stages, max(3, fsdp - 1))),
        dma((2, g.bits + 2)),
        dma((2, g.bits + 2)),
        dma((2, 3)),
    ]
    hbm = pl.BlockSpec(memory_space=pl.ANY)
    vmem = pl.BlockSpec(memory_space=pltpu.VMEM)
    smem = pl.BlockSpec(memory_space=pltpu.SMEM)
    channel_major = jax.ShapeDtypeStruct((nets, slots, chans, g.px), BF16)
    main = pl.pallas_call(
        functools.partial(kernel_body, g),
        out_shape=(
            channel_major,
            channel_major,
            jax.ShapeDtypeStruct((2, 2, g.pack, LANES), F32),
            jax.ShapeDtypeStruct((2, embed_rows, 2 * chans), F32),
            jax.ShapeDtypeStruct((2, 8, 2 * LANES), F32),
        ),
        in_specs=[hbm, hbm, hbm, vmem, vmem, vmem, vmem, smem],
        out_specs=(hbm, hbm, hbm, hbm, vmem),
        scratch_shapes=scratch,
        compiler_params=pltpu.CompilerParams(
            collective_id=0, has_side_effects=True, vmem_limit_bytes=64 << 20
        ),
    )(block_input, out_cotangent, weights, affine_weight, embedding, gains, biases, counts)

    def by_slot(step):
        return (step // slots, step % slots, 0, 0)

    def by_conv(step):
        return (jnp.minimum(step, 3) // 2, jnp.minimum(step, 3) % 2, 0, 0)

    def by_net(step):
        return (jnp.minimum(step, 1), 0, 0)

    image = pl.BlockSpec((1, 1, rows, width, chans), lambda step: by_slot(step) + (0,))
    block_output, input_grad, conv_grads, affine_grad, gain_grads, bias_grads = pl.pallas_call(
        functools.partial(place_body, g),
        grid=(nets * slots,),
        out_shape=(
            jax.ShapeDtypeStruct(block_input.shape, BF16),
            jax.ShapeDtypeStruct(block_input.shape, BF16),
            jax.ShapeDtypeStruct((2, 2, g.low_rows, chans), F32),
            jax.ShapeDtypeStruct((2, embed_rows, 2 * chans), F32),
            jax.ShapeDtypeStruct((2, 2, g.shard), F32),
            jax.ShapeDtypeStruct((2, 6, g.shard), F32),
        ),
        in_specs=[
            pl.BlockSpec((1, 1, chans, g.px), by_slot),
            pl.BlockSpec((1, 1, chans, g.px), by_slot),
            pl.BlockSpec((1, 1, g.pack, LANES), by_conv),
            pl.BlockSpec((1, embed_rows, 2 * chans), by_net),
            vmem,
        ],
        out_specs=(
            image,
            image,
            pl.BlockSpec((1, 1, g.low_rows, chans), by_conv),
            pl.BlockSpec((1, embed_rows, 2 * chans), by_net),
            vmem,
            vmem,
        ),
        compiler_params=pltpu.CompilerParams(vmem_limit_bytes=48 << 20),
    )(*main)
    conv_grads = conv_grads.reshape(2, 2, 3, 3, g.shard, chans)
    return block_output, input_grad, conv_grads, affine_grad, gain_grads, bias_grads


def solution(mesh):
    placed = (
        P(None, "dp", "fsdp", None, None),
        P(None, "dp", None),
        P(None, "dp", "fsdp", None, None),
        P(None, None, None, None, "fsdp", None),
        P(None, "fsdp", None),
        P(None, None, "fsdp"),
        P(None, None, "fsdp"),
        P("dp"),
    )
    return jax.shard_map(
        on_device,
        mesh=mesh,
        in_specs=placed,
        out_specs=(
            P(None, "dp", "fsdp", None, None),
            P(None, "dp", "fsdp", None, None),
            P(None, None, None, None, "fsdp", None),
            P(None, "fsdp", None),
            P(None, None, "fsdp"),
            P(None, None, "fsdp"),
        ),
        check_vma=False,
    )
```

```python
import functools
import types

import jax
import jax.numpy as jnp
from jax import lax
from jax.experimental import pallas as pl
from jax.experimental.pallas import tpu as pltpu
from jax.sharding import PartitionSpec as P

GROUPS = 32
EPSILON = 1e-05
LANES = 128
CHUNK = 64
MESH = pl.DeviceIdType.MESH
F32 = jnp.float32
BF16 = jnp.bfloat16

MU0, R0, G0, G1, B1, B2, B3, SC1, SH, SGY, MU1, R1, SUMH = range(13)
PA0, PB0, PMU0, PBIAS, PA1, PB1, PMU1, PDA, PDB, PDC = range(10)


def settings(dp_size, fsdp_size, nets, slots, rows, width, chans, embed_rows):
    g = types.SimpleNamespace()
    g.dp, g.f, g.nets, g.s, g.r, g.w, g.c, g.ef = (
        dp_size, fsdp_size, nets, slots, rows, width, chans, embed_rows,
    )
    g.np = rows // 2
    g.px = g.np * LANES
    g.count = float(rows * fsdp_size * width * (chans // GROUPS))
    g.pixels = float(rows * fsdp_size * width)
    g.bits = dp_size.bit_length() - 1
    g.shard = chans // fsdp_size
    g.low_rows = 9 * g.shard
    g.high_rows = -(-g.low_rows // 16) * 8
    g.pack = -(-(g.low_rows + g.high_rows) // 64) * 64
    g.half = g.pack // 2
    g.piece = g.pack // 8
    g.wide = max(2 * chans, embed_rows)
    g.stages = g.bits + 2
    g.split = 2 if g.shard % 32 == 0 else 1
    g.rows = g.shard // g.split
    return g


def kernel_body(
    g,
    x_h, gy_h, w_h, aff, emb, gains, biases, counts,
    y_h, dx_h, cg_h, ag_h, sg,
    rx, rg, dhp, xc, gc, xa0, xa1, xg, hb, hbuf, dub, wraw, wf, wb, gacc, pk, r0b, r1b, ryb, rbb,
    ybuf, yc, ags, ex1, ex2, sb, acc, rowt, prm,
    lx, lg, ysem, hs, hr, es, er, wl, wys, wyr, wcs, wcr, cs, cr, ss, sr, osem,
):
    me = lax.axis_index("fsdp")
    dp = lax.axis_index("dp")
    C, NP, F, S, R = g.c, g.np, g.f, g.s, g.r
    PX = g.px

    def net_of(i):
        return (2 * i) % g.nets

    def peer(df):
        return (me + df) % F

    def source(df):
        return (me + F - df) % F

    def bit(b):
        return (dp // (1 << b)) % 2

    def other(*bits):
        where = dp
        for b in bits:
            where = where + (1 << b) * (1 - 2 * bit(b))
        return where

    def remote(src, dst, send, recv, where):
        return pltpu.make_async_remote_copy(
            src_ref=src, dst_ref=dst, send_sem=send, recv_sem=recv,
            device_id=where, device_id_type=MESH,
        )

    def tile(t):
        if isinstance(t, int):
            return pl.ds(t * LANES, LANES)
        return pl.ds(pl.multiple_of(t * LANES, LANES), LANES)

    def kept(s):
        return jnp.where(s < counts[0], 1.0, 0.0)

    lane = lax.broadcasted_iota(jnp.int32, (C, LANES), 1)
    low_lanes = lane < g.w
    top = (me > 0).astype(jnp.int32)
    bottom = (me < F - 1).astype(jnp.int32)
    edge_ok = jnp.where(low_lanes, top, bottom) > 0


    def halo_copy(i, s, t, down):
        src = (x_h, gy_h)[t]
        n = net_of(i)
        if down:
            return remote(
                src.at[n, s, pl.ds(R - 2, 2)], hb.at[i % 2, s, t, 0],
                hs.at[i, s, t, 1], hr.at[i, s, t, 1], {"fsdp": (me + 1) % F},
            )
        return remote(
            src.at[n, s, pl.ds(0, 2)], hb.at[i % 2, s, t, 1],
            hs.at[i, s, t, 0], hr.at[i, s, t, 0], {"fsdp": (me + F - 1) % F},
        )

    def halo_start(i, s, t):
        @pl.when(me > 0)
        def _():
            halo_copy(i, s, t, False).start()

        @pl.when(me < F - 1)
        def _():
            halo_copy(i, s, t, True).start()

    def halo_take(i, s, t):
        @pl.when(me > 0)
        def _():
            halo_copy(i, s, t, True).wait_recv()

        @pl.when(me < F - 1)
        def _():
            halo_copy(i, s, t, False).wait_recv()

    def halo_sent(i, s, t):
        @pl.when(me > 0)
        def _():
            halo_copy(i, s, t, False).wait_send()

        @pl.when(me < F - 1)
        def _():
            halo_copy(i, s, t, True).wait_send()

    def row_copy(i, e, s, df, who):
        ref = ex1.at[i, s, who] if e == 0 else ex2.at[i, e - 1, s, who]
        return remote(ref, ref, es.at[i, e, s, df], er.at[i, e, s, df], {"fsdp": peer(df)})

    def rows_start(i, e, s):
        for df in range(1, F):
            row_copy(i, e, s, df, me).start()

    def rows_take(i, e, s):
        for df in range(1, F):
            row_copy(i, e, s, df, source(df)).wait_recv()
        parts = [ex1[i, s, f] if e == 0 else ex2[i, e - 1, s, f] for f in range(F)]
        total = parts[0]
        for part in parts[1:]:
            total = total + part
        return total

    mine = dp % 2

    TRIPLES = 3

    def weight_rows(half):
        return pl.ds(pl.multiple_of(half * g.rows, g.rows), g.rows)

    def weight_copy(i, k, j, df, who):
        taps, rows = pl.ds(3 * j, 3), weight_rows(mine if g.split == 2 else 0)
        return remote(
            w_h.at[net_of(i), k, taps, rows], wraw.at[i % 2, who, k, taps, rows],
            wys.at[i, k, j, df], wyr.at[i, k, j, df], {"fsdp": peer(df)},
        )

    def weight_share(i, k, df, half):
        ref = wraw.at[i % 2, source(df), k, :, weight_rows(half)]
        return remote(ref, ref, wcs.at[i, k, df], wcr.at[i, k, df], {"dp": other(0)})

    def weight_local(i):
        return pltpu.make_async_copy(w_h.at[net_of(i)], wraw.at[i % 2, me], wl.at[i])

    def weights_start(i, k, j):
        for df in range(1, F):
            weight_copy(i, k, j, df, me).start()

    def weights_forward(i, k):
        for df in range(1, F):
            for j in range(TRIPLES):
                weight_copy(i, k, j, df, source(df)).wait_recv()
            if g.split == 2:
                weight_share(i, k, df, mine).start()

    def weights_take(i, k):
        if g.split == 2:
            for df in range(1, F):
                weight_share(i, k, df, 1 - mine).wait_recv()

    def weights_sent(i):
        for k in range(2):
            for df in range(1, F):
                for j in range(TRIPLES):
                    weight_copy(i, k, j, df, me).wait_send()
                if g.split == 2:
                    weight_share(i, k, df, mine).wait_send()


    def rows_at(offset, size):
        if not isinstance(offset, int):
            offset = pl.multiple_of(offset, 8)
        return pl.ds(offset, size)

    half_start = bit(0) * g.half
    PAIR = ((1,), (2,), (1, 2))

    def piece_start(bits):
        b1 = 1 - bit(1) if 1 in bits else bit(1)
        b2 = 1 - bit(2) if 2 in bits else bit(2)
        return half_start + (2 * b1 + b2) * g.piece

    def core_sums(m, k):
        return r0b.at[0 if g.split == 2 else m, k]

    def stage_copies(m, k, t):
        def sems(j):
            return cs.at[m, k, t, j], cr.at[m, k, t, j]

        mine_at = rows_at(piece_start(()), g.piece)
        own = pk.at[m, k, me, mine_at]
        if t == 0:
            there = rows_at((1 - bit(0)) * g.half, g.half)
            return [(remote(pk.at[m, k, :, there], core_sums(m, k), *sems(0), {"dp": other(0)}), None)]
        if t == 1:
            return [
                (
                    remote(
                        pk.at[m, k, :, rows_at(piece_start(bits), g.piece)], r1b.at[k, j],
                        *sems(j), {"dp": other(*bits)},
                    ),
                    None,
                )
                for j, bits in enumerate(PAIR)
            ]
        if t == 2:
            return [
                (remote(pk.at[m, k, peer(df), mine_at], ryb.at[m, k, df - 1], *sems(df - 1), {"fsdp": peer(df)}), None)
                for df in range(1, F)
            ]
        if t < g.bits:
            return [(remote(own, rbb.at[k, t - 3], *sems(0), {"dp": other(t)}), None)]
        if t == g.bits:
            return [
                (
                    remote(own, own, *sems(j), {"dp": other(*bits)}),
                    remote(own, pk.at[m, k, me, rows_at(piece_start(bits), g.piece)], *sems(j), {"dp": other(*bits)}),
                )
                for j, bits in enumerate(PAIR)
            ]
        own = pk.at[m, k, me, rows_at(half_start, g.half)]
        there = pk.at[m, k, me, rows_at((1 - bit(0)) * g.half, g.half)]
        return [(
            remote(own, own, *sems(0), {"dp": other(0)}), remote(own, there, *sems(0), {"dp": other(0)}),
        )]

    def add_rows(dst, start, sources, size):
        step = max(n for n in range(8, 65, 8) if size % n == 0)

        def body(j, carry):
            at = rows_at(start + j * step, step)
            total = dst[at, :]
            for src in sources:
                total = total + src[rows_at(j * step, step), :]
            dst[at, :] = total
            return carry

        lax.fori_loop(0, size // step, body, 0)

    def stage_start(m, k, t):
        for copy, _ in stage_copies(m, k, t):
            copy.start()

    def stage_finish(m, k, t):
        for copy, received in stage_copies(m, k, t):
            copy.wait_send()
            (received or copy).wait_recv()
        if t == 0:
            for f in range(F):
                add_rows(pk.at[m, k, f], half_start, [core_sums(m, k).at[f]], g.half)
        elif t == 1:
            for f in range(F):
                add_rows(pk.at[m, k, f], piece_start(()), [r1b.at[k, j, f] for j in range(3)], g.piece)
        elif t == 2:
            add_rows(pk.at[m, k, me], piece_start(()), [ryb.at[m, k, df - 1] for df in range(1, F)], g.piece)
        elif t < g.bits:
            add_rows(pk.at[m, k, me], piece_start(()), [rbb.at[k, t - 3]], g.piece)

    place = bit(1) + 2 * bit(2) + 4 * bit(0) + (dp // 8) * 8

    def small_copies(m, r, received):
        targets = PAIR if r == 0 else ((0,),) if r == 1 else ((r + 1,),)
        size = 1 if r == 0 else 1 << (r + 1)
        flips = {1: 1, 2: 2, 0: 4}
        copies = []
        for j, bits in enumerate(targets):
            there = place
            for b in bits:
                there = there + flips.get(b, 1 << b) * (1 - 2 * bit(b))
            own = sb.at[m, pl.ds((place // size) * size, size)]
            dst = sb.at[m, pl.ds((there // size) * size, size)] if received else own
            sem = j if r == 0 else r + 2
            copies.append(remote(own, dst, ss.at[m, sem], sr.at[m, sem], {"dp": other(*bits)}))
        return copies

    def small_start(m, r):
        for copy in small_copies(m, r, False):
            copy.start()

    def small_finish(m, r):
        for copy in small_copies(m, r, False):
            copy.wait_send()
        for copy in small_copies(m, r, True):
            copy.wait_recv()
        if r == g.bits - 2:
            finish_small(m)

    def tick(m, k, t):
        if t == 0:
            pack_rows(m, k)
        else:
            stage_finish(m, k, t - 1)
        if t < g.stages:
            stage_start(m, k, t)
        else:
            pltpu.make_async_copy(pk.at[m, k, me], cg_h.at[m, k], osem.at[m, k]).start()

    def finish_small(m):
        total = sb[m, 0, 0:8, 0 : 2 * LANES]
        for d in range(1, g.dp):
            total = total + sb[m, d, 0:8, 0 : 2 * LANES]
        sg[m] = pltpu.roll(total, 2 * LANES - me * g.shard, 1)
        block = sb[m, :, 8:16, :].reshape(g.dp * 8, g.wide)
        index = lax.broadcasted_iota(jnp.int32, (g.dp * 8, g.ef), 0) & 7
        left = jnp.where(index < S, block[:, : g.ef], 0.0).astype(BF16)
        right = pltpu.roll(block[:, : 2 * C], g.dp * 8 - S, 0).astype(BF16)
        if m > 0:
            pltpu.make_async_copy(ags, ag_h.at[m - 1], osem.at[m - 1, 2]).wait()
        ags[...] = lax.dot_general(left, right, (((0,), (0,)), ((), ())), preferred_element_type=F32)
        pltpu.make_async_copy(ags, ag_h.at[m], osem.at[m, 2]).start()

    def pack_rows(m, k):
        for f in range(F):
            for tap in range(9):
                first, last = tap * g.shard, (tap + 1) * g.shard
                c0 = tap * C + f * g.shard
                pk[m, k, f, first:last, :] = gacc[k, c0 : c0 + g.shard, 0:LANES]
                for lo, hi, lanes in ((0, g.high_rows, 0), (g.high_rows, g.low_rows, CHUNK)):
                    a, b = max(first, lo), min(last, hi)
                    if a < b:
                        at = g.low_rows + a - lo
                        pk[m, k, f, at : at + b - a, lanes : lanes + C - LANES] = gacc[
                            k, c0 + a - first : c0 + b - first, LANES:C
                        ]


    def shifted(v):
        col = lax.broadcasted_iota(jnp.int32, v.shape, 1) & (g.w - 1)
        left = jnp.where(col == 0, 0.0, pltpu.roll(v, 1, 1))
        right = jnp.where(col == g.w - 1, 0.0, pltpu.roll(v, LANES - 1, 1))
        return left, v, right

    def put(buf, s, rows, t, v):
        for j, moved in enumerate(shifted(v)):
            buf[s, j, rows, tile(t)] = moved.astype(BF16)

    def put_edges(buf, s, first_edge, second_edge):
        near = shifted(first_edge)
        far = None if second_edge is None else shifted(second_edge)
        for j in range(3):
            first = buf[s, j, :, tile(1)].astype(F32)
            last = buf[s, j, :, tile(NP)].astype(F32)
            buf[s, j, :, tile(0)] = jnp.where(low_lanes, near[j], pltpu.roll(last, g.w, 1)).astype(BF16)
            buf[s, j, :, tile(NP + 1)] = jnp.where(low_lanes, pltpu.roll(first, g.w, 1), near[j]).astype(BF16)
            if far is not None:
                buf[s, j, :, tile(NP + 2)] = jnp.where(low_lanes, far[j], last).astype(BF16)
                buf[s, j, :, tile(NP + 3)] = near[j].astype(BF16)
                buf[s, j, :, tile(NP + 4)] = jnp.where(low_lanes, first, far[j]).astype(BF16)

    def windows(buf, s, back, edge):
        pieces = []
        for i in range(3):
            for j in range(3):
                ti, tj = (2 - i, 2 - j) if back else (i, j)
                piece = buf[s, tj, :, ti * LANES : ti * LANES + PX]
                if edge:
                    piece = jnp.concatenate([piece, buf[s, tj, :, tile(NP + 2 + ti)]], axis=1)
                pieces.append(piece)
        return jnp.concatenate(pieces, axis=0)

    def chunks():
        return [pl.ds(c0, CHUNK) for c0 in range(0, C, CHUNK)]

    def quads():
        order = [NP - 1] + list(range(NP - 1))
        return [order[q : q + 4] for q in range(0, NP, 4)]

    def clear(count):
        for k in range(count):
            acc[k] = jnp.zeros((C, LANES), F32)

    def total_row(k):
        return jnp.sum(acc[k].T, axis=0, keepdims=True)

    def group_rows(rows):
        high = rows.astype(BF16)
        rest = rows - high.astype(F32)
        middle = rest.astype(BF16)
        low = (rest - middle.astype(F32)).astype(BF16)
        a = lax.broadcasted_iota(jnp.int32, (C, C), 0) // (C // GROUPS)
        b = lax.broadcasted_iota(jnp.int32, (C, C), 1) // (C // GROUPS)
        same = jnp.where(a == b, 1.0, 0.0).astype(BF16)
        three = jnp.dot(jnp.concatenate([high, middle, low], axis=0).astype(BF16), same, preferred_element_type=F32)
        n = rows.shape[0]
        return three[0:n] + three[n : 2 * n] + three[2 * n : 3 * n]

    def stack(*rows):
        fill = 8 - len(rows)
        return jnp.concatenate(list(rows) + [jnp.zeros((fill, C), F32)] * (fill > 0), axis=0)

    def spread(s, k, row):
        prm[s, k] = jnp.broadcast_to(row, (LANES, C)).T

    def save(s, k, row):
        rowt[s, k : k + 1, :] = row

    def row(s, k):
        return rowt[s, k : k + 1, :]

    def moments(total):
        grouped = group_rows(total)
        mean = grouped[0:1] / g.count
        variance = grouped[1:2] / g.count - mean * mean
        return mean, lax.rsqrt(variance + EPSILON)

    def slope_twice(w, t):
        return (1.0 + t) * (1.0 + w * (1.0 - t))

    def pair(buf, s, q):
        return jnp.concatenate([buf[s, q], buf[s, q + NP]], axis=0)

    def pixels(buf, s):
        return jnp.concatenate([buf[s, h] for q in range(NP) for h in (q, q + NP)], axis=0)

    def own_embedding(n):
        whole = emb[n].astype(F32)
        return pltpu.roll(whole, whole.shape[1] - me * g.ef, 1)[:, 0 : g.ef]

    def weight_sums(k, acts, grads, s, factor):
        right = pixels(grads, s)
        for i in range(3):
            left = jnp.concatenate(
                [acts[s, j, :, i * LANES : i * LANES + PX] for j in range(3)], axis=0
            )
            rows = pl.ds(3 * C * i, 3 * C)
            o = jnp.dot(left, right, preferred_element_type=F32)
            gacc[k, rows] = gacc[k, rows] + (o if factor is None else o * factor)


    def input_work(i, s):
        n = net_of(i)
        clear(2)
        for qs in quads():
            for q in qs:
                xc[i % 2, s, :, tile(q)] = pair(rx, s, q).T
            for rows in chunks():
                a0, a1 = acc[0, rows], acc[1, rows]
                for q in qs:
                    xf = xc[i % 2, s, rows, tile(q)].astype(F32)
                    a0 = a0 + xf
                    a1 = a1 + xf * xf
                acc[0, rows], acc[1, rows] = a0, a1
        mod = jnp.dot(own_embedding(n).astype(BF16), aff[n], preferred_element_type=F32)
        which = lax.broadcasted_iota(jnp.int32, mod.shape, 0) == s
        mod = jnp.sum(jnp.where(which, mod, 0.0), axis=0, keepdims=True)
        ex1[i, s, me, 0:8] = stack(total_row(0), total_row(1), mod[:, 0:C], mod[:, C : 2 * C])
        vectors = jnp.concatenate([gains[n], biases[n]], axis=0).astype(F32)
        vectors = jnp.concatenate([vectors, jnp.zeros((8, 2 * LANES - g.shard), F32)], axis=1)
        ex1[i, s, me, 8:16] = pltpu.roll(vectors, me * g.shard, 1)[:, 0:C]
        rows_start(i, 0, s)

    def input_loaded(i, s):
        pltpu.make_async_copy(x_h.at[net_of(i), s], rx.at[s], lx.at[s]).wait()

    def weights_ready(i, k):
        for tap in range(9):
            blocks = [wraw[i % 2, f, k, tap] for f in range(F)]
            if g.shard % 16:
                blocks = [b.astype(F32) for b in blocks]
            whole = jnp.concatenate(blocks, axis=0).astype(BF16)
            wb[k, :, tap * C : (tap + 1) * C] = whole
            wf[k, :, tap * C : (tap + 1) * C] = whole.T

    def edge_tiles(i, s, t):
        near = jnp.concatenate([hb[i % 2, s, t, 0, 1], hb[i % 2, s, t, 1, 0]], axis=0).T.astype(F32)
        far = jnp.concatenate([hb[i % 2, s, t, 0, 0], hb[i % 2, s, t, 1, 1]], axis=0).T.astype(F32)
        return near, far

    def gradient_loaded(i, s):
        pltpu.make_async_copy(gy_h.at[net_of(i), s], rg.at[s], lg.at[s]).wait()

    def prepare(i, s):
        total = rows_take(i, 0, s)
        mean, inverse = moments(total[0:8])
        save(s, MU0, mean)
        save(s, R0, inverse)
        gain0, gain1 = total[8:9], total[9:10]
        save(s, G0, gain0)
        save(s, G1, gain1)
        save(s, B2, total[12:13])
        save(s, B3, total[13:14])
        save(s, SC1, total[2:3] + total[14:15] + 1.0)
        save(s, SH, total[3:4] + total[15:16])
        scale = inverse * gain0
        spread(s, PA0, 0.5 * scale)
        spread(s, PB0, 0.5 * (total[10:11] - mean * scale))
        spread(s, PMU0, mean)
        spread(s, PBIAS, total[11:12])

        def act(xf, a, b):
            w = xf * a + b
            return w * jnp.tanh(w) + w

        for n, qs in enumerate(quads()):
            for rows in chunks():
                a, b = prm[s, PA0, rows], prm[s, PB0, rows]
                for q in qs:
                    put(xa0, s, rows, q + 1, act(xc[i % 2, s, rows, tile(q)].astype(F32), a, b))
            if n == 0:
                near, far = edge_tiles(i, s, 0)
                near = jnp.where(edge_ok, act(near, prm[s, PA0], prm[s, PB0]), 0.0)
                far = jnp.where(edge_ok, act(far, prm[s, PA0], prm[s, PB0]), 0.0)
                put_edges(xa0, s, near, far)

    def prepare_gradient(i, s):
        kf = kept(s)
        acc[2] = jnp.zeros((C, LANES), F32)
        for qs in quads():
            for q in qs:
                gc[s, :, tile(q)] = (pair(rg, s, q).T.astype(F32) * kf).astype(BF16)
            for rows in chunks():
                a2 = acc[2, rows]
                for q in qs:
                    gf = gc[s, rows, tile(q)].astype(F32)
                    a2 = a2 + gf
                    put(xg, s, rows, q + 1, gf)
                acc[2, rows] = a2
        save(s, SGY, total_row(2))

    def first_phase(i, s):
        kf = kept(s)

        def gradient_edges():
            near, far = edge_tiles(i, s, 1)
            put_edges(xg, s, jnp.where(edge_ok, near, 0.0) * kf, jnp.where(edge_ok, far, 0.0) * kf)

        def work(with_prepare):
            if with_prepare:
                gradient_loaded(i, s)
                halo_take(i, s, 0)
                halo_take(i, s, 1)
                prepare(i, s)
            clear(2)
            hbuf[s] = jnp.dot(wf[0], windows(xa0, s, False, True), preferred_element_type=F32)
            for q in range(NP + 1):
                for rows in chunks():
                    h = hbuf[s, rows, tile(q)] + prm[s, PBIAS, rows]
                    hbuf[s, rows, tile(q)] = h
                    if q < NP:
                        acc[0, rows] = acc[0, rows] + h
                        acc[1, rows] = acc[1, rows] + h * h
            if with_prepare:
                prepare_gradient(i, s)
                gradient_edges()

        pl.when(i == 0)(functools.partial(work, False))
        pl.when(i > 0)(functools.partial(work, True))
        ex2[i, 0, s, me] = stack(total_row(0), total_row(1), row(s, SGY))
        rows_start(i, 1, s)

        @pl.when(i == 0)
        def _():
            halo_take(i, s, 1)
            gradient_edges()

    def second_phase(i, s):
        total = rows_take(i, 1, s)
        window(2, i, s)
        mean, inverse = moments(total)
        save(s, MU1, mean)
        save(s, R1, inverse)
        save(s, SUMH, total[0:1])
        save(s, SGY, total[2:3])
        scale = inverse * row(s, G1)
        spread(s, PA1, 0.5 * scale * row(s, SC1))
        spread(s, PB1, 0.5 * (row(s, SH) + (row(s, B2) - mean * scale) * row(s, SC1)))
        spread(s, PMU1, mean)
        clear(2)
        dub[s] = jnp.dot(wb[1], windows(xg, s, True, True), preferred_element_type=F32)
        for q in range(NP + 1):
            for rows in chunks():
                a, b, mu = prm[s, PA1, rows], prm[s, PB1, rows], prm[s, PMU1, rows]
                h = hbuf[s, rows, tile(q)]
                w = h * a + b
                t = jnp.tanh(w)
                d = dub[s, rows, tile(q)] * slope_twice(w, t)
                dub[s, rows, tile(q)] = d
                if q < NP:
                    put(xa1, s, rows, q + 1, w * t + w)
                    acc[0, rows] = acc[0, rows] + d
                    acc[1, rows] = acc[1, rows] + d * (h - mu)
        w = hbuf[s, :, tile(NP)] * prm[s, PA1] + prm[s, PB1]
        put_edges(xa1, s, jnp.where(edge_ok, w * jnp.tanh(w) + w, 0.0), None)
        ex2[i, 1, s, me] = stack(0.5 * total_row(0), 0.5 * total_row(1))
        rows_start(i, 2, s)

        @pl.when(i < 2)
        def _():
            weight_sums(1, xa1, rg, s, kept(s))

    def out_copy(i, s):
        return pltpu.make_async_copy(yc.at[s], y_h.at[net_of(i), s], ysem.at[s])

    def in_grad_copy(i, s):
        return pltpu.make_async_copy(yc.at[s], dx_h.at[net_of(i), s], ysem.at[s])

    def third_phase(i, s):
        kf = kept(s)
        total = rows_take(i, 2, s)
        window(3, i, s)
        spread(s, PBIAS, row(s, B3))
        s1, s2 = total[0:1], total[1:2] * row(s, R1)
        sc1, gain1, inverse, mean = row(s, SC1), row(s, G1), row(s, R1), row(s, MU1)
        grouped = group_rows(stack(gain1 * sc1 * s1, gain1 * sc1 * s2))
        m1, m2 = grouped[0:1] / g.count, grouped[1:2] / g.count
        a = inverse * sc1 * gain1
        b = -inverse * inverse * m2
        c = -inverse * m1 - mean * b
        spread(s, PDA, 0.5 * a)
        spread(s, PDB, b)
        spread(s, PDC, c)
        dscale = gain1 * s2 + row(s, B2) * s1
        here = sb.at[i, place]
        here[1:2, 0:C] = here[1:2, 0:C] + sc1 * s2
        here[3:4, 0:C] = here[3:4, 0:C] + a * s1 + b * row(s, SUMH) + c * g.pixels
        here[4:5, 0:C] = here[4:5, 0:C] + sc1 * s1
        here[5:6, 0:C] = here[5:6, 0:C] + row(s, SGY)
        here[6:7, 0:C] = here[6:7, 0:C] + dscale
        here[7:8, 0:C] = here[7:8, 0:C] + s1
        modulation = jnp.concatenate([dscale, s1], axis=1).astype(BF16).astype(F32)
        for slot in range(S):
            at = 8 + S + slot
            here[at : at + 1, 0 : 2 * C] = jnp.where(s == slot, modulation, here[at : at + 1, 0 : 2 * C])

        def output():
            for q in range(NP):
                for rows in chunks():
                    v = ybuf[rows, tile(q)] + prm[s, PBIAS, rows]
                    v = (v + xc[i % 2, s, rows, tile(q)].astype(F32)) * kf
                    yc[s, rows, tile(q)] = v.astype(BF16)

        def hidden_grad(with_weights):
            ybuf[...] = jnp.dot(wf[1], windows(xa1, s, False, False), preferred_element_type=F32)
            for n, qs in enumerate(quads()):
                for rows in chunks():
                    pa, pb, pc = prm[s, PDA, rows], prm[s, PDB, rows], prm[s, PDC, rows]
                    for q in qs:
                        d = dub[s, rows, tile(q)] * pa + hbuf[s, rows, tile(q)] * pb + pc
                        put(xg, s, rows, q + 1, d)
                if with_weights:
                    for q in qs:
                        flat = xg[s, 1, :, tile(q + 1)].T
                        dhp[s, q] = flat[0 : g.w]
                        dhp[s, q + NP] = flat[g.w : 2 * g.w]
                if n == 0:
                    d = dub[s, :, tile(NP)] * prm[s, PDA] + hbuf[s, :, tile(NP)] * prm[s, PDB] + prm[s, PDC]
                    put_edges(xg, s, jnp.where(edge_ok, d, 0.0), None)

        @pl.when(i > 0)
        def _():
            in_grad_copy(i, s).wait()

        @pl.when(i < 2)
        def _():
            hidden_grad(True)
            input_loaded(i + 1, s)
            weight_sums(0, xa0, dhp, s, None)
            output()
            input_work(i + 1, s)

        @pl.when(i == 2)
        def _():
            hidden_grad(False)
            output()

        out_copy(i, s).start()

    def fourth_phase(i, s):
        clear(2)
        hbuf[s, :, 0:PX] = jnp.dot(wb[0], windows(xg, s, True, False), preferred_element_type=F32)
        for q in range(NP):
            for rows in chunks():
                xf = xc[i % 2, s, rows, tile(q)].astype(F32)
                w = xf * prm[s, PA0, rows] + prm[s, PB0, rows]
                d = hbuf[s, rows, tile(q)] * slope_twice(w, jnp.tanh(w))
                hbuf[s, rows, tile(q)] = d
                acc[0, rows] = acc[0, rows] + d
                acc[1, rows] = acc[1, rows] + d * (xf - prm[s, PMU0, rows])
        ex2[i, 2, s, me] = stack(0.5 * total_row(0), 0.5 * total_row(1))
        rows_start(i, 3, s)

    def last_phase(i, s):
        total = rows_take(i, 3, s)
        inverse, mean, gain0 = row(s, R0), row(s, MU0), row(s, G0)
        s3, s4 = total[0:1], total[1:2] * inverse
        grouped = group_rows(stack(gain0 * s3, gain0 * s4))
        m1, m2 = grouped[0:1] / g.count, grouped[1:2] / g.count
        b = -inverse * inverse * m2
        spread(s, PA1, 0.5 * inverse * gain0)
        spread(s, PB1, b)
        spread(s, PMU1, -inverse * m1 - mean * b)
        here = sb.at[i, place]
        here[0:1, 0:C] = here[0:1, 0:C] + s4
        here[2:3, 0:C] = here[2:3, 0:C] + s3
        out_copy(i, s).wait()
        for qs in quads():
            for rows in chunks():
                pa, pb, pc = prm[s, PA1, rows], prm[s, PB1, rows], prm[s, PMU1, rows]
                for q in qs:
                    xf = xc[i % 2, s, rows, tile(q)].astype(F32)
                    v = hbuf[s, rows, tile(q)] * pa + xf * pb + pc + gc[s, rows, tile(q)].astype(F32)
                    yc[s, rows, tile(q)] = v.astype(BF16)
        in_grad_copy(i, s).start()


    last_slot = S - 1
    plan = {}

    def at(i, number, slot, action, *args):
        plan.setdefault((i, number, slot), []).append(functools.partial(action, *args))

    for m in range(2):
        at(m, 2, last_slot, tick, m, 1, 0)
        at(m, 3, 0, tick, m, 1, 1)
        at(m, 3, last_slot, tick, m, 0, 0)
        at(m, 5, 0, tick, m, 1, 2)
        at(m, 4, last_slot, tick, m, 0, 1)
        at(m + 1, 1, 0, tick, m, 1, 3)
        at(m + 1, 1, last_slot, tick, m, 0, 2)
        at(m + 1, 1, last_slot, small_start, m, 0)
        at(m + 1, 2, last_slot, small_finish, m, 0)
        at(m + 1, 2, last_slot, small_start, m, 1)
        for t in range(4, g.bits + 1):
            at(m + 1, 2, last_slot, tick, m, 1, t)
        at(m + 1, 2, last_slot, tick, m, 0, 3)
        at(m + 1, 3, last_slot, small_finish, m, 1)
        at(m + 1, 3, last_slot, tick, m, 1, g.bits + 1)
        for t in range(4, g.bits + 1):
            at(m + 1, 3, last_slot, tick, m, 0, t)
        for r in range(2, g.bits - 1):
            at(m + 1, 3, last_slot, small_start, m, r)
            if r < g.bits - 2:
                at(m + 1, 3, last_slot, small_finish, m, r)
        at(m + 1, 4, 0, tick, m, 1, g.stages)
        at(m + 1, 5, last_slot, small_finish, m, g.bits - 2)
        at(m + 1, 5, last_slot, tick, m, 0, g.bits + 1)
        end = (m + 2, 1, 0) if m == 0 else (m + 1, 5, last_slot)
        at(*end, tick, m, 0, g.stages)

    def start_x(s):
        return lambda i: halo_start(i, s, 0)

    def start_gy(s):
        return lambda i: halo_start(i, s, 1)

    def start_weights(k, j):
        return lambda i: weights_start(i, k, j)

    sends = {
        (2, 0): [start_x(s) for s in range(S)],
        (2, 1): [start_gy(s) for s in range(S)],
        (3, 0): [start_weights(0, j) for j in range(TRIPLES)],
        (3, S - 1): [start_weights(1, j) for j in range(TRIPLES)],
    }
    def window(number, i, s):
        for (where, slot), actions in sends.items():
            if where == number:
                @pl.when((i < 2) & (s == slot))
                def _():
                    for action in actions:
                        action(i + 1)

    def slots(number, phase, i):
        def step(s, carry):
            phase(i, s)
            for (turn, where, slot), actions in plan.items():
                if where == number:
                    @pl.when((i == turn) & (s == slot))
                    def _():
                        for action in actions:
                            action()
            return carry

        lax.fori_loop(0, S, step, 0)

    def load_x(i):
        for s in range(S):
            pltpu.make_async_copy(x_h.at[net_of(i), s], rx.at[s], lx.at[s]).start()

    def load_gy(i):
        for s in range(S):
            pltpu.make_async_copy(gy_h.at[net_of(i), s], rg.at[s], lg.at[s]).start()

    load_x(0)
    load_gy(0)
    fill = g.low_rows + g.high_rows
    pk[:, :, :, fill:, :] = jnp.zeros((2, 2, F, g.pack - fill, LANES), F32)
    sb[:, place] = jnp.zeros((3, 16, g.wide), F32)
    for n in range(g.nets):
        own = own_embedding(n)
        for i in range(3):
            if (2 * i) % g.nets == n:
                sb[i, place, 8 : 8 + S, 0 : g.ef] = own.astype(F32)

    @pl.when(me == 0)
    def _():
        hb[:, :, :, 0] = jnp.zeros(hb.shape[:3] + hb.shape[4:], BF16)

    @pl.when(me == F - 1)
    def _():
        hb[:, :, :, 1] = jnp.zeros(hb.shape[:3] + hb.shape[4:], BF16)

    barrier = pltpu.get_barrier_semaphore()
    partners = [(b,) for b in range(g.bits)] + [(1, 2)]
    for df in range(1, F):
        pl.semaphore_signal(barrier, inc=1, device_id={"fsdp": peer(df)}, device_id_type=MESH)
    for bits in partners:
        pl.semaphore_signal(barrier, inc=1, device_id={"dp": other(*bits)}, device_id_type=MESH)
    pl.semaphore_wait(barrier, F - 1 + len(partners))
    weight_local(0).start()
    for s in range(S):
        halo_start(0, s, 0)

    def prepare_first(i, s):
        gradient_loaded(i, s)
        halo_take(i, s, 0)
        prepare(i, s)
        prepare_gradient(i, s)

    for s in range(S):
        input_loaded(0, s)
    slots(0, input_work, 0)
    for j in range(TRIPLES):
        weights_start(0, 0, j)
    for s in range(S):
        halo_start(0, s, 1)
    for j in range(TRIPLES):
        weights_start(0, 1, j)
    slots(0, prepare_first, 0)
    weights_forward(0, 0)
    weight_local(0).wait()
    weights_take(0, 0)
    weights_ready(0, 0)

    def first_of_all(i, s):
        first_phase(i, s)

        @pl.when((i == 0) & (s == S - 1))
        def _():
            weights_forward(0, 1)
            weights_take(0, 1)
            weights_ready(0, 1)

    def fourth_and_weights(i, s):
        fourth_phase(i, s)

        @pl.when((i < 2) & (s == 0))
        def _():
            for k in range(2):
                weights_forward(i + 1, k)

    def network(i, carry):
        @pl.when(i < 2)
        def _():
            gacc[...] = jnp.zeros(gacc.shape, F32)

        slots(1, first_of_all, i)
        weights_sent(i)

        @pl.when(i < 2)
        def _():
            load_x(i + 1)
            weight_local(i + 1).start()

        slots(2, second_phase, i)
        slots(3, third_phase, i)

        @pl.when(i < 2)
        def _():
            load_gy(i + 1)

        slots(4, fourth_and_weights, i)

        @pl.when(i < 2)
        def _():
            weight_local(i + 1).wait()
            for k in range(2):
                weights_take(i + 1, k)
                weights_ready(i + 1, k)

        slots(5, last_phase, i)
        return carry

    lax.fori_loop(0, 3, network, 0)


    def drain(i, carry):
        for s in range(S):
            for t in range(2):
                halo_sent(i, s, t)
            for e in range(4):
                for df in range(1, F):
                    row_copy(i, e, s, df, me).wait_send()
        return carry

    lax.fori_loop(0, 3, drain, 0)
    for s in range(S):
        in_grad_copy(2, s).wait()
    for m in range(2):
        for k in range(2):
            pltpu.make_async_copy(pk.at[m, k, me], cg_h.at[m, k], osem.at[m, k]).wait()
    pltpu.make_async_copy(ags, ag_h.at[1], osem.at[1, 2]).wait()


def place_body(g, y_c, dx_c, packed, affine, sums, y, dx, conv, affine_out, gain_out, bias_out):
    for s in range(g.s):
        for src, dst in ((y_c, y), (dx_c, dx)):
            for q in range(g.np):
                flat = src[0, s, :, q * LANES : (q + 1) * LANES].T
                dst[0, s, q] = flat[0 : g.w]
                dst[0, s, q + g.np] = flat[g.w : 2 * g.w]
    step = pl.program_id(0)

    @pl.when(step < 2)
    def _():
        split = g.low_rows - g.high_rows
        rest = g.c - LANES
        for k in range(2):
            conv[0, k, :, 0:LANES] = packed[0, k, 0 : g.low_rows, :]
            conv[0, k, 0 : g.high_rows, LANES : g.c] = packed[0, k, g.low_rows : g.low_rows + g.high_rows, 0:rest]
            conv[0, k, g.high_rows : g.low_rows, LANES : g.c] = packed[
                0, k, g.low_rows : g.low_rows + split, CHUNK : CHUNK + rest
            ]

    @pl.when(step < 2)
    def _():
        affine_out[...] = affine[...]

    @pl.when(step == 0)
    def _():
        gain_out[...] = sums[:, 0:2, 0 : g.shard]
        bias_out[...] = sums[:, 2:8, 0 : g.shard]


def on_device(
    block_input, embedding, out_cotangent, conv_weights, affine_weight, gains, biases, counts
):
    nets, slots, rows, width, chans = block_input.shape
    fsdp = lax.axis_size("fsdp")
    dp = lax.axis_size("dp")
    embed_rows = affine_weight.shape[1]
    g = settings(dp, fsdp, nets, slots, rows, width, chans, embed_rows)
    weights = conv_weights.reshape(nets, 2, 9, g.shard, chans)

    tiles = (g.np + 1) * LANES
    dma = pltpu.SemaphoreType.DMA
    scratch = [
        pltpu.VMEM((slots, rows, width, chans), BF16),
        pltpu.VMEM((slots, rows, width, chans), BF16),
        pltpu.VMEM((slots, rows, width, chans), BF16),
        pltpu.VMEM((2, slots, chans, g.px), BF16),
        pltpu.VMEM((slots, chans, g.px), BF16),
        pltpu.VMEM((slots, 3, chans, (g.np + 5) * LANES), BF16),
        pltpu.VMEM((slots, 3, chans, (g.np + 2) * LANES), BF16),
        pltpu.VMEM((slots, 3, chans, (g.np + 5) * LANES), BF16),
        pltpu.VMEM((2, slots, 2, 2, 2, width, chans), BF16),
        pltpu.VMEM((slots, chans, tiles), F32),
        pltpu.VMEM((slots, chans, tiles), F32),
        pltpu.VMEM((2, fsdp, 2, 9, g.shard, chans), BF16),
        pltpu.VMEM((2, chans, 9 * chans), BF16),
        pltpu.VMEM((2, chans, 9 * chans), BF16),
        pltpu.VMEM((2, 9 * chans, chans), F32),
        pltpu.VMEM((2, 2, fsdp, g.pack, LANES), F32),
        pltpu.VMEM((3 - g.split, 2, fsdp, g.half, LANES), F32),
        pltpu.VMEM((2, 3, fsdp, g.piece, LANES), F32),
        pltpu.VMEM((2, 2, fsdp - 1, g.piece, LANES), F32),
        pltpu.VMEM((2, g.bits - 3, g.piece, LANES), F32),
        pltpu.VMEM((chans, g.px), F32),
        pltpu.VMEM((slots, chans, g.px), BF16),
        pltpu.VMEM((embed_rows, 2 * chans), F32),
        pltpu.VMEM((3, slots, fsdp, 16, chans), F32),
        pltpu.VMEM((3, 3, slots, fsdp, 8, chans), F32),
        pltpu.VMEM((3, dp, 16, g.wide), F32),
        pltpu.VMEM((3, chans, LANES), F32),
        pltpu.VMEM((slots, 16, chans), F32),
        pltpu.VMEM((slots, 10, chans, LANES), F32),
        dma((slots,)),
        dma((slots,)),
        dma((slots,)),
        dma((3, slots, 2, 2)),
        dma((3, slots, 2, 2)),
        dma((3, 4, slots, fsdp)),
        dma((3, 4, slots, fsdp)),
        dma((3,)),
        dma((3, 2, 3, fsdp)),
        dma((3, 2, 3, fsdp)),
        dma((3, 2, fsdp)),
        dma((3, 2, fsdp)),
        dma((2, 2, g.stages, max(3, fsdp - 1))),
        dma((2, 2, g.stages, max(3, fsdp - 1))),
        dma((2, g.bits + 2)),
        dma((2, g.bits + 2)),
        dma((2, 3)),
    ]
    hbm = pl.BlockSpec(memory_space=pl.ANY)
    vmem = pl.BlockSpec(memory_space=pltpu.VMEM)
    smem = pl.BlockSpec(memory_space=pltpu.SMEM)
    channel_major = jax.ShapeDtypeStruct((nets, slots, chans, g.px), BF16)
    main = pl.pallas_call(
        functools.partial(kernel_body, g),
        out_shape=(
            channel_major,
            channel_major,
            jax.ShapeDtypeStruct((2, 2, g.pack, LANES), F32),
            jax.ShapeDtypeStruct((2, embed_rows, 2 * chans), F32),
            jax.ShapeDtypeStruct((2, 8, 2 * LANES), F32),
        ),
        in_specs=[hbm, hbm, hbm, vmem, vmem, vmem, vmem, smem],
        out_specs=(hbm, hbm, hbm, hbm, vmem),
        scratch_shapes=scratch,
        compiler_params=pltpu.CompilerParams(
            collective_id=0, has_side_effects=True, vmem_limit_bytes=64 << 20
        ),
    )(block_input, out_cotangent, weights, affine_weight, embedding, gains, biases, counts)

    def by_slot(step):
        return (step, 0, 0, 0)

    def by_conv(step):
        return (jnp.minimum(step, 1), 0, 0, 0)

    def by_net(step):
        return (jnp.minimum(step, 1), 0, 0)

    image = pl.BlockSpec((1, slots, rows, width, chans), lambda step: by_slot(step) + (0,))
    block_output, input_grad, conv_grads, affine_grad, gain_grads, bias_grads = pl.pallas_call(
        functools.partial(place_body, g),
        grid=(nets,),
        out_shape=(
            jax.ShapeDtypeStruct(block_input.shape, BF16),
            jax.ShapeDtypeStruct(block_input.shape, BF16),
            jax.ShapeDtypeStruct((2, 2, g.low_rows, chans), F32),
            jax.ShapeDtypeStruct((2, embed_rows, 2 * chans), F32),
            jax.ShapeDtypeStruct((2, 2, g.shard), F32),
            jax.ShapeDtypeStruct((2, 6, g.shard), F32),
        ),
        in_specs=[
            pl.BlockSpec((1, slots, chans, g.px), by_slot),
            pl.BlockSpec((1, slots, chans, g.px), by_slot),
            pl.BlockSpec((1, 2, g.pack, LANES), by_conv),
            pl.BlockSpec((1, embed_rows, 2 * chans), by_net),
            vmem,
        ],
        out_specs=(
            image,
            image,
            pl.BlockSpec((1, 2, g.low_rows, chans), by_conv),
            pl.BlockSpec((1, embed_rows, 2 * chans), by_net),
            vmem,
            vmem,
        ),
        compiler_params=pltpu.CompilerParams(vmem_limit_bytes=63 << 20),
    )(*main)
    conv_grads = conv_grads.reshape(2, 2, 3, 3, g.shard, chans)
    return block_output, input_grad, conv_grads, affine_grad, gain_grads, bias_grads


def solution(mesh):
    placed = (
        P(None, "dp", "fsdp", None, None),
        P(None, "dp", None),
        P(None, "dp", "fsdp", None, None),
        P(None, None, None, None, "fsdp", None),
        P(None, "fsdp", None),
        P(None, None, "fsdp"),
        P(None, None, "fsdp"),
        P("dp"),
    )
    return jax.shard_map(
        on_device,
        mesh=mesh,
        in_specs=placed,
        out_specs=(
            P(None, "dp", "fsdp", None, None),
            P(None, "dp", "fsdp", None, None),
            P(None, None, None, None, "fsdp", None),
            P(None, "fsdp", None),
            P(None, None, "fsdp"),
            P(None, None, "fsdp"),
        ),
        check_vma=False,
    )
```

```python
import functools
import types

import jax
import jax.numpy as jnp
from jax import lax
from jax.experimental import pallas as pl
from jax.experimental.pallas import tpu as pltpu
from jax.sharding import PartitionSpec as P

GROUPS = 32
EPSILON = 1e-05
LANES = 128
CHUNK = 64
MESH = pl.DeviceIdType.MESH
F32 = jnp.float32
BF16 = jnp.bfloat16

MU0, R0, G0, G1, B1, B2, B3, SC1, SH, SGY, MU1, R1, SUMH = range(13)
PA0, PB0, PMU0, PBIAS, PA1, PB1, PMU1, PDA, PDB, PDC = range(10)


def settings(dp_size, fsdp_size, nets, slots, rows, width, chans, embed_rows):
    g = types.SimpleNamespace()
    g.dp, g.f, g.nets, g.s, g.r, g.w, g.c, g.ef = (
        dp_size, fsdp_size, nets, slots, rows, width, chans, embed_rows,
    )
    g.np = rows // 2
    g.px = g.np * LANES
    g.count = float(rows * fsdp_size * width * (chans // GROUPS))
    g.pixels = float(rows * fsdp_size * width)
    g.bits = dp_size.bit_length() - 1
    g.shard = chans // fsdp_size
    g.low_rows = 9 * g.shard
    g.high_rows = -(-g.low_rows // 16) * 8
    g.pack = -(-(g.low_rows + g.high_rows) // 64) * 64
    g.half = g.pack // 2
    g.piece = g.pack // 8
    g.wide = max(2 * chans, embed_rows)
    g.stages = g.bits + 2
    g.split = 2 if g.shard % 32 == 0 else 1
    g.rows = g.shard // g.split
    return g


def kernel_body(
    g,
    x_h, gy_h, w_h, aff, emb, gains, biases, counts,
    y_h, dx_h, cg_h, ag_h, sg,
    rx, rg, dhp, xc, gc, xa0, xa1, xg, hb, hbuf, dub, wraw, wf, wb, gacc, pk, r0b, r1b, ryb, rbb,
    ybuf, yc, ags, ex1, ex2, sb, acc, rowt, prm,
    lx, lg, ysem, hs, hr, es, er, wl, wys, wyr, wcs, wcr, cs, cr, ss, sr, osem,
):
    me = lax.axis_index("fsdp")
    dp = lax.axis_index("dp")
    C, NP, F, S, R = g.c, g.np, g.f, g.s, g.r
    PX = g.px

    def net_of(i):
        return (2 * i) % g.nets

    def peer(df):
        return (me + df) % F

    def source(df):
        return (me + F - df) % F

    def bit(b):
        return (dp // (1 << b)) % 2

    def other(*bits):
        where = dp
        for b in bits:
            where = where + (1 << b) * (1 - 2 * bit(b))
        return where

    def remote(src, dst, send, recv, where):
        return pltpu.make_async_remote_copy(
            src_ref=src, dst_ref=dst, send_sem=send, recv_sem=recv,
            device_id=where, device_id_type=MESH,
        )

    def tile(t):
        if isinstance(t, int):
            return pl.ds(t * LANES, LANES)
        return pl.ds(pl.multiple_of(t * LANES, LANES), LANES)

    def kept(s):
        return jnp.where(s < counts[0], 1.0, 0.0)

    lane = lax.broadcasted_iota(jnp.int32, (C, LANES), 1)
    low_lanes = lane < g.w
    top = (me > 0).astype(jnp.int32)
    bottom = (me < F - 1).astype(jnp.int32)
    edge_ok = jnp.where(low_lanes, top, bottom) > 0


    def halo_copy(i, s, t, down):
        src = (x_h, gy_h)[t]
        n = net_of(i)
        if down:
            return remote(
                src.at[n, s, pl.ds(R - 2, 2)], hb.at[i % 2, s, t, 0],
                hs.at[i, s, t, 1], hr.at[i, s, t, 1], {"fsdp": (me + 1) % F},
            )
        return remote(
            src.at[n, s, pl.ds(0, 2)], hb.at[i % 2, s, t, 1],
            hs.at[i, s, t, 0], hr.at[i, s, t, 0], {"fsdp": (me + F - 1) % F},
        )

    def halo_start(i, s, t):
        @pl.when(me > 0)
        def _():
            halo_copy(i, s, t, False).start()

        @pl.when(me < F - 1)
        def _():
            halo_copy(i, s, t, True).start()

    def halo_take(i, s, t):
        @pl.when(me > 0)
        def _():
            halo_copy(i, s, t, True).wait_recv()

        @pl.when(me < F - 1)
        def _():
            halo_copy(i, s, t, False).wait_recv()

    def halo_sent(i, s, t):
        @pl.when(me > 0)
        def _():
            halo_copy(i, s, t, False).wait_send()

        @pl.when(me < F - 1)
        def _():
            halo_copy(i, s, t, True).wait_send()

    def row_copy(i, e, s, df, who):
        ref = ex1.at[i, s, who] if e == 0 else ex2.at[i, e - 1, s, who]
        return remote(ref, ref, es.at[i, e, s, df], er.at[i, e, s, df], {"fsdp": peer(df)})

    def rows_start(i, e, s):
        for df in range(1, F):
            row_copy(i, e, s, df, me).start()

    def rows_take(i, e, s):
        for df in range(1, F):
            row_copy(i, e, s, df, source(df)).wait_recv()
        parts = [ex1[i, s, f] if e == 0 else ex2[i, e - 1, s, f] for f in range(F)]
        total = parts[0]
        for part in parts[1:]:
            total = total + part
        return total

    mine = dp % 2

    TRIPLES = 3

    def weight_rows(half):
        return pl.ds(pl.multiple_of(half * g.rows, g.rows), g.rows)

    def weight_copy(i, k, j, df, who):
        taps, rows = pl.ds(3 * j, 3), weight_rows(mine if g.split == 2 else 0)
        return remote(
            w_h.at[net_of(i), k, taps, rows], wraw.at[i % 2, who, k, taps, rows],
            wys.at[i, k, j, df], wyr.at[i, k, j, df], {"fsdp": peer(df)},
        )

    def weight_share(i, k, df, half):
        ref = wraw.at[i % 2, source(df), k, :, weight_rows(half)]
        return remote(ref, ref, wcs.at[i, k, df], wcr.at[i, k, df], {"dp": other(0)})

    def weight_local(i):
        return pltpu.make_async_copy(w_h.at[net_of(i)], wraw.at[i % 2, me], wl.at[i])

    def weights_start(i, k, j):
        for df in range(1, F):
            weight_copy(i, k, j, df, me).start()

    def weights_forward(i, k):
        for df in range(1, F):
            for j in range(TRIPLES):
                weight_copy(i, k, j, df, source(df)).wait_recv()
            if g.split == 2:
                weight_share(i, k, df, mine).start()

    def weights_take(i, k):
        if g.split == 2:
            for df in range(1, F):
                weight_share(i, k, df, 1 - mine).wait_recv()

    def weights_sent(i):
        for k in range(2):
            for df in range(1, F):
                for j in range(TRIPLES):
                    weight_copy(i, k, j, df, me).wait_send()
                if g.split == 2:
                    weight_share(i, k, df, mine).wait_send()


    def rows_at(offset, size):
        if not isinstance(offset, int):
            offset = pl.multiple_of(offset, 8)
        return pl.ds(offset, size)

    half_start = bit(0) * g.half
    PAIR = ((1,), (2,), (1, 2))

    def piece_start(bits):
        b1 = 1 - bit(1) if 1 in bits else bit(1)
        b2 = 1 - bit(2) if 2 in bits else bit(2)
        return half_start + (2 * b1 + b2) * g.piece

    def core_sums(m, k):
        return r0b.at[0 if g.split == 2 else m, k]

    def stage_copies(m, k, t):
        def sems(j):
            return cs.at[m, k, t, j], cr.at[m, k, t, j]

        mine_at = rows_at(piece_start(()), g.piece)
        own = pk.at[m, k, me, mine_at]
        if t == 0:
            there = rows_at((1 - bit(0)) * g.half, g.half)
            return [(remote(pk.at[m, k, :, there], core_sums(m, k), *sems(0), {"dp": other(0)}), None)]
        if t == 1:
            return [
                (
                    remote(
                        pk.at[m, k, :, rows_at(piece_start(bits), g.piece)], r1b.at[k, j],
                        *sems(j), {"dp": other(*bits)},
                    ),
                    None,
                )
                for j, bits in enumerate(PAIR)
            ]
        if t == 2:
            return [
                (remote(pk.at[m, k, peer(df), mine_at], ryb.at[m, k, df - 1], *sems(df - 1), {"fsdp": peer(df)}), None)
                for df in range(1, F)
            ]
        if t < g.bits:
            return [(remote(own, rbb.at[k, t - 3], *sems(0), {"dp": other(t)}), None)]
        if t == g.bits:
            return [
                (
                    remote(own, own, *sems(j), {"dp": other(*bits)}),
                    remote(own, pk.at[m, k, me, rows_at(piece_start(bits), g.piece)], *sems(j), {"dp": other(*bits)}),
                )
                for j, bits in enumerate(PAIR)
            ]
        own = pk.at[m, k, me, rows_at(half_start, g.half)]
        there = pk.at[m, k, me, rows_at((1 - bit(0)) * g.half, g.half)]
        return [(
            remote(own, own, *sems(0), {"dp": other(0)}), remote(own, there, *sems(0), {"dp": other(0)}),
        )]

    def add_rows(dst, start, sources, size):
        step = max(n for n in range(8, 65, 8) if size % n == 0)

        def body(j, carry):
            at = rows_at(start + j * step, step)
            total = dst[at, :]
            for src in sources:
                total = total + src[rows_at(j * step, step), :]
            dst[at, :] = total
            return carry

        lax.fori_loop(0, size // step, body, 0)

    def stage_start(m, k, t):
        for copy, _ in stage_copies(m, k, t):
            copy.start()

    def stage_finish(m, k, t):
        for copy, received in stage_copies(m, k, t):
            copy.wait_send()
            (received or copy).wait_recv()
        if t == 0:
            for f in range(F):
                add_rows(pk.at[m, k, f], half_start, [core_sums(m, k).at[f]], g.half)
        elif t == 1:
            for f in range(F):
                add_rows(pk.at[m, k, f], piece_start(()), [r1b.at[k, j, f] for j in range(3)], g.piece)
        elif t == 2:
            add_rows(pk.at[m, k, me], piece_start(()), [ryb.at[m, k, df - 1] for df in range(1, F)], g.piece)
        elif t < g.bits:
            add_rows(pk.at[m, k, me], piece_start(()), [rbb.at[k, t - 3]], g.piece)

    place = bit(1) + 2 * bit(2) + 4 * bit(0) + (dp // 8) * 8

    def small_copies(m, r, received):
        targets = PAIR if r == 0 else ((0,),) if r == 1 else ((r + 1,),)
        size = 1 if r == 0 else 1 << (r + 1)
        flips = {1: 1, 2: 2, 0: 4}
        copies = []
        for j, bits in enumerate(targets):
            there = place
            for b in bits:
                there = there + flips.get(b, 1 << b) * (1 - 2 * bit(b))
            own = sb.at[m, pl.ds((place // size) * size, size)]
            dst = sb.at[m, pl.ds((there // size) * size, size)] if received else own
            sem = j if r == 0 else r + 2
            copies.append(remote(own, dst, ss.at[m, sem], sr.at[m, sem], {"dp": other(*bits)}))
        return copies

    def small_start(m, r):
        for copy in small_copies(m, r, False):
            copy.start()

    def small_finish(m, r):
        for copy in small_copies(m, r, False):
            copy.wait_send()
        for copy in small_copies(m, r, True):
            copy.wait_recv()
        if r == g.bits - 2:
            finish_small(m)

    def tick(m, k, t):
        if t == 0:
            pack_rows(m, k)
        else:
            stage_finish(m, k, t - 1)
        if t < g.stages:
            stage_start(m, k, t)
        else:
            pltpu.make_async_copy(pk.at[m, k, me], cg_h.at[m, k], osem.at[m, k]).start()

    def finish_small(m):
        total = sb[m, 0, 0:8, 0 : 2 * LANES]
        for d in range(1, g.dp):
            total = total + sb[m, d, 0:8, 0 : 2 * LANES]
        sg[m] = pltpu.roll(total, 2 * LANES - me * g.shard, 1)
        block = sb[m, :, 8:16, :].reshape(g.dp * 8, g.wide)
        index = lax.broadcasted_iota(jnp.int32, (g.dp * 8, g.ef), 0) & 7
        left = jnp.where(index < S, block[:, : g.ef], 0.0).astype(BF16)
        right = pltpu.roll(block[:, : 2 * C], g.dp * 8 - S, 0).astype(BF16)
        if m > 0:
            pltpu.make_async_copy(ags, ag_h.at[m - 1], osem.at[m - 1, 2]).wait()
        ags[...] = lax.dot_general(left, right, (((0,), (0,)), ((), ())), preferred_element_type=F32)
        pltpu.make_async_copy(ags, ag_h.at[m], osem.at[m, 2]).start()

    def pack_rows(m, k):
        for f in range(F):
            for tap in range(9):
                first, last = tap * g.shard, (tap + 1) * g.shard
                c0 = tap * C + f * g.shard
                pk[m, k, f, first:last, :] = gacc[k, c0 : c0 + g.shard, 0:LANES]
                for lo, hi, lanes in ((0, g.high_rows, 0), (g.high_rows, g.low_rows, CHUNK)):
                    a, b = max(first, lo), min(last, hi)
                    if a < b:
                        at = g.low_rows + a - lo
                        pk[m, k, f, at : at + b - a, lanes : lanes + C - LANES] = gacc[
                            k, c0 + a - first : c0 + b - first, LANES:C
                        ]


    def shifted(v):
        col = lax.broadcasted_iota(jnp.int32, v.shape, 1) & (g.w - 1)
        left = jnp.where(col == 0, 0.0, pltpu.roll(v, 1, 1))
        right = jnp.where(col == g.w - 1, 0.0, pltpu.roll(v, LANES - 1, 1))
        return left, v, right

    def put(buf, s, rows, t, v):
        for j, moved in enumerate(shifted(v)):
            buf[s, j, rows, tile(t)] = moved.astype(BF16)

    def put_edges(buf, s, first_edge, second_edge):
        near = shifted(first_edge)
        far = None if second_edge is None else shifted(second_edge)
        for j in range(3):
            first = buf[s, j, :, tile(1)].astype(F32)
            last = buf[s, j, :, tile(NP)].astype(F32)
            buf[s, j, :, tile(0)] = jnp.where(low_lanes, near[j], pltpu.roll(last, g.w, 1)).astype(BF16)
            buf[s, j, :, tile(NP + 1)] = jnp.where(low_lanes, pltpu.roll(first, g.w, 1), near[j]).astype(BF16)
            if far is not None:
                buf[s, j, :, tile(NP + 2)] = jnp.where(low_lanes, far[j], last).astype(BF16)
                buf[s, j, :, tile(NP + 3)] = near[j].astype(BF16)
                buf[s, j, :, tile(NP + 4)] = jnp.where(low_lanes, first, far[j]).astype(BF16)

    def windows(buf, s, back, edge):
        pieces = []
        for i in range(3):
            for j in range(3):
                ti, tj = (2 - i, 2 - j) if back else (i, j)
                piece = buf[s, tj, :, ti * LANES : ti * LANES + PX]
                if edge:
                    piece = jnp.concatenate([piece, buf[s, tj, :, tile(NP + 2 + ti)]], axis=1)
                pieces.append(piece)
        return jnp.concatenate(pieces, axis=0)

    def chunks():
        return [pl.ds(c0, CHUNK) for c0 in range(0, C, CHUNK)]

    def quads():
        order = [NP - 1] + list(range(NP - 1))
        return [order[q : q + 4] for q in range(0, NP, 4)]

    def clear(count):
        for k in range(count):
            acc[k] = jnp.zeros((C, LANES), F32)

    def total_row(k):
        return jnp.sum(acc[k].T, axis=0, keepdims=True)

    def group_rows(rows):
        high = rows.astype(BF16)
        rest = rows - high.astype(F32)
        middle = rest.astype(BF16)
        low = (rest - middle.astype(F32)).astype(BF16)
        a = lax.broadcasted_iota(jnp.int32, (C, C), 0) // (C // GROUPS)
        b = lax.broadcasted_iota(jnp.int32, (C, C), 1) // (C // GROUPS)
        same = jnp.where(a == b, 1.0, 0.0).astype(BF16)
        three = jnp.dot(jnp.concatenate([high, middle, low], axis=0).astype(BF16), same, preferred_element_type=F32)
        n = rows.shape[0]
        return three[0:n] + three[n : 2 * n] + three[2 * n : 3 * n]

    def stack(*rows):
        fill = 8 - len(rows)
        return jnp.concatenate(list(rows) + [jnp.zeros((fill, C), F32)] * (fill > 0), axis=0)

    def spread(s, k, row):
        prm[s, k] = jnp.broadcast_to(row, (LANES, C)).T

    def save(s, k, row):
        rowt[s, k : k + 1, :] = row

    def row(s, k):
        return rowt[s, k : k + 1, :]

    def moments(total):
        grouped = group_rows(total)
        mean = grouped[0:1] / g.count
        variance = grouped[1:2] / g.count - mean * mean
        return mean, lax.rsqrt(variance + EPSILON)

    def slope_twice(w, t):
        return (1.0 + t) * (1.0 + w * (1.0 - t))

    def pair(buf, s, q):
        return jnp.concatenate([buf[s, q], buf[s, q + NP]], axis=0)

    def pixels(buf, s):
        return jnp.concatenate([buf[s, h] for q in range(NP) for h in (q, q + NP)], axis=0)

    def own_embedding(n):
        whole = emb[n].astype(F32)
        return pltpu.roll(whole, whole.shape[1] - me * g.ef, 1)[:, 0 : g.ef]

    def weight_sums(k, acts, grads, s, factor):
        right = pixels(grads, s)
        for i in range(3):
            left = jnp.concatenate(
                [acts[s, j, :, i * LANES : i * LANES + PX] for j in range(3)], axis=0
            )
            rows = pl.ds(3 * C * i, 3 * C)
            o = jnp.dot(left, right, preferred_element_type=F32)
            gacc[k, rows] = gacc[k, rows] + (o if factor is None else o * factor)


    def input_work(i, s):
        n = net_of(i)
        clear(2)
        for qs in quads():
            for q in qs:
                xc[i % 2, s, :, tile(q)] = pair(rx, s, q).T
            for rows in chunks():
                a0, a1 = acc[0, rows], acc[1, rows]
                for q in qs:
                    xf = xc[i % 2, s, rows, tile(q)].astype(F32)
                    a0 = a0 + xf
                    a1 = a1 + xf * xf
                acc[0, rows], acc[1, rows] = a0, a1
        mod = jnp.dot(own_embedding(n).astype(BF16), aff[n], preferred_element_type=F32)
        which = lax.broadcasted_iota(jnp.int32, mod.shape, 0) == s
        mod = jnp.sum(jnp.where(which, mod, 0.0), axis=0, keepdims=True)
        ex1[i, s, me, 0:8] = stack(total_row(0), total_row(1), mod[:, 0:C], mod[:, C : 2 * C])
        vectors = jnp.concatenate([gains[n], biases[n]], axis=0).astype(F32)
        vectors = jnp.concatenate([vectors, jnp.zeros((8, 2 * LANES - g.shard), F32)], axis=1)
        ex1[i, s, me, 8:16] = pltpu.roll(vectors, me * g.shard, 1)[:, 0:C]
        rows_start(i, 0, s)

    def input_loaded(i, s):
        pltpu.make_async_copy(x_h.at[net_of(i), s], rx.at[s], lx.at[s]).wait()

    def weights_ready(i, k):
        for tap in range(9):
            blocks = [wraw[i % 2, f, k, tap] for f in range(F)]
            if g.shard % 16:
                blocks = [b.astype(F32) for b in blocks]
            whole = jnp.concatenate(blocks, axis=0).astype(BF16)
            wb[k, :, tap * C : (tap + 1) * C] = whole
            wf[k, :, tap * C : (tap + 1) * C] = whole.T

    def edge_tiles(i, s, t):
        near = jnp.concatenate([hb[i % 2, s, t, 0, 1], hb[i % 2, s, t, 1, 0]], axis=0).T.astype(F32)
        far = jnp.concatenate([hb[i % 2, s, t, 0, 0], hb[i % 2, s, t, 1, 1]], axis=0).T.astype(F32)
        return near, far

    def gradient_loaded(i, s):
        pltpu.make_async_copy(gy_h.at[net_of(i), s], rg.at[s], lg.at[s]).wait()

    def prepare(i, s):
        total = rows_take(i, 0, s)
        mean, inverse = moments(total[0:8])
        save(s, MU0, mean)
        save(s, R0, inverse)
        gain0, gain1 = total[8:9], total[9:10]
        save(s, G0, gain0)
        save(s, G1, gain1)
        save(s, B2, total[12:13])
        save(s, B3, total[13:14])
        save(s, SC1, total[2:3] + total[14:15] + 1.0)
        save(s, SH, total[3:4] + total[15:16])
        scale = inverse * gain0
        spread(s, PA0, 0.5 * scale)
        spread(s, PB0, 0.5 * (total[10:11] - mean * scale))
        spread(s, PMU0, mean)
        spread(s, PBIAS, total[11:12])

        def act(xf, a, b):
            w = xf * a + b
            return w * jnp.tanh(w) + w

        for n, qs in enumerate(quads()):
            for rows in chunks():
                a, b = prm[s, PA0, rows], prm[s, PB0, rows]
                for q in qs:
                    put(xa0, s, rows, q + 1, act(xc[i % 2, s, rows, tile(q)].astype(F32), a, b))
            if n == 0:
                near, far = edge_tiles(i, s, 0)
                near = jnp.where(edge_ok, act(near, prm[s, PA0], prm[s, PB0]), 0.0)
                far = jnp.where(edge_ok, act(far, prm[s, PA0], prm[s, PB0]), 0.0)
                put_edges(xa0, s, near, far)

    def prepare_gradient(i, s):
        kf = kept(s)
        acc[2] = jnp.zeros((C, LANES), F32)
        for qs in quads():
            for q in qs:
                gc[s, :, tile(q)] = (pair(rg, s, q).T.astype(F32) * kf).astype(BF16)
            for rows in chunks():
                a2 = acc[2, rows]
                for q in qs:
                    gf = gc[s, rows, tile(q)].astype(F32)
                    a2 = a2 + gf
                    put(xg, s, rows, q + 1, gf)
                acc[2, rows] = a2
        save(s, SGY, total_row(2))

    def first_phase(i, s):
        kf = kept(s)

        def gradient_edges():
            near, far = edge_tiles(i, s, 1)
            put_edges(xg, s, jnp.where(edge_ok, near, 0.0) * kf, jnp.where(edge_ok, far, 0.0) * kf)

        def work(with_prepare):
            if with_prepare:
                gradient_loaded(i, s)
                halo_take(i, s, 0)
                halo_take(i, s, 1)
                prepare(i, s)
            clear(2)
            hbuf[s] = jnp.dot(wf[0], windows(xa0, s, False, True), preferred_element_type=F32)
            for q in range(NP + 1):
                for rows in chunks():
                    h = hbuf[s, rows, tile(q)] + prm[s, PBIAS, rows]
                    hbuf[s, rows, tile(q)] = h
                    if q < NP:
                        acc[0, rows] = acc[0, rows] + h
                        acc[1, rows] = acc[1, rows] + h * h
            if with_prepare:
                prepare_gradient(i, s)
                gradient_edges()

        pl.when(i == 0)(functools.partial(work, False))
        pl.when(i > 0)(functools.partial(work, True))
        ex2[i, 0, s, me] = stack(total_row(0), total_row(1), row(s, SGY))
        rows_start(i, 1, s)

        @pl.when(i == 0)
        def _():
            halo_take(i, s, 1)
            gradient_edges()

    def second_phase(i, s):
        total = rows_take(i, 1, s)
        window(2, i, s)
        mean, inverse = moments(total)
        save(s, MU1, mean)
        save(s, R1, inverse)
        save(s, SUMH, total[0:1])
        save(s, SGY, total[2:3])
        scale = inverse * row(s, G1)
        spread(s, PA1, 0.5 * scale * row(s, SC1))
        spread(s, PB1, 0.5 * (row(s, SH) + (row(s, B2) - mean * scale) * row(s, SC1)))
        spread(s, PMU1, mean)
        clear(2)
        dub[s] = jnp.dot(wb[1], windows(xg, s, True, True), preferred_element_type=F32)
        for q in range(NP + 1):
            for rows in chunks():
                a, b, mu = prm[s, PA1, rows], prm[s, PB1, rows], prm[s, PMU1, rows]
                h = hbuf[s, rows, tile(q)]
                w = h * a + b
                t = jnp.tanh(w)
                d = dub[s, rows, tile(q)] * slope_twice(w, t)
                dub[s, rows, tile(q)] = d
                if q < NP:
                    put(xa1, s, rows, q + 1, w * t + w)
                    acc[0, rows] = acc[0, rows] + d
                    acc[1, rows] = acc[1, rows] + d * (h - mu)
        w = hbuf[s, :, tile(NP)] * prm[s, PA1] + prm[s, PB1]
        put_edges(xa1, s, jnp.where(edge_ok, w * jnp.tanh(w) + w, 0.0), None)
        ex2[i, 1, s, me] = stack(0.5 * total_row(0), 0.5 * total_row(1))
        rows_start(i, 2, s)

        @pl.when(i < 2)
        def _():
            weight_sums(1, xa1, rg, s, kept(s))

    def out_copy(i, s):
        return pltpu.make_async_copy(yc.at[s], y_h.at[net_of(i), s], ysem.at[s])

    def in_grad_copy(i, s):
        return pltpu.make_async_copy(yc.at[s], dx_h.at[net_of(i), s], ysem.at[s])

    def third_phase(i, s):
        kf = kept(s)
        total = rows_take(i, 2, s)
        window(3, i, s)
        spread(s, PBIAS, row(s, B3))
        s1, s2 = total[0:1], total[1:2] * row(s, R1)
        sc1, gain1, inverse, mean = row(s, SC1), row(s, G1), row(s, R1), row(s, MU1)
        grouped = group_rows(stack(gain1 * sc1 * s1, gain1 * sc1 * s2))
        m1, m2 = grouped[0:1] / g.count, grouped[1:2] / g.count
        a = inverse * sc1 * gain1
        b = -inverse * inverse * m2
        c = -inverse * m1 - mean * b
        spread(s, PDA, 0.5 * a)
        spread(s, PDB, b)
        spread(s, PDC, c)
        dscale = gain1 * s2 + row(s, B2) * s1
        here = sb.at[i, place]
        here[1:2, 0:C] = here[1:2, 0:C] + sc1 * s2
        here[3:4, 0:C] = here[3:4, 0:C] + a * s1 + b * row(s, SUMH) + c * g.pixels
        here[4:5, 0:C] = here[4:5, 0:C] + sc1 * s1
        here[5:6, 0:C] = here[5:6, 0:C] + row(s, SGY)
        here[6:7, 0:C] = here[6:7, 0:C] + dscale
        here[7:8, 0:C] = here[7:8, 0:C] + s1
        modulation = jnp.concatenate([dscale, s1], axis=1).astype(BF16).astype(F32)
        for slot in range(S):
            at = 8 + S + slot
            here[at : at + 1, 0 : 2 * C] = jnp.where(s == slot, modulation, here[at : at + 1, 0 : 2 * C])

        def output():
            for q in range(NP):
                for rows in chunks():
                    v = ybuf[rows, tile(q)] + prm[s, PBIAS, rows]
                    v = (v + xc[i % 2, s, rows, tile(q)].astype(F32)) * kf
                    yc[s, rows, tile(q)] = v.astype(BF16)

        def hidden_grad(with_weights):
            ybuf[...] = jnp.dot(wf[1], windows(xa1, s, False, False), preferred_element_type=F32)
            for n, qs in enumerate(quads()):
                for rows in chunks():
                    pa, pb, pc = prm[s, PDA, rows], prm[s, PDB, rows], prm[s, PDC, rows]
                    for q in qs:
                        d = dub[s, rows, tile(q)] * pa + hbuf[s, rows, tile(q)] * pb + pc
                        put(xg, s, rows, q + 1, d)
                if with_weights:
                    for q in qs:
                        flat = xg[s, 1, :, tile(q + 1)].T
                        dhp[s, q] = flat[0 : g.w]
                        dhp[s, q + NP] = flat[g.w : 2 * g.w]
                if n == 0:
                    d = dub[s, :, tile(NP)] * prm[s, PDA] + hbuf[s, :, tile(NP)] * prm[s, PDB] + prm[s, PDC]
                    put_edges(xg, s, jnp.where(edge_ok, d, 0.0), None)

        @pl.when(i > 0)
        def _():
            in_grad_copy(i, s).wait()

        @pl.when(i < 2)
        def _():
            hidden_grad(True)
            input_loaded(i + 1, s)
            weight_sums(0, xa0, dhp, s, None)
            output()
            input_work(i + 1, s)

        @pl.when(i == 2)
        def _():
            hidden_grad(False)
            output()

        out_copy(i, s).start()

    def fourth_phase(i, s):
        clear(2)
        hbuf[s, :, 0:PX] = jnp.dot(wb[0], windows(xg, s, True, False), preferred_element_type=F32)
        for q in range(NP):
            for rows in chunks():
                xf = xc[i % 2, s, rows, tile(q)].astype(F32)
                w = xf * prm[s, PA0, rows] + prm[s, PB0, rows]
                d = hbuf[s, rows, tile(q)] * slope_twice(w, jnp.tanh(w))
                hbuf[s, rows, tile(q)] = d
                acc[0, rows] = acc[0, rows] + d
                acc[1, rows] = acc[1, rows] + d * (xf - prm[s, PMU0, rows])
        ex2[i, 2, s, me] = stack(0.5 * total_row(0), 0.5 * total_row(1))
        rows_start(i, 3, s)

    def last_phase(i, s):
        total = rows_take(i, 3, s)
        inverse, mean, gain0 = row(s, R0), row(s, MU0), row(s, G0)
        s3, s4 = total[0:1], total[1:2] * inverse
        grouped = group_rows(stack(gain0 * s3, gain0 * s4))
        m1, m2 = grouped[0:1] / g.count, grouped[1:2] / g.count
        b = -inverse * inverse * m2
        spread(s, PA1, 0.5 * inverse * gain0)
        spread(s, PB1, b)
        spread(s, PMU1, -inverse * m1 - mean * b)
        here = sb.at[i, place]
        here[0:1, 0:C] = here[0:1, 0:C] + s4
        here[2:3, 0:C] = here[2:3, 0:C] + s3
        out_copy(i, s).wait()
        for qs in quads():
            for rows in chunks():
                pa, pb, pc = prm[s, PA1, rows], prm[s, PB1, rows], prm[s, PMU1, rows]
                for q in qs:
                    xf = xc[i % 2, s, rows, tile(q)].astype(F32)
                    v = hbuf[s, rows, tile(q)] * pa + xf * pb + pc + gc[s, rows, tile(q)].astype(F32)
                    yc[s, rows, tile(q)] = v.astype(BF16)
        in_grad_copy(i, s).start()


    last_slot = S - 1
    plan = {}

    def at(i, number, slot, action, *args):
        plan.setdefault((i, number, slot), []).append(functools.partial(action, *args))

    for m in range(2):
        at(m, 2, last_slot, tick, m, 1, 0)
        at(m, 3, 0, tick, m, 1, 1)
        at(m, 3, last_slot, tick, m, 0, 0)
        at(m, 5, 0, tick, m, 1, 2)
        at(m, 4, last_slot, tick, m, 0, 1)
        at(m + 1, 1, 0, tick, m, 1, 3)
        at(m + 1, 1, last_slot, tick, m, 0, 2)
        at(m + 1, 1, last_slot, small_start, m, 0)
        at(m + 1, 2, last_slot, small_finish, m, 0)
        at(m + 1, 2, last_slot, small_start, m, 1)
        for t in range(4, g.bits + 1):
            at(m + 1, 2, last_slot, tick, m, 1, t)
        at(m + 1, 2, last_slot, tick, m, 0, 3)
        at(m + 1, 3, last_slot, small_finish, m, 1)
        at(m + 1, 3, last_slot, tick, m, 1, g.bits + 1)
        for t in range(4, g.bits + 1):
            at(m + 1, 3, last_slot, tick, m, 0, t)
        for r in range(2, g.bits - 1):
            at(m + 1, 3, last_slot, small_start, m, r)
            if r < g.bits - 2:
                at(m + 1, 3, last_slot, small_finish, m, r)
        at(m + 1, 4, 0, tick, m, 1, g.stages)
        at(m + 1, 5, last_slot, small_finish, m, g.bits - 2)
        at(m + 1, 5, last_slot, tick, m, 0, g.bits + 1)
        end = (m + 2, 1, 0) if m == 0 else (m + 1, 5, last_slot)
        at(*end, tick, m, 0, g.stages)

    def start_x(s):
        return lambda i: halo_start(i, s, 0)

    def start_gy(s):
        return lambda i: halo_start(i, s, 1)

    def start_weights(k, j):
        return lambda i: weights_start(i, k, j)

    sends = {
        (2, 0): [start_x(s) for s in range(S)],
        (2, 1): [start_gy(s) for s in range(S)],
        (3, 0): [start_weights(0, j) for j in range(TRIPLES)],
        (3, S - 1): [start_weights(1, j) for j in range(TRIPLES)],
    }
    def window(number, i, s):
        for (where, slot), actions in sends.items():
            if where == number:
                @pl.when((i < 2) & (s == slot))
                def _():
                    for action in actions:
                        action(i + 1)

    def slots(number, phase, i):
        def step(s, carry):
            phase(i, s)
            for (turn, where, slot), actions in plan.items():
                if where == number:
                    @pl.when((i == turn) & (s == slot))
                    def _():
                        for action in actions:
                            action()
            return carry

        lax.fori_loop(0, S, step, 0)

    def load_x(i):
        for s in range(S):
            pltpu.make_async_copy(x_h.at[net_of(i), s], rx.at[s], lx.at[s]).start()

    def load_gy(i):
        for s in range(S):
            pltpu.make_async_copy(gy_h.at[net_of(i), s], rg.at[s], lg.at[s]).start()

    load_x(0)
    load_gy(0)
    fill = g.low_rows + g.high_rows
    pk[:, :, :, fill:, :] = jnp.zeros((2, 2, F, g.pack - fill, LANES), F32)
    sb[:, place] = jnp.zeros((3, 16, g.wide), F32)
    for n in range(g.nets):
        own = own_embedding(n)
        for i in range(3):
            if (2 * i) % g.nets == n:
                sb[i, place, 8 : 8 + S, 0 : g.ef] = own.astype(F32)

    @pl.when(me == 0)
    def _():
        hb[:, :, :, 0] = jnp.zeros(hb.shape[:3] + hb.shape[4:], BF16)

    @pl.when(me == F - 1)
    def _():
        hb[:, :, :, 1] = jnp.zeros(hb.shape[:3] + hb.shape[4:], BF16)

    barrier = pltpu.get_barrier_semaphore()
    partners = [(b,) for b in range(g.bits)] + [(1, 2)]
    for df in range(1, F):
        pl.semaphore_signal(barrier, inc=1, device_id={"fsdp": peer(df)}, device_id_type=MESH)
    for bits in partners:
        pl.semaphore_signal(barrier, inc=1, device_id={"dp": other(*bits)}, device_id_type=MESH)
    pl.semaphore_wait(barrier, F - 1 + len(partners))
    weight_local(0).start()
    for s in range(S):
        halo_start(0, s, 0)

    def prepare_first(i, s):
        gradient_loaded(i, s)
        halo_take(i, s, 0)
        prepare(i, s)
        prepare_gradient(i, s)

    for s in range(S):
        input_loaded(0, s)
    slots(0, input_work, 0)
    for j in range(TRIPLES):
        weights_start(0, 0, j)
    for s in range(S):
        halo_start(0, s, 1)
    for j in range(TRIPLES):
        weights_start(0, 1, j)
    slots(0, prepare_first, 0)
    weights_forward(0, 0)
    weight_local(0).wait()
    weights_take(0, 0)
    weights_ready(0, 0)

    def first_of_all(i, s):
        first_phase(i, s)

        @pl.when((i == 0) & (s == S - 1))
        def _():
            weights_forward(0, 1)
            weights_take(0, 1)
            weights_ready(0, 1)

    def fourth_and_weights(i, s):
        fourth_phase(i, s)

        @pl.when((i < 2) & (s == 0))
        def _():
            for k in range(2):
                weights_forward(i + 1, k)

    def network(i, carry):
        @pl.when(i < 2)
        def _():
            gacc[...] = jnp.zeros(gacc.shape, F32)

        slots(1, first_of_all, i)
        weights_sent(i)

        @pl.when(i < 2)
        def _():
            load_x(i + 1)
            weight_local(i + 1).start()

        slots(2, second_phase, i)
        slots(3, third_phase, i)

        @pl.when(i < 2)
        def _():
            load_gy(i + 1)

        slots(4, fourth_and_weights, i)

        @pl.when(i < 2)
        def _():
            weight_local(i + 1).wait()
            for k in range(2):
                weights_take(i + 1, k)
                weights_ready(i + 1, k)

        slots(5, last_phase, i)
        return carry

    lax.fori_loop(0, 3, network, 0)


    def drain(i, carry):
        for s in range(S):
            for t in range(2):
                halo_sent(i, s, t)
            for e in range(4):
                for df in range(1, F):
                    row_copy(i, e, s, df, me).wait_send()
        return carry

    lax.fori_loop(0, 3, drain, 0)
    for s in range(S):
        in_grad_copy(2, s).wait()
    for m in range(2):
        for k in range(2):
            pltpu.make_async_copy(pk.at[m, k, me], cg_h.at[m, k], osem.at[m, k]).wait()
    pltpu.make_async_copy(ags, ag_h.at[1], osem.at[1, 2]).wait()


def place_body(g, y_c, dx_c, packed, affine, sums, y, dx, conv, affine_out, gain_out, bias_out):
    for s in range(g.s):
        for src, dst in ((y_c, y), (dx_c, dx)):
            for q in range(g.np):
                flat = src[0, s, :, q * LANES : (q + 1) * LANES].T
                dst[0, s, q] = flat[0 : g.w]
                dst[0, s, q + g.np] = flat[g.w : 2 * g.w]
    step = pl.program_id(0)

    @pl.when(step < 2)
    def _():
        split = g.low_rows - g.high_rows
        rest = g.c - LANES
        for k in range(2):
            conv[0, k, :, 0:LANES] = packed[0, k, 0 : g.low_rows, :]
            conv[0, k, 0 : g.high_rows, LANES : g.c] = packed[0, k, g.low_rows : g.low_rows + g.high_rows, 0:rest]
            conv[0, k, g.high_rows : g.low_rows, LANES : g.c] = packed[
                0, k, g.low_rows : g.low_rows + split, CHUNK : CHUNK + rest
            ]

    @pl.when(step < 2)
    def _():
        affine_out[...] = affine[...]

    @pl.when(step == 0)
    def _():
        gain_out[...] = sums[:, 0:2, 0 : g.shard]
        for j in range(6):
            bias_out[j] = sums[:, 2 + j, 0 : g.shard]


def on_device(
    block_input, embedding, out_cotangent, conv_weights, affine_weight, gains, biases, counts
):
    nets, slots, rows, width, chans = block_input.shape
    fsdp = lax.axis_size("fsdp")
    dp = lax.axis_size("dp")
    embed_rows = affine_weight.shape[1]
    g = settings(dp, fsdp, nets, slots, rows, width, chans, embed_rows)
    weights = conv_weights.reshape(nets, 2, 9, g.shard, chans)

    tiles = (g.np + 1) * LANES
    dma = pltpu.SemaphoreType.DMA
    scratch = [
        pltpu.VMEM((slots, rows, width, chans), BF16),
        pltpu.VMEM((slots, rows, width, chans), BF16),
        pltpu.VMEM((slots, rows, width, chans), BF16),
        pltpu.VMEM((2, slots, chans, g.px), BF16),
        pltpu.VMEM((slots, chans, g.px), BF16),
        pltpu.VMEM((slots, 3, chans, (g.np + 5) * LANES), BF16),
        pltpu.VMEM((slots, 3, chans, (g.np + 2) * LANES), BF16),
        pltpu.VMEM((slots, 3, chans, (g.np + 5) * LANES), BF16),
        pltpu.VMEM((2, slots, 2, 2, 2, width, chans), BF16),
        pltpu.VMEM((slots, chans, tiles), F32),
        pltpu.VMEM((slots, chans, tiles), F32),
        pltpu.VMEM((2, fsdp, 2, 9, g.shard, chans), BF16),
        pltpu.VMEM((2, chans, 9 * chans), BF16),
        pltpu.VMEM((2, chans, 9 * chans), BF16),
        pltpu.VMEM((2, 9 * chans, chans), F32),
        pltpu.VMEM((2, 2, fsdp, g.pack, LANES), F32),
        pltpu.VMEM((3 - g.split, 2, fsdp, g.half, LANES), F32),
        pltpu.VMEM((2, 3, fsdp, g.piece, LANES), F32),
        pltpu.VMEM((2, 2, fsdp - 1, g.piece, LANES), F32),
        pltpu.VMEM((2, g.bits - 3, g.piece, LANES), F32),
        pltpu.VMEM((chans, g.px), F32),
        pltpu.VMEM((slots, chans, g.px), BF16),
        pltpu.VMEM((embed_rows, 2 * chans), F32),
        pltpu.VMEM((3, slots, fsdp, 16, chans), F32),
        pltpu.VMEM((3, 3, slots, fsdp, 8, chans), F32),
        pltpu.VMEM((3, dp, 16, g.wide), F32),
        pltpu.VMEM((3, chans, LANES), F32),
        pltpu.VMEM((slots, 16, chans), F32),
        pltpu.VMEM((slots, 10, chans, LANES), F32),
        dma((slots,)),
        dma((slots,)),
        dma((slots,)),
        dma((3, slots, 2, 2)),
        dma((3, slots, 2, 2)),
        dma((3, 4, slots, fsdp)),
        dma((3, 4, slots, fsdp)),
        dma((3,)),
        dma((3, 2, 3, fsdp)),
        dma((3, 2, 3, fsdp)),
        dma((3, 2, fsdp)),
        dma((3, 2, fsdp)),
        dma((2, 2, g.stages, max(3, fsdp - 1))),
        dma((2, 2, g.stages, max(3, fsdp - 1))),
        dma((2, g.bits + 2)),
        dma((2, g.bits + 2)),
        dma((2, 3)),
    ]
    hbm = pl.BlockSpec(memory_space=pl.ANY)
    vmem = pl.BlockSpec(memory_space=pltpu.VMEM)
    smem = pl.BlockSpec(memory_space=pltpu.SMEM)
    channel_major = jax.ShapeDtypeStruct((nets, slots, chans, g.px), BF16)
    main = pl.pallas_call(
        functools.partial(kernel_body, g),
        out_shape=(
            channel_major,
            channel_major,
            jax.ShapeDtypeStruct((2, 2, g.pack, LANES), F32),
            jax.ShapeDtypeStruct((2, embed_rows, 2 * chans), F32),
            jax.ShapeDtypeStruct((2, 8, 2 * LANES), F32),
        ),
        in_specs=[hbm, hbm, hbm, vmem, vmem, vmem, vmem, smem],
        out_specs=(hbm, hbm, hbm, hbm, vmem),
        scratch_shapes=scratch,
        compiler_params=pltpu.CompilerParams(
            collective_id=0, has_side_effects=True, vmem_limit_bytes=64 << 20
        ),
    )(block_input, out_cotangent, weights, affine_weight, embedding, gains, biases, counts)

    def by_slot(step):
        return (step, 0, 0, 0)

    def by_conv(step):
        return (jnp.minimum(step, 1), 0, 0, 0)

    def by_net(step):
        return (jnp.minimum(step, 1), 0, 0)

    image = pl.BlockSpec((1, slots, rows, width, chans), lambda step: by_slot(step) + (0,))
    block_output, input_grad, conv_grads, affine_grad, gain_grads, bias_grads = pl.pallas_call(
        functools.partial(place_body, g),
        grid=(nets,),
        out_shape=(
            jax.ShapeDtypeStruct(block_input.shape, BF16),
            jax.ShapeDtypeStruct(block_input.shape, BF16),
            jax.ShapeDtypeStruct((2, 2, g.low_rows, chans), F32),
            jax.ShapeDtypeStruct((2, embed_rows, 2 * chans), F32),
            jax.ShapeDtypeStruct((2, 2, g.shard), F32),
            jax.ShapeDtypeStruct((6, 2, g.shard), F32),
        ),
        in_specs=[
            pl.BlockSpec((1, slots, chans, g.px), by_slot),
            pl.BlockSpec((1, slots, chans, g.px), by_slot),
            pl.BlockSpec((1, 2, g.pack, LANES), by_conv),
            pl.BlockSpec((1, embed_rows, 2 * chans), by_net),
            vmem,
        ],
        out_specs=(
            image,
            image,
            pl.BlockSpec((1, 2, g.low_rows, chans), by_conv),
            pl.BlockSpec((1, embed_rows, 2 * chans), by_net),
            vmem,
            vmem,
        ),
        compiler_params=pltpu.CompilerParams(vmem_limit_bytes=63 << 20),
    )(*main)
    conv_grads = conv_grads.reshape(2, 2, 3, 3, g.shard, chans)
    return block_output, input_grad, conv_grads, affine_grad, gain_grads, bias_grads.transpose(1, 0, 2)


def solution(mesh):
    placed = (
        P(None, "dp", "fsdp", None, None),
        P(None, "dp", None),
        P(None, "dp", "fsdp", None, None),
        P(None, None, None, None, "fsdp", None),
        P(None, "fsdp", None),
        P(None, None, "fsdp"),
        P(None, None, "fsdp"),
        P("dp"),
    )
    return jax.shard_map(
        on_device,
        mesh=mesh,
        in_specs=placed,
        out_specs=(
            P(None, "dp", "fsdp", None, None),
            P(None, "dp", "fsdp", None, None),
            P(None, None, None, None, "fsdp", None),
            P(None, "fsdp", None),
            P(None, None, "fsdp"),
            P(None, None, "fsdp"),
        ),
        check_vma=False,
    )
```
